256 devices in a mesh: slab: 16 (over x, y_lo, core), tile: 16 (over z, y_hi).
Axes of the slice: x: 4, y: 4 (y_hi: 2, y_lo: 2; y = y_hi * 2 + y_lo), z: 8, core: 2. Of those that a mesh axis runs over, the one named last changes fastest.
Arguments:
- volume: bfloat16 [128, 2048, 2048], P('slab', None, 'tile'), may hold values from -6 to 6
- measured: bfloat16 [2, 192, 8, 2048], P(None, 'slab', None, 'tile'), may hold values from -6 to 6
- ray_weight: bfloat16 [2, 192, 2048], P(None, 'slab', 'tile'), may hold values from -0.75 to 0.75
- view_owner: int32 [2, 192, 1], P(None, 'slab'), may hold values from 0 to 15; in each aligned block of 12 rows (0 to 11, 12 to 23, ..., all dimensions but the last counted through in order) at most 2 rows name the same one
- band_offset: int32 [2, 192], P(None, 'slab'), may hold values from 0 to 127, as said below
- band_width: int32 [2, 192], P(None, 'slab'), may hold values from 1 to 64
- beta: float32 [1], replicated, may hold values from 0.3 to 1
Outputs:
- gradient: bfloat16 [128, 2048, 2048], P('slab', None, 'tile')
The draws below stay inside these ranges and needn't reach their ends.
Inputs may be any that keep to these rules, and one draw needn't show every extreme that they name: `view_owner`: among the views of one batch acquired on one slab (aligned blocks of 12 views), no slab is named more than 2 times. band_offset + band_width <= 128 for every view.
All inputs are finite; a program needn't handle non-finite values.
Results may differ from the reference program's by a relative error of at most 0.0053.
Values may be sent and summed in bfloat16 or wider, within the bound.
No kernel may reach another device: no remote copies, remote signals or barrier semaphores. Data moves between devices by JAX's collectives and lax.ppermute only.
A program may use at most 128 MiB of HBM per device.

```python
import math
import jax
import jax.numpy as jnp
import numpy as np
from jax import lax

NX = 2048
NY = 2048
BAND = 128
WMAX = 64
BATCHES = 2
CAPP = 2
ZS = 8
VIEWS_DEV = 12
NZ = 128
VIEWS = 192
YT = 128
CAP = 32
N_SLAB = 16
N_TILE = 16


def band_pair(key):
    width_key, offset_key = jax.random.split(key)
    widths = jax.random.randint(width_key, (BATCHES, VIEWS), 1, min(WMAX, 8) + 1)
    widths = widths.at[:, 0].set(WMAX)
    widths = widths.at[:, 1].set(1)
    spread = jax.random.randint(offset_key, (BATCHES, VIEWS), 0, 1 << 20)
    offsets = spread % (BAND + 1 - widths)
    offsets = offsets.at[:, 0].set(0)
    offsets = offsets.at[:, 1].set(BAND - 1)
    return (offsets.astype(jnp.int32), widths.astype(jnp.int32))


def draw_band_offset(key, part):
    return band_pair(key)[0]


def draw_band_width(key, part):
    return band_pair(key)[1]


def levels(own_key, shape, cuts, smallest, top_value):
    loudness = 1.0
    for position, blocks in cuts:
        draws = jax.random.uniform(jax.random.fold_in(jax.random.fold_in(own_key, 6), position), (blocks,), jnp.float32, smallest / len(cuts), top_value / len(cuts))
        loudness = loudness * jnp.repeat(jnp.exp(draws), shape[position] // blocks).reshape((-1,) + (1,) * (len(shape) - 1 - position))
    return loudness


def shared_out(own_key, own, number, rows, number_of, top, reach, slope):
    order = jax.random.permutation(own_key, number_of)
    crowded, usual = shares(number_of, rows * top, reach, slope, True), shares(number_of, rows * top, reach, slope, False)
    places = jnp.arange(number_of)

    def named(sizes, turn):
        used = int((sizes > 0).sum())
        fixed = max(1, used // 4)
        passed = fixed + (places - fixed + turn * (used - fixed)) % max(1, number_of - fixed)
        return jnp.zeros((number_of,), jnp.int32).at[order[jnp.where(places < fixed, places, passed)]].set(jnp.asarray(sizes, jnp.int32))

    sizes = jnp.where(number % 4 == 0, named(crowded, number // 4), named(usual, number - number // 4 - 1))
    mixed = jax.random.permutation(jax.random.fold_in(own, 3), number_of)
    donor, sink = mixed[0:number_of // 2 * 2:2], mixed[1:number_of // 2 * 2:2]
    room = jnp.minimum(sizes[donor] - 1, reach - sizes[sink]) // 2
    room = jnp.where((donor == order[0]) | (sink == order[0]) | (sizes[sink] == 0), 0, jnp.maximum(room, 0))
    passed = jax.random.randint(jax.random.fold_in(own, 4), (number_of // 2,), 0, 1 << 20) % (room + 1)
    sizes = sizes.at[donor].add(-passed).at[sink].add(passed)
    members = jnp.searchsorted(jnp.cumsum(sizes), jnp.arange(rows * top), side="right").astype(jnp.int32)
    listing = members.reshape(top, rows).T
    listing = listing[jax.random.permutation(jax.random.fold_in(own, 1), rows)]
    turn = jax.random.randint(jax.random.fold_in(own, 2), (rows, 1), 0, top)
    return jnp.take_along_axis(listing, (jnp.arange(top)[None, :] + turn) % top, axis=1)


def shares(count, total, most, lean, full):
    weights = [(1 << 20) // math.isqrt(grade ** lean) + 1 for grade in range(1, count + 1)]
    largest = most if full else min(most, max(-(-total // count), total * weights[0] // sum(weights)))
    least = 1 if total - largest >= count - 1 else 0
    holding, surplus = [largest] + [least] * (count - 1), total - largest - least * (count - 1)
    while surplus > 0:
        candidates = [i for i in range(1, count) if holding[i] < largest] or [i for i in range(1, count) if holding[i] < most]
        pool, left = sum([weights[i] for i in candidates]), surplus
        for i in candidates:
            more = min(most - holding[i], max(1, left * weights[i] // pool), surplus)
            holding[i] = holding[i] + more
            surplus = surplus - more
    return np.array(holding)


def bell_draw(key, shape, scale, limit, pieces=(), held_as=jnp.bfloat16):
    entries = jax.random.normal(key, shape, jnp.float32) * scale
    if len(pieces) > 0:
        entries = levels(key, shape, pieces, -0.22, 0.18) * entries
    return jnp.clip(entries, min=-limit, max=limit).astype(held_as)


def setup_inputs(seed: int = 0) -> dict:
    arg_keys = jax.random.split(jax.random.key(seed), 8)
    volume = bell_draw(arg_keys[0], (NZ, NX, NY), 1.0, 6.0, ((0, 16), (2, 16)))
    measured = bell_draw(arg_keys[1], (BATCHES, VIEWS, ZS, NX), 1.0, 6.0, ((1, 16), (3, 16)))
    ray_weight = bell_draw(arg_keys[2], (BATCHES, VIEWS, NY), (NY // 32) ** -0.5, 0.75, ((1, 16), (2, 16)))
    view_owner_keys = jax.random.split(jax.random.fold_in(arg_keys[3], 1), BATCHES * VIEWS // VIEWS_DEV)
    view_owner_turns = jax.random.permutation(jax.random.fold_in(arg_keys[3], 3), BATCHES * VIEWS // VIEWS_DEV)
    view_owner = jax.vmap(lambda own, number: shared_out(jax.random.fold_in(arg_keys[3], 2), own, number, VIEWS_DEV, N_SLAB, 1, CAPP, 2))(view_owner_keys, view_owner_turns).reshape((BATCHES, VIEWS, 1))
    band_offset = draw_band_offset(jax.random.fold_in(arg_keys[7], 71), 0)
    band_width = draw_band_width(jax.random.fold_in(arg_keys[7], 71), 0)
    beta = jnp.clip(jnp.exp(jax.random.uniform(arg_keys[6], (1,), jnp.float32, math.log(0.3), math.log(1.0))), 0.3, 1.0)
    return dict(volume=volume, measured=measured, ray_weight=ray_weight, view_owner=view_owner, band_offset=band_offset, band_width=band_width, beta=beta)


def penalty(diff):
    return diff / jnp.sqrt(1.0 + diff * diff)

def band_matrices(offsets, widths):
    column = jnp.arange(2 * BAND, dtype=jnp.int32)[None, :, None]
    channel = jnp.arange(BAND, dtype=jnp.int32)[None, None, :]
    delta = channel + BAND - column - offsets[:, None, None]
    inside = (delta >= 0) & (delta < widths[:, None, None])
    recip = (1.0 / widths.astype(jnp.float32)).astype(jnp.bfloat16)
    return jnp.where(inside, recip[:, None, None], jnp.zeros((), jnp.bfloat16))

def forward_band(rows, mats):
    count, depth, extent = rows.shape
    blocks = rows.reshape(count, depth, extent // BAND, BAND)
    before = jnp.concatenate([jnp.zeros_like(blocks[:, :, :1]), blocks[:, :, :-1]], axis=2)
    paired = jnp.concatenate([before, blocks], axis=3)
    out = jnp.einsum('jznc,jcd->jznd', paired, mats, precision=lax.Precision.HIGHEST)
    return out.reshape(count, depth, extent)

def backward_band(rows, mats):
    count, depth, extent = rows.shape
    blocks = rows.reshape(count, depth, extent // BAND, BAND)
    spread = jnp.einsum('jznd,jcd->jznc', blocks, mats, precision=lax.Precision.HIGHEST)
    later = jnp.concatenate([spread[:, :, 1:, :BAND], jnp.zeros_like(spread[:, :, :1, :BAND])], axis=2)
    return (spread[:, :, :, BAND:] + later).reshape(count, depth, extent)

def reference(volume, measured, ray_weight, view_owner, band_offset, band_width, beta):

    def one_slab(slab):
        start = (slab * ZS).astype(jnp.int32)
        block = lax.dynamic_slice_in_dim(volume, start, ZS, 0)
        below = lax.dynamic_slice_in_dim(volume, jnp.maximum(start - 1, 0).astype(jnp.int32), 1, 0)
        above = lax.dynamic_slice_in_dim(volume, jnp.minimum(start + ZS, NZ - 1).astype(jnp.int32), 1, 0)
        data = jnp.zeros((ZS, NX, NY), jnp.float32)
        for batch in range(BATCHES):
            owned = view_owner[batch, :, 0] == slab
            order = jnp.argsort(jnp.where(owned, 0, 1).astype(jnp.int32), stable=True)[:CAP]
            valid = owned[order]
            weights = jnp.where(valid[:, None], ray_weight[batch][order], jnp.zeros((), jnp.bfloat16))
            offsets = jnp.where(valid, band_offset[batch][order], 0).astype(jnp.int32)
            widths = jnp.where(valid, band_width[batch][order], 1).astype(jnp.int32)
            rows = jnp.where(valid[:, None, None], measured[batch][order], jnp.zeros((), jnp.bfloat16)).astype(jnp.float32)
            strips = jnp.einsum('jty,zxty->jtzx', weights.reshape(CAP, N_TILE, YT).astype(jnp.float32), block.reshape(ZS, NX, N_TILE, YT).astype(jnp.float32))
            rounded = lax.optimization_barrier(strips.astype(jnp.bfloat16))
            summed = lax.optimization_barrier(jnp.sum(rounded.astype(jnp.float32), axis=1))
            mats = band_matrices(offsets, widths).astype(jnp.float32)
            sums = forward_band(summed, mats)
            residual = (sums - rows).astype(jnp.bfloat16)
            image = backward_band(residual.astype(jnp.float32), mats).astype(jnp.bfloat16)
            data = data + jnp.einsum('jy,jzx->zxy', weights.astype(jnp.float32), image.astype(jnp.float32))
        center = block.astype(jnp.float32)
        stacked = jnp.concatenate([below, block, above], axis=0).astype(jnp.float32)
        slice_index = jnp.arange(ZS, dtype=jnp.int32)[:, None, None] + start
        regular = jnp.where(slice_index > 0, penalty(center - stacked[:-2]), 0.0)
        regular = regular + jnp.where(slice_index < NZ - 1, penalty(center - stacked[2:]), 0.0)
        along_x = penalty(jnp.diff(center, axis=1))
        regular = regular + jnp.pad(along_x, ((0, 0), (1, 0), (0, 0))) - jnp.pad(along_x, ((0, 0), (0, 1), (0, 0)))
        along_y = penalty(jnp.diff(center, axis=2))
        regular = regular + jnp.pad(along_y, ((0, 0), (0, 0), (1, 0))) - jnp.pad(along_y, ((0, 0), (0, 0), (0, 1)))
        return (data + beta[0] * regular).astype(jnp.bfloat16)
    slabs = lax.map(one_slab, jnp.arange(N_SLAB, dtype=jnp.int32))
    return slabs.reshape(NZ, NX, NY)
```

```python
import functools

import jax
import jax.numpy as jnp
from jax import lax
from jax.experimental import pallas as pl
from jax.experimental.pallas import tpu as pltpu
from jax.sharding import PartitionSpec as P

BAND = 128
BATCHES = 2
CAPP = 2
SLOTS = BATCHES * CAPP
ROWS = 16
RUN = SLOTS * 8
PIECES = 4
XT = 256
F32 = jnp.float32
BF16 = jnp.bfloat16
VMEM = pl.BlockSpec(memory_space=pltpu.VMEM)
SMEM = pl.BlockSpec(memory_space=pltpu.SMEM)
ANY = pl.BlockSpec(memory_space=pl.ANY)


def cost(flops, moved):
    return pl.CostEstimate(flops=flops, bytes_accessed=moved, transcendentals=0)


def iota(shape, dim):
    return lax.broadcasted_iota(jnp.int32, shape, dim)


def pack_kernel(owner_ref, offset_ref, width_ref, weight_ref, measured_ref, out_ref, count_ref):
    out_ref[...] = jnp.zeros_like(out_ref)
    slabs = out_ref.shape[0]
    views = owner_ref.shape[1]
    row = iota((ROWS, BAND), 0)
    lane = iota((ROWS, BAND), 1)
    empty = jnp.zeros((8, BAND), F32)
    for batch in range(BATCHES):
        for slab in range(slabs):
            count_ref[slab] = 0
        for view in range(views):
            owner = owner_ref[batch, view]
            rank = count_ref[owner]
            count_ref[owner] = rank + 1
            rows = jnp.concatenate([measured_ref[batch, view].astype(F32), empty], axis=0)
            band = jnp.where(
                lane == 0,
                offset_ref[batch, view].astype(F32),
                jnp.where(lane == 1, width_ref[batch, view].astype(F32), 0.0),
            )
            rows = jnp.where(row == 8, weight_ref[view].astype(F32)[batch : batch + 1], jnp.where(row == 9, band, rows))
            out_ref[owner, batch * CAPP + rank] = rows.astype(BF16)


def pack(owner, offset, width, weight, measured, slabs):
    return pl.pallas_call(
        pack_kernel,
        out_shape=jax.ShapeDtypeStruct((slabs, SLOTS, ROWS, BAND), BF16),
        in_specs=[SMEM, SMEM, SMEM, VMEM, VMEM],
        out_specs=VMEM,
        scratch_shapes=[pltpu.SMEM((slabs,), jnp.int32)],
        name="pack_messages",
    )(owner, offset, width, jnp.transpose(weight, (1, 0, 2)), measured)


def joined(block):
    return jnp.concatenate([block[z] for z in range(block.shape[0])], axis=1)


def edge_kernel(volume_ref, order_ref, first_ref, last_ref, bottom_ref, top_ref):
    depth, _, strip = volume_ref.shape
    shape = (2 * depth, depth * strip)
    row, lane = iota(shape, 0), iota(shape, 1)
    target = jnp.where(row < depth, row * strip, (row - depth) * strip + strip - 1)
    pick = jnp.where(lane == target, 1.0, 0.0).astype(BF16)
    out = lax.dot_general(
        pick, joined(volume_ref), (((1,), (1,)), ((), ())), preferred_element_type=F32
    )
    first_ref[...] = out[:depth]
    last_ref[...] = out[depth:]
    bottom_ref[...] = volume_ref[0]
    top_ref[...] = volume_ref[depth - 1]


def edges(volume, order):
    depth, extent, strip = volume.shape
    line = jax.ShapeDtypeStruct((depth, extent), F32)
    plane = jax.ShapeDtypeStruct((extent, strip), BF16)
    line_spec = pl.BlockSpec((depth, XT), lambda i: (0, i))
    plane_spec = pl.BlockSpec((XT, strip), lambda i: (i, 0))
    return pl.pallas_call(
        edge_kernel,
        grid=(extent // XT,),
        out_shape=(line, line, plane, plane),
        in_specs=[pl.BlockSpec((depth, XT, strip), lambda i: (0, i, 0)), ANY],
        out_specs=(line_spec, line_spec, plane_spec, plane_spec),
        cost_estimate=cost(2 * 256 * volume.size, 3 * volume.size),
        name="strip_edges",
    )(volume, order)


def spread_weights(tiles, out_ref, first, depth):
    rows = tiles.shape[0] * depth
    weights = jnp.broadcast_to(
        tiles.astype(F32)[:, 8:9, :], (tiles.shape[0], depth, BAND)
    ).reshape(rows, BAND)
    slice_of = lax.rem(iota((rows, BAND), 0), depth)
    for z in range(depth):
        out_ref[first : first + rows, z * BAND : (z + 1) * BAND] = jnp.where(
            slice_of == z, weights, 0.0
        ).astype(BF16)


def hops(tiles):
    half = tiles // 4
    return [0] + [sign * hop for hop in range(1, half) for sign in (1, -1)] + [half]


def forward_kernel(tiles, place_ref, got_ref, volume_ref, *refs):
    spread_ref, outs = refs[0], refs[1:]
    me = place_ref[1]

    @pl.when(pl.program_id(0) == 0)
    def _():
        row = 0
        for hop in hops(tiles):
            tile = lax.rem(me + 2 * hop + tiles, tiles)
            for source in (tile, tile ^ 1):
                spread_weights(got_ref[pl.ds(source * SLOTS, SLOTS)], spread_ref, row, 8)
                row += RUN

    out = lax.dot_general(
        spread_ref[...], joined(volume_ref), (((1,), (1,)), ((), ())), preferred_element_type=F32
    ).astype(BF16)
    row = 0
    for ref in outs:
        ref[...] = out[row : row + ref.shape[0]]
        row += ref.shape[0]


def forward(place, got, volume, tiles):
    depth, extent, strip = volume.shape
    slots = got.shape[0]
    rows = [2 * RUN] * (tiles // 2 - 1) + [RUN] * 2
    spread = (slots * depth, depth * strip)
    return pl.pallas_call(
        functools.partial(forward_kernel, tiles),
        grid=(extent // XT,),
        out_shape=[jax.ShapeDtypeStruct(spread, BF16)]
        + [jax.ShapeDtypeStruct((count, extent), BF16) for count in rows],
        in_specs=[
            SMEM,
            pl.BlockSpec(got.shape, lambda i: (0, 0, 0)),
            pl.BlockSpec((depth, XT, strip), lambda i: (0, i, 0)),
        ],
        out_specs=[pl.BlockSpec(spread, lambda i: (0, 0))]
        + [pl.BlockSpec((count, XT), lambda i: (0, i)) for count in rows],
        cost_estimate=cost(2 * slots * depth * volume.size, 3 * volume.size),
        name="forward",
    )(place, got, volume)


def sums_kernel(from_below_ref, up_ref, from_above_ref, down_ref, *refs):
    up_out_ref, down_out_ref = refs[-2:]
    part = from_below_ref.shape[0]
    rows = up_ref.shape[0]
    up_out_ref[:part] = (from_below_ref[...].astype(F32) + up_ref[:part].astype(F32)).astype(BF16)
    low = rows - part
    down_out_ref[low:] = (from_above_ref[...].astype(F32) + down_ref[low:].astype(F32)).astype(BF16)
    if low:
        up_out_ref[part:] = up_ref[part:]
        down_out_ref[:low] = down_ref[:low]


def ring_sums(from_below, up, from_above, down, *order):
    out = jax.ShapeDtypeStruct(up.shape, BF16)
    return pl.pallas_call(
        sums_kernel,
        out_shape=(out, out),
        in_specs=[VMEM] * 4 + [ANY] * len(order),
        out_specs=(VMEM, VMEM),
        cost_estimate=cost(2 * up.size, 8 * up.size),
        name="ring_sums",
    )(from_below, up, from_above, down, *order)


def last_sums_kernel(from_below_ref, from_above_ref, own_ref, *refs):
    kept_ref, sent_ref = refs[-2:]
    total = (
        from_below_ref[...].astype(F32) + from_above_ref[...].astype(F32) + own_ref[...].astype(F32)
    )
    kept_ref[...] = total[:RUN]
    sent_ref[...] = total[RUN:].astype(BF16)


def last_sums(from_below, from_above, own, *order):
    extent = own.shape[1]
    return pl.pallas_call(
        last_sums_kernel,
        out_shape=(
            jax.ShapeDtypeStruct((RUN, extent), F32),
            jax.ShapeDtypeStruct((RUN, extent), BF16),
        ),
        in_specs=[VMEM] * 3 + [ANY] * len(order),
        out_specs=(VMEM, VMEM),
        cost_estimate=cost(2 * own.size, 8 * own.size),
        name="last_sums",
    )(from_below, from_above, own, *order)


def residual_kernel(kept_ref, arrived_ref, views_ref, *refs):
    out_ref = refs[-1]
    extent = kept_ref.shape[1]
    blocks = extent // BAND
    empty = jnp.zeros((8, BAND), F32)
    for slot in range(SLOTS):
        low = slot * 8
        total = kept_ref[low : low + 8] + arrived_ref[...].astype(F32)[low : low + 8]
        band = views_ref[0, slot].astype(F32)
        offset = band[9:10, 0:1].astype(jnp.int32)
        width = jnp.maximum(band[9:10, 1:2], 1.0)
        recip = 1.0 / width
        width = width.astype(jnp.int32)

        def inside(delta):
            delta = delta - offset
            return jnp.where((delta >= 0) & (delta < width), recip, 0.0).astype(BF16)

        shape = (2 * BAND, BAND)
        onward = inside(iota(shape, 1) + BAND - iota(shape, 0))
        back = inside(iota(shape, 0) - iota(shape, 1))
        parts = [total[:, n * BAND : (n + 1) * BAND] for n in range(blocks)]
        here = jnp.concatenate(parts, axis=0)
        before = jnp.concatenate([empty] + parts[:-1], axis=0)
        paired = jnp.concatenate([before, here], axis=1)
        high = paired.astype(BF16)
        rest = (paired - high.astype(F32)).astype(BF16)
        sums = jnp.dot(high, onward, preferred_element_type=F32) + jnp.dot(
            rest, onward, preferred_element_type=F32
        )
        rows = jnp.concatenate(
            [views_ref[n, slot].astype(F32)[:8] for n in range(blocks)], axis=0
        )
        residual = (sums - rows).astype(BF16).astype(F32)
        later = jnp.concatenate([residual[8:], empty], axis=0)
        both = jnp.concatenate([residual, later], axis=1).astype(BF16)
        image = jnp.dot(both, back, preferred_element_type=F32)
        image = jnp.concatenate([image[n * 8 : (n + 1) * 8] for n in range(blocks)], axis=1)
        if slot % 2 == 0:
            even = image
        else:
            out_ref[low - 8 : low + 8] = jnp.concatenate([even, image], axis=0).astype(BF16)


def residual_images(kept, arrived, views, *order):
    return pl.pallas_call(
        residual_kernel,
        out_shape=jax.ShapeDtypeStruct(arrived.shape, BF16),
        in_specs=[VMEM] * 3 + [ANY] * len(order),
        out_specs=VMEM,
        cost_estimate=cost(4 * 8 * 16 * 256 * 128 * 6, 2 * views.size),
        name="residual_images",
    )(kept, arrived, views, *order)


def penalty(diff):
    return diff * lax.rsqrt(1.0 + diff * diff)


def regularizer_kernel(
    first_tile,
    count,
    place_ref,
    beta_ref,
    block_ref,
    before_ref,
    after_ref,
    below_ref,
    above_ref,
    first_ref,
    last_ref,
    left_ref,
    right_ref,
    *refs,
):
    out_ref, under_ref, side_ref = refs[-3:]
    depth, tile, strip = block_ref.shape
    at = pl.program_id(0) + first_tile
    beta = beta_ref[0]
    has_below = (place_ref[0] > 0).astype(F32)
    has_above = (place_ref[0] < place_ref[3] - 1).astype(F32)
    has_left = (place_ref[1] > 0).astype(F32)
    has_right = (place_ref[1] < place_ref[2] - 1).astype(F32)
    has_before = (at > 0).astype(F32)
    has_after = (at < count - 1).astype(F32)
    spacing = strip // 8

    on_left = penalty(first_ref[...] - left_ref[...]) * has_left
    on_right = penalty(right_ref[...] - last_ref[...]) * has_right
    end = iota((spacing, tile), 0)
    rows = []
    for level in range(8):
        up = (level + 1) % 8
        rows.append(
            jnp.where(
                end == 0,
                on_left[level : level + 1],
                jnp.where(end == spacing - 1, on_right[up : up + 1], 0.0),
            )
        )
    side_ref[...] = jnp.concatenate(rows, axis=0).T
    under_ref[...] = (
        penalty(block_ref[0].astype(F32) - below_ref[...].astype(F32)) * has_below
    )
    row = iota((tile, strip), 0)
    lane = iota((tile, strip), 1)

    def body(z, carry):
        center = block_ref[z].astype(F32)
        top = z == depth - 1
        upper = jnp.where(top, above_ref[...], block_ref[jnp.minimum(z + 1, depth - 1)])
        over = penalty(upper.astype(F32) - center) * jnp.where(top, has_above, 1.0)
        total = under_ref[...] - over
        under_ref[...] = over
        ahead = after_ref[z].astype(F32)[0:1]
        behind = penalty(center[0:1] - before_ref[z].astype(F32)[15:16]) * has_before
        along = penalty(jnp.where(row == tile - 1, ahead, pltpu.roll(center, tile - 1, 0)) - center)
        along = jnp.where(row == tile - 1, along * has_after, along)
        total = total + jnp.where(row == 0, behind, pltpu.roll(along, 1, 0)) - along
        side = pltpu.roll(side_ref[...], lax.rem(strip - z * spacing, strip), 1)
        across = penalty(pltpu.roll(center, strip - 1, 1) - center)
        across = jnp.where(lane == strip - 1, side, across)
        total = total + jnp.where(lane == 0, side, pltpu.roll(across, 1, 1)) - across
        out_ref[z] = (total * beta).astype(BF16)
        return carry

    lax.fori_loop(0, depth, body, 0, unroll=2)


def regularizer(index, done, place, beta, volume, below, above, lines, *order):
    depth, extent, strip = volume.shape
    count = extent // XT
    length = count // PIECES
    start = index * length
    edge = XT // 16
    line = pl.BlockSpec((depth, XT), lambda i: (0, start + i))
    plane = pl.BlockSpec((XT, strip), lambda i: (start + i, 0))
    block = pl.BlockSpec((depth, XT, strip), lambda i: (0, start + i, 0))
    ends = [
        lambda i: (0, jnp.maximum((start + i) * edge - 1, 0), 0),
        lambda i: (0, jnp.minimum((start + i + 1) * edge, count * edge - 1), 0),
    ]
    specs = [SMEM, SMEM, block]
    specs += [pl.BlockSpec((depth, 16, strip), where) for where in ends]
    specs += [plane] * 2 + [line] * 4 + [ANY] * len(order)
    before = [] if done is None else [done]
    return pl.pallas_call(
        functools.partial(regularizer_kernel, start, count),
        grid=(length,),
        out_shape=jax.ShapeDtypeStruct(volume.shape, BF16),
        in_specs=specs + [ANY] * len(before),
        out_specs=block,
        scratch_shapes=[pltpu.VMEM((XT, strip), F32), pltpu.VMEM((XT, strip), F32)],
        input_output_aliases={len(specs): 0} if before else {},
        cost_estimate=cost(30 * volume.size // PIECES, 8 * volume.size // PIECES),
        name="regularizer",
    )(place, beta, volume, volume, volume, below, above, *lines, *order, *before)


def gradient_kernel(count, spread_ref, *refs):
    chunk_refs = refs[:count]
    regular_ref, out_ref = refs[count:]
    depth, tile, strip = out_ref.shape
    rows = jnp.concatenate([ref[...] for ref in chunk_refs], axis=0)
    out = lax.dot_general(
        rows, spread_ref[...], (((0,), (0,)), ((), ())), preferred_element_type=F32
    )
    for z in range(depth):
        regular = regular_ref[z].astype(F32)
        out_ref[z] = (out[:, z * strip : (z + 1) * strip] + regular).astype(BF16)


def gradient(spread, chunks, regular):
    depth, extent, strip = regular.shape
    block = pl.BlockSpec((depth, XT, strip), lambda i: (0, i, 0))
    size = depth * extent * strip
    return pl.pallas_call(
        functools.partial(gradient_kernel, len(chunks)),
        grid=(extent // XT,),
        out_shape=jax.ShapeDtypeStruct(regular.shape, BF16),
        in_specs=[pl.BlockSpec(spread.shape, lambda i: (0, 0))]
        + [pl.BlockSpec((chunk.shape[0], XT), lambda i: (0, i)) for chunk in chunks]
        + [block],
        out_specs=block,
        cost_estimate=cost(2 * spread.shape[0] * size, 5 * size),
        name="gradient",
    )(spread, *chunks, regular)


def shards(volume, measured, ray_weight, view_owner, band_offset, band_width, beta):
    slabs = lax.axis_size("slab")
    tiles = lax.axis_size("tile")
    slab, tile = lax.axis_index("slab"), lax.axis_index("tile")
    place = jnp.stack([slab, tile, jnp.int32(tiles), jnp.int32(slabs)])

    def along_z(block, by):
        return lax.ppermute(block, "tile", [(i, (i + 2 * by) % tiles) for i in range(tiles)])

    def along_y(block):
        return lax.ppermute(block, "tile", [(i, i ^ 1) for i in range(tiles)])

    packed = pack(view_owner[:, :, 0], band_offset, band_width, ray_weight, measured, slabs)
    got = lax.all_to_all(packed, "slab", split_axis=0, concat_axis=0, tiled=True)
    first, last, bottom, top = edges(volume, packed)
    got, first, last, bottom, top = lax.optimization_barrier((got, first, last, bottom, top))

    spread, *outs = forward(place, got.reshape(slabs * SLOTS, ROWS, BAND), volume, tiles)
    own = dict(zip(hops(tiles)[:-1], outs))
    up, down = outs[-2:]
    first, last, up = lax.optimization_barrier((first, last, up))
    from_below, from_above = along_z(up, 1), along_z(down, -1)
    left = lax.ppermute(last, "tile", [(i, i + 1) for i in range(tiles - 1)])
    right = lax.ppermute(first, "tile", [(i + 1, i) for i in range(tiles - 1)])
    lines = (first, last, left, right)

    up, down = ring_sums(from_below, own[3], from_above, own[-3], left)
    bottom, top, up = lax.optimization_barrier((bottom, top, up))
    from_below, from_above = along_z(up, 1), along_z(down, -1)
    below = lax.ppermute(top, "slab", [(i, i + 1) for i in range(slabs - 1)])
    above = lax.ppermute(bottom, "slab", [(i + 1, i) for i in range(slabs - 1)])

    up, down = ring_sums(from_below, own[2], from_above, own[-2], right)
    got, up = lax.optimization_barrier((got, up))
    from_below, from_above = along_z(up, 1), along_z(down, -1)
    views = lax.all_to_all(got, "tile", split_axis=0, concat_axis=0, tiled=True)

    up, down = ring_sums(from_below, own[1], from_above, own[-1], below, above)
    from_below, from_above = along_z(up, 1), along_z(down, -1)
    regular = None

    def piece(index, after):
        return regularizer(index, regular, place, beta, volume, below, above, lines, after)

    kept, sent = last_sums(from_below, from_above, own[0], views)
    arrived = along_y(sent)
    regular = piece(0, sent)
    images = residual_images(kept, arrived, views, regular)

    partner = along_y(images)
    regular = piece(1, images)
    pair = jnp.concatenate([images, partner], axis=0)
    chunks = [pair]
    up, down = pair, pair
    for hop in range(1, tiles // 4):
        if hop <= 2:
            up, down, regular = lax.optimization_barrier((up, down, regular))
            after = up
        up, down = along_z(up, 1), along_z(down, -1)
        chunks += [down, up]
        if hop <= 2:
            regular = piece(hop + 1, after)
    up, down, regular = lax.optimization_barrier((up, down, regular))
    chunks += [along_z(up[:RUN], 1), along_z(down[RUN:], -1)]
    return gradient(spread, chunks, regular)


def solution(mesh):
    in_specs = (
        P("slab", None, "tile"),
        P(None, "slab", None, "tile"),
        P(None, "slab", "tile"),
        P(None, "slab", None),
        P(None, "slab"),
        P(None, "slab"),
        P(),
    )
    out_specs = P("slab", None, "tile")
    return jax.shard_map(shards, mesh=mesh, in_specs=in_specs, out_specs=out_specs, check_vma=False)
```

```python
import functools

import jax
import jax.numpy as jnp
from jax import lax
from jax.experimental import pallas as pl
from jax.experimental.pallas import tpu as pltpu
from jax.sharding import PartitionSpec as P

BAND = 128
BATCHES = 2
CAPP = 2
SLOTS = BATCHES * CAPP
ROWS = 16
RUN = SLOTS * 8
PAIR = 2 * RUN
LINES = 16
PIECES = 4


def limit(mib):
    return pltpu.CompilerParams(vmem_limit_bytes=mib << 20)

XT = 256
F32 = jnp.float32
BF16 = jnp.bfloat16
VMEM = pl.BlockSpec(memory_space=pltpu.VMEM)
SMEM = pl.BlockSpec(memory_space=pltpu.SMEM)
ANY = pl.BlockSpec(memory_space=pl.ANY)


def cost(flops, moved):
    return pl.CostEstimate(flops=flops, bytes_accessed=moved, transcendentals=0)


def iota(shape, dim):
    return lax.broadcasted_iota(jnp.int32, shape, dim)


def pack_kernel(owner_ref, offset_ref, width_ref, weight_ref, measured_ref, out_ref, count_ref):
    out_ref[...] = jnp.zeros_like(out_ref)
    slabs = out_ref.shape[0]
    views = owner_ref.shape[1]
    row = iota((ROWS, BAND), 0)
    lane = iota((ROWS, BAND), 1)
    empty = jnp.zeros((8, BAND), F32)
    for batch in range(BATCHES):
        for slab in range(slabs):
            count_ref[slab] = 0
        for view in range(views):
            owner = owner_ref[batch, view]
            rank = count_ref[owner]
            count_ref[owner] = rank + 1
            rows = jnp.concatenate([measured_ref[batch, view].astype(F32), empty], axis=0)
            band = jnp.where(
                lane == 0,
                offset_ref[batch, view].astype(F32),
                jnp.where(lane == 1, width_ref[batch, view].astype(F32), 0.0),
            )
            rows = jnp.where(row == 8, weight_ref[view].astype(F32)[batch : batch + 1], jnp.where(row == 9, band, rows))
            out_ref[owner, batch * CAPP + rank] = rows.astype(BF16)


def pack(owner, offset, width, weight, measured, slabs):
    return pl.pallas_call(
        pack_kernel,
        out_shape=jax.ShapeDtypeStruct((slabs, SLOTS, ROWS, BAND), BF16),
        in_specs=[SMEM, SMEM, SMEM, VMEM, VMEM],
        out_specs=VMEM,
        scratch_shapes=[pltpu.SMEM((slabs,), jnp.int32)],
        name="pack_messages",
    )(owner, offset, width, jnp.transpose(weight, (1, 0, 2)), measured)


def joined(block):
    return jnp.concatenate([block[z] for z in range(block.shape[0])], axis=1)


def spread_weights(tiles, out_ref, first, depth):
    rows = tiles.shape[0] * depth
    weights = jnp.broadcast_to(
        tiles.astype(F32)[:, 8:9, :], (tiles.shape[0], depth, BAND)
    ).reshape(rows, BAND)
    slice_of = lax.rem(iota((rows, BAND), 0), depth)
    for z in range(depth):
        out_ref[first : first + rows, z * BAND : (z + 1) * BAND] = jnp.where(
            slice_of == z, weights, 0.0
        ).astype(BF16)


def hops(tiles):
    half = tiles // 4
    return [0] + [sign * hop for hop in range(1, half) for sign in (1, -1)] + [half]


def fill_spread(tiles, me, got_ref, spread_ref):
    row = 0
    for hop in hops(tiles):
        tile = lax.rem(me + 2 * hop + tiles, tiles)
        for source in (tile, tile ^ 1):
            spread_weights(got_ref[pl.ds(source * SLOTS, SLOTS)], spread_ref, row, 8)
            row += RUN
    shape = (LINES, spread_ref.shape[1])
    line = iota(shape, 0)
    target = jnp.where(line < 8, line * BAND, (line - 8) * BAND + BAND - 1)
    spread_ref[row:] = jnp.where(iota(shape, 1) == target, 1.0, 0.0).astype(BF16)


def spread_kernel(tiles, place_ref, got_ref, order_ref, out_ref):
    fill_spread(tiles, place_ref[1], got_ref, out_ref)


def spread_rows(place, got, tiles, order):
    shape = (got.shape[0] * 8 + LINES, 8 * BAND)
    return pl.pallas_call(
        functools.partial(spread_kernel, tiles),
        out_shape=jax.ShapeDtypeStruct(shape, BF16),
        in_specs=[SMEM, VMEM, ANY],
        out_specs=VMEM,
        compiler_params=limit(16),
        cost_estimate=cost(4 * shape[0] * shape[1], 4 * shape[0] * shape[1]),
        name="spread_rows",
    )(place, got, order)


def forward_kernel(tiles, place_ref, got_ref, volume_ref, *refs):
    outs, spread_ref = refs[:-1], refs[-1]

    @pl.when(pl.program_id(0) == 0)
    def _():
        fill_spread(tiles, place_ref[1], got_ref, spread_ref)

    out = lax.dot_general(
        spread_ref[...], joined(volume_ref), (((1,), (1,)), ((), ())), preferred_element_type=F32
    ).astype(BF16)
    row = 0
    for ref in outs:
        count = min(ref.shape[0], PAIR)
        ref[:count] = out[row : row + count]
        if ref.shape[0] > PAIR:
            ref[PAIR:] = out[-LINES:]
        row += count


def forward(place, got, volume, tiles, *order):
    depth, extent, strip = volume.shape
    slots = got.shape[0]
    rows = [PAIR] + [PAIR + LINES] * 2 + [PAIR] * (tiles // 2 - 4) + [RUN] * 2

    def kernel(place_ref, got_ref, volume_ref, *refs):
        forward_kernel(tiles, place_ref, got_ref, volume_ref, *refs[len(order) :])

    return pl.pallas_call(
        kernel,
        grid=(extent // XT,),
        out_shape=[jax.ShapeDtypeStruct((count, extent), BF16) for count in rows],
        in_specs=[
            SMEM,
            pl.BlockSpec(got.shape, lambda i: (0, 0, 0)),
            pl.BlockSpec((depth, XT, strip), lambda i: (0, i, 0)),
        ]
        + [ANY] * len(order),
        out_specs=[pl.BlockSpec((count, XT), lambda i: (0, i)) for count in rows],
        scratch_shapes=[pltpu.VMEM((slots * depth + LINES, depth * strip), BF16)],
        cost_estimate=cost(2 * slots * depth * volume.size, 3 * volume.size),
        name="forward",
    )(place, got, volume, *order)


def sums_kernel(up_ref, up_near_ref, up_far_ref, down_ref, down_near_ref, down_far_ref, *refs):
    up_out_ref, down_out_ref = refs[-2:]

    def add(*parts):
        return functools.reduce(jnp.add, [part.astype(F32) for part in parts]).astype(BF16)

    up_out_ref[:RUN] = add(up_ref[:RUN], up_near_ref[:RUN], up_far_ref[...])
    up_out_ref[RUN:] = add(up_ref[RUN:], up_near_ref[RUN:])
    down_out_ref[:RUN] = add(down_ref[:RUN], down_near_ref[:RUN])
    down_out_ref[RUN:] = add(down_ref[RUN:], down_near_ref[RUN:], down_far_ref[...])


def round_sums(*operands):
    out = jax.ShapeDtypeStruct(operands[0].shape, BF16)
    return pl.pallas_call(
        sums_kernel,
        out_shape=(out, out),
        in_specs=[VMEM] * 6 + [ANY] * (len(operands) - 6),
        out_specs=(VMEM, VMEM),
        compiler_params=limit(16),
        cost_estimate=cost(6 * out.size, 14 * out.size),
        name="round_sums",
    )(*operands)


def last_sums_kernel(
    place_ref, own_ref, mine_ref, below_ref, above_ref, up_ref, down_ref, *refs
):
    kept_ref, sent_ref = refs[-2:]
    total = (
        own_ref[...].astype(F32)
        + below_ref[:PAIR].astype(F32)
        + above_ref[:PAIR].astype(F32)
        + up_ref[...].astype(F32)
        + down_ref[...].astype(F32)
    )
    kept_ref[...] = total[:RUN]
    sent_ref[:RUN] = total[RUN:].astype(BF16)
    mine, below, above = [ref[PAIR:].astype(F32) for ref in (mine_ref, below_ref, above_ref)]
    even = place_ref[1] % 2 == 0
    left = jnp.where(even, mine[8:], below[8:])
    right = jnp.where(even, above[:8], mine[:8])
    sent_ref[RUN:] = jnp.concatenate([left, right], axis=0).astype(BF16)


def last_sums(place, own, mine, below, above, up, down, *order):
    extent = own.shape[1]
    return pl.pallas_call(
        last_sums_kernel,
        out_shape=(
            jax.ShapeDtypeStruct((RUN, extent), F32),
            jax.ShapeDtypeStruct((RUN + LINES, extent), BF16),
        ),
        in_specs=[SMEM] + [VMEM] * 6 + [ANY] * len(order),
        out_specs=(VMEM, VMEM),
        compiler_params=limit(16),
        cost_estimate=cost(5 * own.size, 14 * own.size),
        name="last_sums",
    )(place, own, mine, below, above, up, down, *order)


def residual_kernel(kept_ref, arrived_ref, views_ref, *refs):
    out_ref = refs[-1]
    extent = kept_ref.shape[1]
    blocks = extent // BAND
    empty = jnp.zeros((8, BAND), F32)
    arrived = arrived_ref[:RUN].astype(F32)
    for slot in range(SLOTS):
        low = slot * 8
        total = kept_ref[low : low + 8] + arrived[low : low + 8]
        band = views_ref[0, slot].astype(F32)
        offset = band[9:10, 0:1].astype(jnp.int32)
        width = jnp.maximum(band[9:10, 1:2], 1.0)
        recip = 1.0 / width
        width = width.astype(jnp.int32)

        def inside(delta):
            delta = delta - offset
            return jnp.where((delta >= 0) & (delta < width), recip, 0.0).astype(BF16)

        shape = (2 * BAND, BAND)
        onward = inside(iota(shape, 1) + BAND - iota(shape, 0))
        back = inside(iota(shape, 0) - iota(shape, 1))
        parts = [total[:, n * BAND : (n + 1) * BAND] for n in range(blocks)]
        here = jnp.concatenate(parts, axis=0)
        before = jnp.concatenate([empty] + parts[:-1], axis=0)
        paired = jnp.concatenate([before, here], axis=1)
        high = paired.astype(BF16)
        rest = (paired - high.astype(F32)).astype(BF16)
        sums = jnp.dot(high, onward, preferred_element_type=F32) + jnp.dot(
            rest, onward, preferred_element_type=F32
        )
        rows = jnp.concatenate(
            [views_ref[n, slot].astype(F32)[:8] for n in range(blocks)], axis=0
        )
        residual = (sums - rows).astype(BF16).astype(F32)
        later = jnp.concatenate([residual[8:], empty], axis=0)
        both = jnp.concatenate([residual, later], axis=1).astype(BF16)
        image = jnp.dot(both, back, preferred_element_type=F32)
        image = jnp.concatenate([image[n * 8 : (n + 1) * 8] for n in range(blocks)], axis=1)
        if slot % 2 == 0:
            even = image
        else:
            out_ref[low - 8 : low + 8] = jnp.concatenate([even, image], axis=0).astype(BF16)


def residual_images(kept, arrived, views, *order):
    return pl.pallas_call(
        residual_kernel,
        out_shape=jax.ShapeDtypeStruct(kept.shape, BF16),
        in_specs=[VMEM] * 3 + [ANY] * len(order),
        out_specs=VMEM,
        compiler_params=limit(16),
        cost_estimate=cost(4 * 8 * 16 * 256 * 128 * 6, 2 * views.size),
        name="residual_images",
    )(kept, arrived, views, *order)


def penalty(diff):
    return diff * lax.rsqrt(1.0 + diff * diff)


def regularizer_kernel(
    first_tile,
    count,
    place_ref,
    beta_ref,
    block_ref,
    before_ref,
    after_ref,
    below_ref,
    above_ref,
    *refs,
):
    out_ref, under_ref = refs[-2:]
    depth, tile, strip = block_ref.shape
    at = pl.program_id(0) + first_tile
    beta = beta_ref[0]
    has_below = (place_ref[0] > 0).astype(F32)
    has_above = (place_ref[0] < place_ref[3] - 1).astype(F32)
    has_before = (at > 0).astype(F32)
    has_after = (at < count - 1).astype(F32)
    under_ref[...] = penalty(block_ref[0].astype(F32) - below_ref[0].astype(F32)) * has_below
    row = iota((tile, strip), 0)
    lane = iota((tile, strip), 1)

    def body(z, carry):
        center = block_ref[z].astype(F32)
        top = z == depth - 1
        upper = jnp.where(top, above_ref[0], block_ref[jnp.minimum(z + 1, depth - 1)])
        over = penalty(upper.astype(F32) - center) * jnp.where(top, has_above, 1.0)
        total = under_ref[...] - over
        under_ref[...] = over
        ahead = after_ref[z].astype(F32)[0:1]
        behind = penalty(center[0:1] - before_ref[z].astype(F32)[15:16]) * has_before
        along = penalty(jnp.where(row == tile - 1, ahead, pltpu.roll(center, tile - 1, 0)) - center)
        along = jnp.where(row == tile - 1, along * has_after, along)
        total = total + jnp.where(row == 0, behind, pltpu.roll(along, 1, 0)) - along
        across = penalty(pltpu.roll(center, strip - 1, 1) - center)
        across = jnp.where(lane == strip - 1, 0.0, across)
        total = total + pltpu.roll(across, 1, 1) - across
        out_ref[z] = (total * beta).astype(BF16)
        return carry

    lax.fori_loop(0, depth, body, 0, unroll=2)


def regularizer(index, done, place, beta, volume, below, above, *order):
    depth, extent, strip = volume.shape
    count = extent // XT
    length = count // PIECES
    start = index * length
    edge = XT // 16
    plane = pl.BlockSpec((1, XT, strip), lambda i: (0, start + i, 0))
    block = pl.BlockSpec((depth, XT, strip), lambda i: (0, start + i, 0))
    ends = [
        lambda i: (0, jnp.maximum((start + i) * edge - 1, 0), 0),
        lambda i: (0, jnp.minimum((start + i + 1) * edge, count * edge - 1), 0),
    ]
    specs = [SMEM, SMEM, block]
    specs += [pl.BlockSpec((depth, 16, strip), where) for where in ends]
    specs += [plane] * 2 + [ANY] * len(order)
    before = [] if done is None else [done]
    return pl.pallas_call(
        functools.partial(regularizer_kernel, start, count),
        grid=(length,),
        out_shape=jax.ShapeDtypeStruct(volume.shape, BF16),
        in_specs=specs + [ANY] * len(before),
        out_specs=block,
        scratch_shapes=[pltpu.VMEM((XT, strip), F32)],
        input_output_aliases={len(specs): 0} if before else {},
        cost_estimate=cost(30 * volume.size // PIECES, 8 * volume.size // PIECES),
        name="regularizer",
    )(place, beta, volume, volume, volume, below, above, *order, *before)


def gradient_kernel(place_ref, beta_ref, spread_ref, mine_ref, beside_ref, *refs):
    chunk_refs = refs[:-2]
    regular_ref, out_ref = refs[-2:]
    depth, tile, strip = out_ref.shape
    beta = beta_ref[0]
    has_left = (place_ref[1] > 0).astype(F32)
    has_right = (place_ref[1] < place_ref[2] - 1).astype(F32)
    mine, beside = mine_ref[...].astype(F32), beside_ref[...].astype(F32)
    on_left = penalty(mine[:8] - beside[:8]) * (has_left * beta)
    on_right = penalty(mine[8:] - beside[8:]) * (has_right * beta)
    ends = jnp.concatenate([on_left, on_right], axis=0).astype(BF16)
    rows = jnp.concatenate([ref[...] for ref in chunk_refs] + [ends], axis=0)
    out = lax.dot_general(
        rows, spread_ref[...], (((0,), (0,)), ((), ())), preferred_element_type=F32
    )
    for z in range(depth):
        regular = regular_ref[z].astype(F32)
        out_ref[z] = (out[:, z * strip : (z + 1) * strip] + regular).astype(BF16)


def gradient(place, beta, spread, mine, arrived, chunks, regular):
    depth, extent, strip = regular.shape
    block = pl.BlockSpec((depth, XT, strip), lambda i: (0, i, 0))
    size = depth * extent * strip
    return pl.pallas_call(
        gradient_kernel,
        grid=(extent // XT,),
        out_shape=jax.ShapeDtypeStruct(regular.shape, BF16),
        in_specs=[
            SMEM,
            SMEM,
            pl.BlockSpec(spread.shape, lambda i: (0, 0)),
            pl.BlockSpec((LINES, XT), lambda i: (PAIR // LINES, i)),
            pl.BlockSpec((LINES, XT), lambda i: (RUN // LINES, i)),
        ]
        + [pl.BlockSpec((chunk.shape[0], XT), lambda i: (0, i)) for chunk in chunks]
        + [block],
        out_specs=block,
        compiler_params=limit(16),
        cost_estimate=cost(2 * spread.shape[0] * size, 5 * size),
        name="gradient",
    )(place, beta, spread, mine, arrived, *chunks, regular)


def shards(volume, measured, ray_weight, view_owner, band_offset, band_width, beta):
    slabs = lax.axis_size("slab")
    tiles = lax.axis_size("tile")
    slab, tile = lax.axis_index("slab"), lax.axis_index("tile")
    depth = volume.shape[0]
    place = jnp.stack([slab, tile, jnp.int32(tiles), jnp.int32(slabs)])

    def along_z(block, by):
        return lax.ppermute(block, "tile", [(i, (i + 2 * by) % tiles) for i in range(tiles)])

    def along_y(block):
        return lax.ppermute(block, "tile", [(i, i ^ 1) for i in range(tiles)])

    packed = pack(view_owner[:, :, 0], band_offset, band_width, ray_weight, measured, slabs)
    packed, after = lax.optimization_barrier((packed, volume))
    got = lax.all_to_all(packed, "slab", split_axis=0, concat_axis=0, tiled=True)
    top, bottom = after[depth - 1 :], after[:1]
    below = lax.ppermute(top, "slab", [(i, i + 1) for i in range(slabs - 1)])
    above = lax.ppermute(bottom, "slab", [(i + 1, i) for i in range(slabs - 1)])
    flat = got.reshape(slabs * SLOTS, ROWS, BAND)

    own, up1, down1, up2, down2, up3, down3, far_up, far_down = forward(
        place, flat, volume, tiles, top, bottom
    )
    mine = up1
    near = along_z(up3, 1), along_z(down3, -1)
    far = along_z(far_up, 2), along_z(far_down, -2)
    one = along_z(up1, 1), along_z(down1, -1)
    regular = regularizer(0, None, place, beta, volume, below, above, far_up)
    up, down = round_sums(up2, near[0], far[0], down2, near[1], far[1], regular)
    got, up = lax.optimization_barrier((got, up))
    two = along_z(up, 2), along_z(down, -2)
    views = lax.all_to_all(got, "tile", split_axis=0, concat_axis=0, tiled=True)
    kept, sent = last_sums(place, own, up1, *one, *two, views)
    arrived = along_y(sent)
    regular = regularizer(1, regular, place, beta, volume, below, above, sent)
    images = residual_images(kept, arrived, views, regular)

    partner = along_y(images)
    regular = regularizer(2, regular, place, beta, volume, below, above, images)
    pair = jnp.concatenate([images, partner], axis=0)
    pair, regular = lax.optimization_barrier((pair, regular))
    up2, down2 = along_z(pair, 2), along_z(pair, -2)
    up1, down1 = along_z(pair, 1), along_z(pair, -1)
    spread = spread_rows(place, flat, tiles, pair)
    regular = regularizer(3, regular, place, beta, volume, below, above, pair, spread)
    up2, down2, regular = lax.optimization_barrier((up2, down2, regular))
    up3, down3 = along_z(up2, 1), along_z(down2, -1)
    far_up, far_down = along_z(up2[:RUN], 2), along_z(down2[RUN:], -2)
    chunks = [pair, down1, up1, down2, up2, down3, up3, far_up, far_down]
    return gradient(place, beta, spread, mine, arrived, chunks, regular)


def solution(mesh):
    in_specs = (
        P("slab", None, "tile"),
        P(None, "slab", None, "tile"),
        P(None, "slab", "tile"),
        P(None, "slab", None),
        P(None, "slab"),
        P(None, "slab"),
        P(),
    )
    out_specs = P("slab", None, "tile")
    return jax.shard_map(shards, mesh=mesh, in_specs=in_specs, out_specs=out_specs, check_vma=False)
```

```python
import functools

import jax
import jax.numpy as jnp
from jax import lax
from jax.experimental import pallas as pl
from jax.experimental.pallas import tpu as pltpu
from jax.sharding import PartitionSpec as P

BAND = 128
BATCHES = 2
CAPP = 2
SLOTS = BATCHES * CAPP
ROWS = 16
RUN = SLOTS * 8
PAIR = 2 * RUN
LINES = 16
EDGE = 16
PIECES = 4


def limit(mib):
    return pltpu.CompilerParams(vmem_limit_bytes=mib << 20)

XT = 256
F32 = jnp.float32
BF16 = jnp.bfloat16
VMEM = pl.BlockSpec(memory_space=pltpu.VMEM)
SMEM = pl.BlockSpec(memory_space=pltpu.SMEM)
ANY = pl.BlockSpec(memory_space=pl.ANY)
HBM = pl.BlockSpec(memory_space=pltpu.HBM)


def cost(flops, moved):
    return pl.CostEstimate(flops=flops, bytes_accessed=moved, transcendentals=0)


def iota(shape, dim):
    return lax.broadcasted_iota(jnp.int32, shape, dim)


def pack_kernel(owner_ref, offset_ref, width_ref, weight_ref, measured_ref, out_ref, count_ref):
    out_ref[...] = jnp.zeros_like(out_ref)
    slabs = out_ref.shape[0]
    views = owner_ref.shape[1]
    row = iota((ROWS, BAND), 0)
    lane = iota((ROWS, BAND), 1)
    empty = jnp.zeros((8, BAND), F32)
    for batch in range(BATCHES):
        for slab in range(slabs):
            count_ref[slab] = 0
        for view in range(views):
            owner = owner_ref[batch, view]
            rank = count_ref[owner]
            count_ref[owner] = rank + 1
            rows = jnp.concatenate([measured_ref[batch, view].astype(F32), empty], axis=0)
            band = jnp.where(
                lane == 0,
                offset_ref[batch, view].astype(F32),
                jnp.where(lane == 1, width_ref[batch, view].astype(F32), 0.0),
            )
            rows = jnp.where(row == 8, weight_ref[view].astype(F32)[batch : batch + 1], jnp.where(row == 9, band, rows))
            out_ref[owner, batch * CAPP + rank] = rows.astype(BF16)


def pack(owner, offset, width, weight, measured, slabs):
    return pl.pallas_call(
        pack_kernel,
        out_shape=jax.ShapeDtypeStruct((slabs, SLOTS, ROWS, BAND), BF16),
        in_specs=[SMEM, SMEM, SMEM, VMEM, VMEM],
        out_specs=VMEM,
        scratch_shapes=[pltpu.SMEM((slabs,), jnp.int32)],
        name="pack_messages",
    )(owner, offset, width, jnp.transpose(weight, (1, 0, 2)), measured)


def joined(block):
    return jnp.concatenate([block[z] for z in range(block.shape[0])], axis=1)


def streamed(ref, buffer_ref, sem_ref, first, edge=0):
    step, steps = pl.program_id(0), pl.num_programs(0)
    extent = ref.shape[1]

    def copies(index):
        slot = lax.rem(index, 2)
        start = (first + index) * XT
        parts = [(start, edge, XT)]
        if edge:
            parts.append((jnp.maximum(start - edge, 0), 0, edge))
            parts.append((jnp.minimum(start + XT, extent - edge), edge + XT, edge))
        return [
            pltpu.make_async_copy(
                ref.at[:, pl.ds(pl.multiple_of(source, 16), size)],
                buffer_ref.at[slot, :, pl.ds(target, size)],
                sem_ref.at[slot, part],
            )
            for part, (source, target, size) in enumerate(parts)
        ]

    @pl.when(step == 0)
    def _():
        for copy in copies(step):
            copy.start()

    @pl.when(step + 1 < steps)
    def _():
        for copy in copies(step + 1):
            copy.start()

    for copy in copies(step):
        copy.wait()
    return buffer_ref.at[lax.rem(step, 2)]


def stream_scratch(depth, strip, edge=0):
    return [
        pltpu.VMEM((2, depth, XT + 2 * edge, strip), BF16),
        pltpu.SemaphoreType.DMA((2, 3 if edge else 1)),
    ]


def spread_weights(tiles, out_ref, first, depth):
    rows = tiles.shape[0] * depth
    weights = jnp.broadcast_to(
        tiles.astype(F32)[:, 8:9, :], (tiles.shape[0], depth, BAND)
    ).reshape(rows, BAND)
    slice_of = lax.rem(iota((rows, BAND), 0), depth)
    for z in range(depth):
        out_ref[first : first + rows, z * BAND : (z + 1) * BAND] = jnp.where(
            slice_of == z, weights, 0.0
        ).astype(BF16)


def hops(tiles):
    half = tiles // 4
    return [0] + [sign * hop for hop in range(1, half) for sign in (1, -1)] + [half]


def fill_spread(tiles, me, got_ref, spread_ref):
    row = 0
    for hop in hops(tiles):
        tile = lax.rem(me + 2 * hop + tiles, tiles)
        for source in (tile, tile ^ 1):
            spread_weights(got_ref[pl.ds(source * SLOTS, SLOTS)], spread_ref, row, 8)
            row += RUN
    shape = (LINES, spread_ref.shape[1])
    line = iota(shape, 0)
    target = jnp.where(line < 8, line * BAND, (line - 8) * BAND + BAND - 1)
    spread_ref[row:] = jnp.where(iota(shape, 1) == target, 1.0, 0.0).astype(BF16)


def spread_kernel(tiles, place_ref, got_ref, order_ref, out_ref, views_ref):
    fill_spread(tiles, place_ref[1], got_ref, out_ref)
    views_ref[...] = got_ref[...]


def spread_rows(place, got, tiles, order):
    shape = (got.shape[0] * 8 + LINES, 8 * BAND)
    return pl.pallas_call(
        functools.partial(spread_kernel, tiles),
        out_shape=(
            jax.ShapeDtypeStruct(shape, BF16),
            jax.ShapeDtypeStruct(got.shape, BF16),
        ),
        in_specs=[SMEM, VMEM, ANY],
        out_specs=(VMEM, VMEM),
        compiler_params=limit(8),
        cost_estimate=cost(4 * shape[0] * shape[1], 4 * shape[0] * shape[1]),
        name="spread_rows",
    )(place, got, order)


def forward_kernel(tiles, place_ref, got_ref, volume_ref, *refs):
    outs, (spread_ref, buffer_ref, sem_ref) = refs[:-3], refs[-3:]
    block_ref = streamed(volume_ref, buffer_ref, sem_ref, 0)

    @pl.when(pl.program_id(0) == 0)
    def _():
        fill_spread(tiles, place_ref[1], got_ref, spread_ref)

    out = lax.dot_general(
        spread_ref[...], joined(block_ref), (((1,), (1,)), ((), ())), preferred_element_type=F32
    ).astype(BF16)
    row = 0
    for ref in outs:
        count = min(ref.shape[0], PAIR)
        ref[:count] = out[row : row + count]
        if ref.shape[0] > PAIR:
            ref[PAIR:] = out[-LINES:]
        row += count


def forward(place, got, volume, tiles, *order):
    depth, extent, strip = volume.shape
    slots = got.shape[0]
    rows = [PAIR] + [PAIR + LINES] * 2 + [PAIR] * (tiles // 2 - 4) + [RUN] * 2

    def kernel(place_ref, got_ref, volume_ref, *refs):
        forward_kernel(tiles, place_ref, got_ref, volume_ref, *refs[len(order) :])

    return pl.pallas_call(
        kernel,
        grid=(extent // XT,),
        out_shape=[jax.ShapeDtypeStruct((count, extent), BF16) for count in rows],
        in_specs=[
            SMEM,
            pl.BlockSpec(got.shape, lambda i: (0, 0, 0)),
            HBM,
        ]
        + [ANY] * len(order),
        out_specs=[pl.BlockSpec((count, XT), lambda i: (0, i)) for count in rows],
        scratch_shapes=[pltpu.VMEM((slots * depth + LINES, depth * strip), BF16)]
        + stream_scratch(depth, strip),
        compiler_params=limit(10),
        cost_estimate=cost(2 * slots * depth * volume.size, 3 * volume.size),
        name="forward",
    )(place, got, volume, *order)


def sums_kernel(up_ref, up_near_ref, up_far_ref, down_ref, down_near_ref, down_far_ref, *refs):
    up_out_ref, down_out_ref = refs[-2:]

    def add(*parts):
        return functools.reduce(jnp.add, [part.astype(F32) for part in parts]).astype(BF16)

    up_out_ref[:RUN] = add(up_ref[:RUN], up_near_ref[:RUN], up_far_ref[...])
    up_out_ref[RUN:] = add(up_ref[RUN:], up_near_ref[RUN:])
    down_out_ref[:RUN] = add(down_ref[:RUN], down_near_ref[:RUN])
    down_out_ref[RUN:] = add(down_ref[RUN:], down_near_ref[RUN:], down_far_ref[...])


def round_sums(*operands):
    out = jax.ShapeDtypeStruct(operands[0].shape, BF16)
    return pl.pallas_call(
        sums_kernel,
        out_shape=(out, out),
        in_specs=[VMEM] * 6 + [ANY] * (len(operands) - 6),
        out_specs=(VMEM, VMEM),
        compiler_params=limit(8),
        cost_estimate=cost(6 * out.size, 14 * out.size),
        name="round_sums",
    )(*operands)


def last_sums_kernel(
    place_ref, own_ref, mine_ref, below_ref, above_ref, up_ref, down_ref, *refs
):
    kept_ref, sent_ref = refs[-2:]
    total = (
        own_ref[...].astype(F32)
        + below_ref[:PAIR].astype(F32)
        + above_ref[:PAIR].astype(F32)
        + up_ref[...].astype(F32)
        + down_ref[...].astype(F32)
    )
    kept_ref[...] = total[:RUN]
    sent_ref[:RUN] = total[RUN:].astype(BF16)
    mine, below, above = [ref[PAIR:].astype(F32) for ref in (mine_ref, below_ref, above_ref)]
    even = place_ref[1] % 2 == 0
    left = jnp.where(even, mine[8:], below[8:])
    right = jnp.where(even, above[:8], mine[:8])
    sent_ref[RUN:] = jnp.concatenate([left, right], axis=0).astype(BF16)


def last_sums(place, own, mine, below, above, up, down, *order):
    extent = own.shape[1]
    return pl.pallas_call(
        last_sums_kernel,
        out_shape=(
            jax.ShapeDtypeStruct((RUN, extent), F32),
            jax.ShapeDtypeStruct((RUN + LINES, extent), BF16),
        ),
        in_specs=[SMEM] + [VMEM] * 6 + [ANY] * len(order),
        out_specs=(VMEM, VMEM),
        compiler_params=limit(8),
        cost_estimate=cost(5 * own.size, 14 * own.size),
        name="last_sums",
    )(place, own, mine, below, above, up, down, *order)


def residual_kernel(kept_ref, arrived_ref, views_ref, *refs):
    out_ref = refs[-1]
    extent = kept_ref.shape[1]
    blocks = extent // BAND
    empty = jnp.zeros((8, BAND), F32)
    arrived = arrived_ref[:RUN].astype(F32)
    for slot in range(SLOTS):
        low = slot * 8
        total = kept_ref[low : low + 8] + arrived[low : low + 8]
        band = views_ref[0, slot].astype(F32)
        offset = band[9:10, 0:1].astype(jnp.int32)
        width = jnp.maximum(band[9:10, 1:2], 1.0)
        recip = 1.0 / width
        width = width.astype(jnp.int32)

        def inside(delta):
            delta = delta - offset
            return jnp.where((delta >= 0) & (delta < width), recip, 0.0).astype(BF16)

        shape = (2 * BAND, BAND)
        onward = inside(iota(shape, 1) + BAND - iota(shape, 0))
        back = inside(iota(shape, 0) - iota(shape, 1))
        parts = [total[:, n * BAND : (n + 1) * BAND] for n in range(blocks)]
        here = jnp.concatenate(parts, axis=0)
        before = jnp.concatenate([empty] + parts[:-1], axis=0)
        paired = jnp.concatenate([before, here], axis=1)
        high = paired.astype(BF16)
        rest = (paired - high.astype(F32)).astype(BF16)
        sums = jnp.dot(high, onward, preferred_element_type=F32) + jnp.dot(
            rest, onward, preferred_element_type=F32
        )
        rows = jnp.concatenate(
            [views_ref[n, slot].astype(F32)[:8] for n in range(blocks)], axis=0
        )
        residual = (sums - rows).astype(BF16).astype(F32)
        later = jnp.concatenate([residual[8:], empty], axis=0)
        both = jnp.concatenate([residual, later], axis=1).astype(BF16)
        image = jnp.dot(both, back, preferred_element_type=F32)
        image = jnp.concatenate([image[n * 8 : (n + 1) * 8] for n in range(blocks)], axis=1)
        if slot % 2 == 0:
            even = image
        else:
            out_ref[low - 8 : low + 8] = jnp.concatenate([even, image], axis=0).astype(BF16)


def residual_images(kept, arrived, views, *order):
    return pl.pallas_call(
        residual_kernel,
        out_shape=jax.ShapeDtypeStruct(kept.shape, BF16),
        in_specs=[VMEM] * 3 + [ANY] * len(order),
        out_specs=VMEM,
        compiler_params=limit(8),
        cost_estimate=cost(4 * 8 * 16 * 256 * 128 * 6, 2 * views.size),
        name="residual_images",
    )(kept, arrived, views, *order)


def join_kernel(first_ref, second_ref, order_ref, out_ref):
    out_ref[:RUN] = first_ref[...]
    out_ref[RUN:] = second_ref[...]


def join(first, second, order):
    return pl.pallas_call(
        join_kernel,
        out_shape=jax.ShapeDtypeStruct((PAIR, first.shape[1]), BF16),
        in_specs=[VMEM, VMEM, ANY],
        out_specs=VMEM,
        compiler_params=limit(8),
        cost_estimate=cost(0, 8 * first.size),
        name="join",
    )(first, second, order)


def penalty(diff):
    return diff * lax.rsqrt(1.0 + diff * diff)


def regularizer_kernel(
    first_tile,
    count,
    place_ref,
    beta_ref,
    volume_ref,
    below_ref,
    above_ref,
    *refs,
):
    out_ref, token_ref, under_ref, buffer_ref, sem_ref = refs[-5:]
    block_ref = streamed(volume_ref, buffer_ref, sem_ref, first_tile, EDGE)
    depth, strip, tile = block_ref.shape[0], block_ref.shape[2], XT
    at = pl.program_id(0) + first_tile
    beta = beta_ref[0]
    has_below = (place_ref[0] > 0).astype(F32)
    has_above = (place_ref[0] < place_ref[3] - 1).astype(F32)
    has_before = (at > 0).astype(F32)
    has_after = (at < count - 1).astype(F32)
    here = pl.ds(EDGE, tile)
    under_ref[...] = (
        penalty(block_ref[0, here].astype(F32) - below_ref[0].astype(F32)) * has_below
    )
    row = iota((tile, strip), 0)
    lane = iota((tile, strip), 1)

    def body(z, carry):
        center = block_ref[z, here].astype(F32)
        top = z == depth - 1
        upper = jnp.where(top, above_ref[0], block_ref[jnp.minimum(z + 1, depth - 1), here])
        over = penalty(upper.astype(F32) - center) * jnp.where(top, has_above, 1.0)
        total = under_ref[...] - over
        under_ref[...] = over
        ahead = block_ref[z, pl.ds(EDGE + tile, EDGE)].astype(F32)[0:1]
        behind = block_ref[z, pl.ds(0, EDGE)].astype(F32)[EDGE - 1 :]
        behind = penalty(center[0:1] - behind) * has_before
        along = penalty(jnp.where(row == tile - 1, ahead, pltpu.roll(center, tile - 1, 0)) - center)
        along = jnp.where(row == tile - 1, along * has_after, along)
        total = total + jnp.where(row == 0, behind, pltpu.roll(along, 1, 0)) - along
        across = penalty(pltpu.roll(center, strip - 1, 1) - center)
        across = jnp.where(lane == strip - 1, 0.0, across)
        total = total + pltpu.roll(across, 1, 1) - across
        out_ref[z] = (total * beta).astype(BF16)
        return carry

    lax.fori_loop(0, depth, body, 0, unroll=2)
    token_ref[...] = under_ref[:8]


def regularizer(index, done, place, beta, volume, below, above, *order):
    depth, extent, strip = volume.shape
    count = extent // XT
    length = count // PIECES
    start = index * length
    plane = pl.BlockSpec((1, XT, strip), lambda i: (0, start + i, 0))
    block = pl.BlockSpec((depth, XT, strip), lambda i: (0, start + i, 0))
    specs = [SMEM, SMEM, HBM]
    specs += [plane] * 2 + [ANY] * len(order)
    before = [] if done is None else [done]
    return pl.pallas_call(
        functools.partial(regularizer_kernel, start, count),
        grid=(length,),
        out_shape=(pltpu.HBM(volume.shape, BF16), jax.ShapeDtypeStruct((8, strip), F32)),
        in_specs=specs + [HBM] * len(before),
        out_specs=(block, pl.BlockSpec((8, strip), lambda i: (0, 0))),
        scratch_shapes=[pltpu.VMEM((XT, strip), F32)] + stream_scratch(depth, strip, EDGE),
        compiler_params=limit(8),
        input_output_aliases={len(specs): 0} if before else {},
        cost_estimate=cost(30 * volume.size // PIECES, 8 * volume.size // PIECES),
        name="regularizer",
    )(place, beta, volume, below, above, *order, *before)


def gradient_kernel(place_ref, beta_ref, spread_ref, mine_ref, beside_ref, *refs):
    chunk_refs = refs[:-4]
    whole_ref, out_ref, buffer_ref, sem_ref = refs[-4:]
    regular_ref = streamed(whole_ref, buffer_ref, sem_ref, 0)
    depth, tile, strip = out_ref.shape
    beta = beta_ref[0]
    has_left = (place_ref[1] > 0).astype(F32)
    has_right = (place_ref[1] < place_ref[2] - 1).astype(F32)
    mine, beside = mine_ref[...].astype(F32), beside_ref[...].astype(F32)
    on_left = penalty(mine[:8] - beside[:8]) * (has_left * beta)
    on_right = penalty(mine[8:] - beside[8:]) * (has_right * beta)
    ends = jnp.concatenate([on_left, on_right], axis=0).astype(BF16)
    rows = jnp.concatenate([ref[...] for ref in chunk_refs] + [ends], axis=0)
    out = lax.dot_general(
        rows, spread_ref[...], (((0,), (0,)), ((), ())), preferred_element_type=F32
    )
    for z in range(depth):
        regular = regular_ref[z].astype(F32)
        out_ref[z] = (out[:, z * strip : (z + 1) * strip] + regular).astype(BF16)


def gradient(place, beta, spread, mine, arrived, chunks, regular):
    depth, extent, strip = regular.shape
    block = pl.BlockSpec((depth, XT, strip), lambda i: (0, i, 0))
    size = depth * extent * strip
    return pl.pallas_call(
        gradient_kernel,
        grid=(extent // XT,),
        out_shape=jax.ShapeDtypeStruct(regular.shape, BF16),
        in_specs=[
            SMEM,
            SMEM,
            pl.BlockSpec(spread.shape, lambda i: (0, 0)),
            pl.BlockSpec((LINES, XT), lambda i: (PAIR // LINES, i)),
            pl.BlockSpec((LINES, XT), lambda i: (RUN // LINES, i)),
        ]
        + [pl.BlockSpec((chunk.shape[0], XT), lambda i: (0, i)) for chunk in chunks]
        + [HBM],
        out_specs=block,
        scratch_shapes=stream_scratch(depth, strip),
        compiler_params=limit(12),
        cost_estimate=cost(2 * spread.shape[0] * size, 5 * size),
        name="gradient",
    )(place, beta, spread, mine, arrived, *chunks, regular)


def shards(volume, measured, ray_weight, view_owner, band_offset, band_width, beta):
    slabs = lax.axis_size("slab")
    tiles = lax.axis_size("tile")
    slab, tile = lax.axis_index("slab"), lax.axis_index("tile")
    depth = volume.shape[0]
    place = jnp.stack([slab, tile, jnp.int32(tiles), jnp.int32(slabs)])

    def along_z(block, by):
        return lax.ppermute(block, "tile", [(i, (i + 2 * by) % tiles) for i in range(tiles)])

    def along_y(block):
        return lax.ppermute(block, "tile", [(i, i ^ 1) for i in range(tiles)])

    packed = pack(view_owner[:, :, 0], band_offset, band_width, ray_weight, measured, slabs)
    packed, after = lax.optimization_barrier((packed, volume))
    got = lax.all_to_all(packed, "slab", split_axis=0, concat_axis=0, tiled=True)
    top, bottom = after[depth - 1 :], after[:1]
    below = lax.ppermute(top, "slab", [(i, i + 1) for i in range(slabs - 1)])
    above = lax.ppermute(bottom, "slab", [(i + 1, i) for i in range(slabs - 1)])
    flat = got.reshape(slabs * SLOTS, ROWS, BAND)
    volume = pltpu.with_memory_space_constraint(volume, pltpu.HBM)

    own, up1, down1, up2, down2, up3, down3, far_up, far_down = forward(
        place, flat, volume, tiles, top, bottom
    )
    mine = up1
    near = along_z(up3, 1), along_z(down3, -1)
    far = along_z(far_up, 2), along_z(far_down, -2)
    one = along_z(up1, 1), along_z(down1, -1)
    regular, token = regularizer(0, None, place, beta, volume, below, above, far_up)
    up, down = round_sums(up2, near[0], far[0], down2, near[1], far[1], token, *one)
    two = along_z(up, 2), along_z(down, -2)
    spread, views = spread_rows(place, flat, tiles, up)
    views = views.reshape(got.shape)
    views = lax.all_to_all(views, "tile", split_axis=0, concat_axis=0, tiled=True)
    kept, sent = last_sums(place, own, up1, *one, *two, views)
    arrived = along_y(sent)
    regular, token = regularizer(1, regular, place, beta, volume, below, above, sent)
    images = residual_images(kept, arrived, views, token)

    partner = along_y(images)
    regular, token = regularizer(2, regular, place, beta, volume, below, above, images)
    pair = join(images, partner, token)
    up2, down2 = along_z(pair, 2), along_z(pair, -2)
    up1, down1 = along_z(pair, 1), along_z(pair, -1)
    regular, token = regularizer(3, regular, place, beta, volume, below, above, pair)
    up3, down3 = along_z(up2, 1), along_z(down2, -1)
    far_up, far_down = along_z(up2[:RUN], 2), along_z(down2[RUN:], -2)
    chunks = [pair, down1, up1, down2, up2, down3, up3, far_up, far_down]
    regular = pltpu.with_memory_space_constraint(regular, pltpu.HBM)
    return gradient(place, beta, spread, mine, arrived, chunks, regular)


def solution(mesh):
    in_specs = (
        P("slab", None, "tile"),
        P(None, "slab", None, "tile"),
        P(None, "slab", "tile"),
        P(None, "slab", None),
        P(None, "slab"),
        P(None, "slab"),
        P(),
    )
    out_specs = P("slab", None, "tile")
    return jax.shard_map(shards, mesh=mesh, in_specs=in_specs, out_specs=out_specs, check_vma=False)
```

```python
import functools

import jax
import jax.numpy as jnp
from jax import lax
from jax.experimental import pallas as pl
from jax.experimental.pallas import tpu as pltpu
from jax.sharding import PartitionSpec as P

BAND = 128
BATCHES = 2
CAPP = 2
SLOTS = BATCHES * CAPP
ROWS = 16
RUN = SLOTS * 8
PAIR = 2 * RUN
LINES = 16
EDGE = 16
PIECES = 4


def limit(mib):
    return pltpu.CompilerParams(vmem_limit_bytes=mib << 20)

XT = 256
F32 = jnp.float32
BF16 = jnp.bfloat16
VMEM = pl.BlockSpec(memory_space=pltpu.VMEM)
SMEM = pl.BlockSpec(memory_space=pltpu.SMEM)
ANY = pl.BlockSpec(memory_space=pl.ANY)
HBM = pl.BlockSpec(memory_space=pltpu.HBM)


def cost(flops, moved):
    return pl.CostEstimate(flops=flops, bytes_accessed=moved, transcendentals=0)


def iota(shape, dim):
    return lax.broadcasted_iota(jnp.int32, shape, dim)


def pack_kernel(owner_ref, offset_ref, width_ref, weight_ref, measured_ref, out_ref, count_ref):
    out_ref[...] = jnp.zeros_like(out_ref)
    slabs = out_ref.shape[0]
    views = owner_ref.shape[1]
    row = iota((ROWS, BAND), 0)
    lane = iota((ROWS, BAND), 1)
    empty = jnp.zeros((8, BAND), F32)
    for batch in range(BATCHES):
        for slab in range(slabs):
            count_ref[slab] = 0
        for view in range(views):
            owner = owner_ref[batch, view]
            rank = count_ref[owner]
            count_ref[owner] = rank + 1
            rows = jnp.concatenate([measured_ref[batch, view].astype(F32), empty], axis=0)
            band = jnp.where(
                lane == 0,
                offset_ref[batch, view].astype(F32),
                jnp.where(lane == 1, width_ref[batch, view].astype(F32), 0.0),
            )
            rows = jnp.where(row == 8, weight_ref[view].astype(F32)[batch : batch + 1], jnp.where(row == 9, band, rows))
            out_ref[owner, batch * CAPP + rank] = rows.astype(BF16)


def pack(owner, offset, width, weight, measured, slabs):
    return pl.pallas_call(
        pack_kernel,
        out_shape=jax.ShapeDtypeStruct((slabs, SLOTS, ROWS, BAND), BF16),
        in_specs=[SMEM, SMEM, SMEM, VMEM, VMEM],
        out_specs=VMEM,
        scratch_shapes=[pltpu.SMEM((slabs,), jnp.int32)],
        name="pack_messages",
    )(owner, offset, width, jnp.transpose(weight, (1, 0, 2)), measured)


def joined(block):
    return jnp.concatenate([block[z] for z in range(block.shape[0])], axis=1)


def tile_copies(ref, buffer_ref, sem_ref, index, first=0, edge=0):
    slot = lax.rem(index, 2)
    extent = ref.shape[1]
    start = (first + index) * XT
    parts = [(start, edge, XT)]
    if edge:
        parts.append((jnp.maximum(start - edge, 0), 0, edge))
        parts.append((jnp.minimum(start + XT, extent - edge), edge + XT, edge))
    return [
        pltpu.make_async_copy(
            ref.at[:, pl.ds(pl.multiple_of(source, 16), size)],
            buffer_ref.at[slot, :, pl.ds(target, size)],
            sem_ref.at[slot, part],
        )
        for part, (source, target, size) in enumerate(parts)
    ]


def start(copies):
    for copy in copies:
        copy.start()


def streamed(ref, buffer_ref, sem_ref, step, steps, first=0, edge=0):
    @pl.when(step + 1 < steps)
    def _():
        start(tile_copies(ref, buffer_ref, sem_ref, step + 1, first, edge))

    for copy in tile_copies(ref, buffer_ref, sem_ref, step, first, edge):
        copy.wait()
    return buffer_ref.at[lax.rem(step, 2)]


def stream_scratch(depth, strip, edge=0):
    return [
        pltpu.VMEM((2, depth, XT + 2 * edge, strip), BF16),
        pltpu.SemaphoreType.DMA((2, 3 if edge else 1)),
    ]


def spread_weights(tiles, out_ref, first, depth):
    rows = tiles.shape[0] * depth
    weights = jnp.broadcast_to(
        tiles.astype(F32)[:, 8:9, :], (tiles.shape[0], depth, BAND)
    ).reshape(rows, BAND)
    slice_of = lax.rem(iota((rows, BAND), 0), depth)
    for z in range(depth):
        out_ref[first : first + rows, z * BAND : (z + 1) * BAND] = jnp.where(
            slice_of == z, weights, 0.0
        ).astype(BF16)


def hops(tiles):
    half = tiles // 4
    return [0] + [sign * hop for hop in range(1, half) for sign in (1, -1)] + [half]


def fill_spread(tiles, me, got_ref, spread_ref):
    row = 0
    for hop in hops(tiles):
        tile = lax.rem(me + 2 * hop + tiles, tiles)
        for source in (tile, tile ^ 1):
            spread_weights(got_ref[pl.ds(source * SLOTS, SLOTS)], spread_ref, row, 8)
            row += RUN
    shape = (LINES, spread_ref.shape[1])
    line = iota(shape, 0)
    target = jnp.where(line < 8, line * BAND, (line - 8) * BAND + BAND - 1)
    spread_ref[row:] = jnp.where(iota(shape, 1) == target, 1.0, 0.0).astype(BF16)


def spread_kernel(tiles, place_ref, got_ref, order_ref, out_ref):
    fill_spread(tiles, place_ref[1], got_ref, out_ref)


def spread_rows(place, got, tiles, order):
    shape = (got.shape[0] * 8 + LINES, 8 * BAND)
    return pl.pallas_call(
        functools.partial(spread_kernel, tiles),
        out_shape=jax.ShapeDtypeStruct(shape, BF16),
        in_specs=[SMEM, VMEM, ANY],
        out_specs=VMEM,
        compiler_params=limit(8),
        cost_estimate=cost(4 * shape[0] * shape[1], 4 * shape[0] * shape[1]),
        name="spread_rows",
    )(place, got, order)


def measured_rows(got_ref, source):
    rows = got_ref[pl.ds(source * SLOTS, SLOTS)].astype(F32)[:, :8]
    return rows.reshape(RUN, BAND).astype(BF16)


PLACES = {
    0: [(0, 0), (0, RUN)],
    1: [(3, PAIR), (3, PAIR + RUN)],
    -1: [(4, PAIR), (4, PAIR + RUN)],
    2: [(1, 0), (1, RUN)],
    -2: [(2, 0), (2, RUN)],
    3: [(3, 0), (3, RUN)],
    -3: [(4, 0), (4, RUN)],
    4: [(5, 0), (6, 0)],
}
NEAR = 2 * PAIR + LINES


def forward_kernel(tiles, place_ref, got_ref, volume_ref, *refs):
    outs, (spread_ref, buffer_ref, sem_ref) = refs[:-3], refs[-3:]
    extent = volume_ref.shape[1]
    me = place_ref[1]
    start(tile_copies(volume_ref, buffer_ref, sem_ref, 0))
    fill_spread(tiles, me, got_ref, spread_ref)
    where = [(outs[index], row) for hop in hops(tiles) for index, row in PLACES[hop]]
    beyond = pl.ds(extent, BAND)
    for index, hop in enumerate(hops(tiles)):
        tile = lax.rem(me + 2 * hop + tiles, tiles)
        for turn, source in enumerate((tile, tile ^ 1)):
            ref, row = where[2 * index + turn]
            ref[row : row + RUN, beyond] = measured_rows(got_ref, source)
    for ref in outs[3:5]:
        ref[NEAR - LINES :, beyond] = jnp.zeros((LINES, BAND), BF16)
    steps = extent // XT

    def body(step, carry):
        block_ref = streamed(volume_ref, buffer_ref, sem_ref, step, steps)
        out = lax.dot_general(
            spread_ref[...],
            joined(block_ref),
            (((1,), (1,)), ((), ())),
            preferred_element_type=F32,
        ).astype(BF16)
        here = pl.ds(pl.multiple_of(step * XT, XT), XT)
        for index, (ref, row) in enumerate(where):
            ref[row : row + RUN, here] = out[index * RUN : (index + 1) * RUN]
        for ref in outs[3:5]:
            ref[NEAR - LINES :, here] = out[-LINES:]
        return carry

    lax.fori_loop(0, steps, body, 0)


def forward(place, got, volume, tiles, *order):
    depth, extent, strip = volume.shape
    slots = got.shape[0]
    rows = [PAIR] * 3 + [NEAR] * 2 + [RUN] * 2

    def kernel(place_ref, got_ref, volume_ref, *refs):
        forward_kernel(tiles, place_ref, got_ref, volume_ref, *refs[len(order) :])

    return pl.pallas_call(
        kernel,
        out_shape=[jax.ShapeDtypeStruct((count, extent + BAND), BF16) for count in rows],
        in_specs=[SMEM, VMEM, HBM] + [ANY] * len(order),
        out_specs=[VMEM] * len(rows),
        scratch_shapes=[pltpu.VMEM((slots * depth + LINES, depth * strip), BF16)]
        + stream_scratch(depth, strip),
        compiler_params=limit(10),
        cost_estimate=cost(2 * slots * depth * volume.size, 3 * volume.size),
        name="forward",
    )(place, got, volume, *order)


def sums_kernel(up_ref, up_near_ref, up_far_ref, down_ref, down_near_ref, down_far_ref, *refs):
    extent = up_ref.shape[1] - BAND
    for own_ref, near_ref, far_ref, low, out_ref in (
        (up_ref, up_near_ref, up_far_ref, 0, refs[-2]),
        (down_ref, down_near_ref, down_far_ref, RUN, refs[-1]),
    ):
        for row in (0, RUN):
            rows = slice(row, row + RUN)
            total = own_ref[rows, :extent].astype(F32) + near_ref[rows, :extent].astype(F32)
            last = jnp.zeros((RUN, BAND), BF16)
            if row == low:
                total = total + far_ref[:, :extent].astype(F32)
                last = far_ref[:, extent:]
            out_ref[rows, :extent] = total.astype(BF16)
            out_ref[rows, extent : extent + BAND] = own_ref[rows, extent:]
            out_ref[rows, extent + BAND : extent + 2 * BAND] = near_ref[rows, extent:]
            out_ref[rows, extent + 2 * BAND :] = last


def round_sums(*operands):
    rows, lanes = operands[0].shape
    out = jax.ShapeDtypeStruct((rows, lanes + 2 * BAND), BF16)
    return pl.pallas_call(
        sums_kernel,
        out_shape=(out, out),
        in_specs=[VMEM] * 6 + [ANY] * (len(operands) - 6),
        out_specs=(VMEM, VMEM),
        compiler_params=limit(8),
        cost_estimate=cost(6 * out.size, 14 * out.size),
        name="round_sums",
    )(*operands)


STRIPS = (0, -1, 1, -2, 2, -3, 3, 4)


def last_sums_kernel(
    place_ref, own_ref, mine_ref, below_ref, above_ref, up_ref, down_ref, *refs
):
    kept_ref, strips_ref, sent_ref = refs[-3:]
    extent = own_ref.shape[1] - BAND
    for row in (0, RUN):
        rows, beside = slice(row, row + RUN), slice(PAIR + row, PAIR + row + RUN)
        total = (
            own_ref[rows, :extent].astype(F32)
            + below_ref[beside, :extent].astype(F32)
            + above_ref[beside, :extent].astype(F32)
            + up_ref[rows, :extent].astype(F32)
            + down_ref[rows, :extent].astype(F32)
        )
        near, far = slice(extent, extent + BAND), slice(extent + BAND, extent + 2 * BAND)
        across = slice(extent + 2 * BAND, extent + 3 * BAND)
        strips = [
            own_ref[rows, near],
            below_ref[beside, near],
            above_ref[beside, near],
            up_ref[rows, near],
            down_ref[rows, near],
            up_ref[rows, far],
            down_ref[rows, far],
            up_ref[rows, across] if row == 0 else down_ref[rows, across],
        ]
        if row == 0:
            kept_ref[...] = total
            for index, strip in enumerate(strips):
                strips_ref[:, index * BAND : (index + 1) * BAND] = strip
        else:
            sent_ref[:RUN] = total.astype(BF16)
            halves = [strip[low : low + 16] for strip in strips for low in (0, 16)]
            sent_ref[RUN + LINES :] = jnp.concatenate(halves, axis=1)
    mine, below, above = [
        ref[NEAR - LINES :, :extent].astype(F32) for ref in (mine_ref, below_ref, above_ref)
    ]
    even = place_ref[1] % 2 == 0
    left = jnp.where(even, mine[8:], below[8:])
    right = jnp.where(even, above[:8], mine[:8])
    sent_ref[RUN : RUN + LINES] = jnp.concatenate([left, right], axis=0).astype(BF16)


def last_sums(place, own, mine, below, above, up, down, *order):
    extent = own.shape[1] - BAND
    return pl.pallas_call(
        last_sums_kernel,
        out_shape=(
            jax.ShapeDtypeStruct((RUN, extent), F32),
            jax.ShapeDtypeStruct((RUN, len(STRIPS) * BAND), BF16),
            jax.ShapeDtypeStruct((RUN + LINES + 16, extent), BF16),
        ),
        in_specs=[SMEM] + [VMEM] * 6 + [ANY] * len(order),
        out_specs=(VMEM,) * 3,
        compiler_params=limit(8),
        cost_estimate=cost(5 * own.size, 14 * own.size),
        name="last_sums",
    )(place, own, mine, below, above, up, down, *order)


def residual_kernel(place_ref, kept_ref, strips_ref, arrived_ref, got_ref, *refs):
    out_ref, measured_ref = refs[-2:]
    extent = kept_ref.shape[1]
    blocks = extent // BAND
    me = place_ref[1]
    for index, hop in enumerate(STRIPS):
        tile = lax.rem(me + 2 * hop + blocks, blocks)
        measured_ref[tile] = strips_ref[:, index * BAND : (index + 1) * BAND].astype(F32)
        for half in (0, 1):
            lanes = slice((2 * index + half) * BAND, (2 * index + half + 1) * BAND)
            measured_ref[tile ^ 1, half * 16 : (half + 1) * 16] = arrived_ref[
                RUN + LINES :, lanes
            ].astype(F32)
    empty = jnp.zeros((8, BAND), F32)
    arrived = arrived_ref[:RUN].astype(F32)
    for slot in range(SLOTS):
        low = slot * 8
        total = kept_ref[low : low + 8] + arrived[low : low + 8]
        band = got_ref[me * SLOTS + slot].astype(F32)
        offset = band[9:10, 0:1].astype(jnp.int32)
        width = jnp.maximum(band[9:10, 1:2], 1.0)
        recip = 1.0 / width
        width = width.astype(jnp.int32)

        def inside(delta):
            delta = delta - offset
            return jnp.where((delta >= 0) & (delta < width), recip, 0.0).astype(BF16)

        shape = (2 * BAND, BAND)
        onward = inside(iota(shape, 1) + BAND - iota(shape, 0))
        back = inside(iota(shape, 0) - iota(shape, 1))
        parts = [total[:, n * BAND : (n + 1) * BAND] for n in range(blocks)]
        here = jnp.concatenate(parts, axis=0)
        before = jnp.concatenate([empty] + parts[:-1], axis=0)
        paired = jnp.concatenate([before, here], axis=1)
        high = paired.astype(BF16)
        rest = (paired - high.astype(F32)).astype(BF16)
        sums = jnp.dot(high, onward, preferred_element_type=F32) + jnp.dot(
            rest, onward, preferred_element_type=F32
        )
        rows = measured_ref[:, low : low + 8].reshape(blocks * 8, BAND)
        residual = (sums - rows).astype(BF16).astype(F32)
        later = jnp.concatenate([residual[8:], empty], axis=0)
        both = jnp.concatenate([residual, later], axis=1).astype(BF16)
        image = jnp.dot(both, back, preferred_element_type=F32)
        image = jnp.concatenate([image[n * 8 : (n + 1) * 8] for n in range(blocks)], axis=1)
        if slot % 2 == 0:
            even = image
        else:
            out_ref[low - 8 : low + 8] = jnp.concatenate([even, image], axis=0).astype(BF16)


def residual_images(place, kept, strips, arrived, got, *order):
    return pl.pallas_call(
        residual_kernel,
        out_shape=jax.ShapeDtypeStruct(kept.shape, BF16),
        in_specs=[SMEM] + [VMEM] * 4 + [ANY] * len(order),
        out_specs=VMEM,
        scratch_shapes=[pltpu.VMEM((kept.shape[1] // BAND, RUN, BAND), F32)],
        compiler_params=limit(8),
        cost_estimate=cost(4 * 8 * 16 * 256 * 128 * 6, 12 * kept.size),
        name="residual_images",
    )(place, kept, strips, arrived, got, *order)


def join_kernel(first_ref, second_ref, order_ref, out_ref):
    out_ref[:RUN] = first_ref[...]
    out_ref[RUN:] = second_ref[...]


def join(first, second, order):
    return pl.pallas_call(
        join_kernel,
        out_shape=jax.ShapeDtypeStruct((PAIR, first.shape[1]), BF16),
        in_specs=[VMEM, VMEM, ANY],
        out_specs=VMEM,
        compiler_params=limit(8),
        cost_estimate=cost(0, 8 * first.size),
        name="join",
    )(first, second, order)


def penalty(diff):
    return diff * lax.rsqrt(1.0 + diff * diff)


def regularizer_kernel(
    first_tile,
    count,
    place_ref,
    beta_ref,
    volume_ref,
    below_ref,
    above_ref,
    *refs,
):
    out_ref, token_ref, under_ref, buffer_ref, sem_ref = refs[-5:]
    step, steps = pl.program_id(0), pl.num_programs(0)

    @pl.when(step == 0)
    def _():
        start(tile_copies(volume_ref, buffer_ref, sem_ref, 0, first_tile, EDGE))

    block_ref = streamed(volume_ref, buffer_ref, sem_ref, step, steps, first_tile, EDGE)
    depth, strip, tile = block_ref.shape[0], block_ref.shape[2], XT
    at = pl.program_id(0) + first_tile
    beta = beta_ref[0]
    has_below = (place_ref[0] > 0).astype(F32)
    has_above = (place_ref[0] < place_ref[3] - 1).astype(F32)
    has_before = (at > 0).astype(F32)
    has_after = (at < count - 1).astype(F32)
    here = pl.ds(EDGE, tile)
    under_ref[...] = (
        penalty(block_ref[0, here].astype(F32) - below_ref[0].astype(F32)) * has_below
    )
    row = iota((tile, strip), 0)
    lane = iota((tile, strip), 1)

    def body(z, carry):
        center = block_ref[z, here].astype(F32)
        top = z == depth - 1
        upper = jnp.where(top, above_ref[0], block_ref[jnp.minimum(z + 1, depth - 1), here])
        over = penalty(upper.astype(F32) - center) * jnp.where(top, has_above, 1.0)
        total = under_ref[...] - over
        under_ref[...] = over
        ahead = block_ref[z, pl.ds(EDGE + tile, EDGE)].astype(F32)[0:1]
        behind = block_ref[z, pl.ds(0, EDGE)].astype(F32)[EDGE - 1 :]
        behind = penalty(center[0:1] - behind) * has_before
        along = penalty(jnp.where(row == tile - 1, ahead, pltpu.roll(center, tile - 1, 0)) - center)
        along = jnp.where(row == tile - 1, along * has_after, along)
        total = total + jnp.where(row == 0, behind, pltpu.roll(along, 1, 0)) - along
        across = penalty(pltpu.roll(center, strip - 1, 1) - center)
        across = jnp.where(lane == strip - 1, 0.0, across)
        total = total + pltpu.roll(across, 1, 1) - across
        out_ref[z] = (total * beta).astype(BF16)
        return carry

    lax.fori_loop(0, depth, body, 0, unroll=2)
    token_ref[...] = under_ref[:8]


def regularizer(index, done, place, beta, volume, below, above, *order):
    depth, extent, strip = volume.shape
    count = extent // XT
    length = count // PIECES
    origin = index * length
    plane = pl.BlockSpec((1, XT, strip), lambda i: (0, origin + i, 0))
    block = pl.BlockSpec((depth, XT, strip), lambda i: (0, origin + i, 0))
    specs = [SMEM, SMEM, HBM]
    specs += [plane] * 2 + [ANY] * len(order)
    before = [] if done is None else [done]
    return pl.pallas_call(
        functools.partial(regularizer_kernel, origin, count),
        grid=(length,),
        out_shape=(pltpu.HBM(volume.shape, BF16), jax.ShapeDtypeStruct((8, strip), F32)),
        in_specs=specs + [HBM] * len(before),
        out_specs=(block, pl.BlockSpec((8, strip), lambda i: (0, 0))),
        scratch_shapes=[pltpu.VMEM((XT, strip), F32)] + stream_scratch(depth, strip, EDGE),
        compiler_params=limit(8),
        input_output_aliases={len(specs): 0} if before else {},
        cost_estimate=cost(30 * volume.size // PIECES, 8 * volume.size // PIECES),
        name="regularizer",
    )(place, beta, volume, below, above, *order, *before)


def gradient_kernel(place_ref, beta_ref, spread_ref, mine_ref, beside_ref, *refs):
    chunk_refs = refs[:-6]
    whole_ref, out_ref, buffer_ref, sem_ref, result_ref, result_sem_ref = refs[-6:]
    depth, extent, strip = whole_ref.shape
    steps = extent // XT
    beta = beta_ref[0]
    has_left = (place_ref[1] > 0).astype(F32)
    has_right = (place_ref[1] < place_ref[2] - 1).astype(F32)
    start(tile_copies(whole_ref, buffer_ref, sem_ref, 0))

    def result(step):
        slot = lax.rem(step, 2)
        here = pl.ds(pl.multiple_of(step * XT, XT), XT)
        return pltpu.make_async_copy(
            result_ref.at[slot], out_ref.at[:, here], result_sem_ref.at[slot]
        )

    def body(step, carry):
        here = pl.ds(pl.multiple_of(step * XT, XT), XT)
        mine = mine_ref[NEAR - LINES :, here].astype(F32)
        beside = beside_ref[RUN : RUN + LINES, here].astype(F32)
        on_left = penalty(mine[:8] - beside[:8]) * (has_left * beta)
        on_right = penalty(mine[8:] - beside[8:]) * (has_right * beta)
        ends = jnp.concatenate([on_left, on_right], axis=0).astype(BF16)
        rows = jnp.concatenate([ref[:, here] for ref in chunk_refs] + [ends], axis=0)
        out = lax.dot_general(
            rows, spread_ref[...], (((0,), (0,)), ((), ())), preferred_element_type=F32
        )
        regular_ref = streamed(whole_ref, buffer_ref, sem_ref, step, steps)

        @pl.when(step >= 2)
        def _():
            result(step - 2).wait()

        slot = lax.rem(step, 2)
        for z in range(depth):
            regular = regular_ref[z].astype(F32)
            result_ref[slot, z] = (out[:, z * strip : (z + 1) * strip] + regular).astype(BF16)
        result(step).start()
        return carry

    lax.fori_loop(0, steps, body, 0)
    result(jnp.int32(steps - 2)).wait()
    result(jnp.int32(steps - 1)).wait()


def gradient(place, beta, spread, mine, arrived, chunks, regular):
    depth, extent, strip = regular.shape
    size = depth * extent * strip
    return pl.pallas_call(
        gradient_kernel,
        out_shape=jax.ShapeDtypeStruct(regular.shape, BF16),
        in_specs=[SMEM, SMEM] + [VMEM] * (3 + len(chunks)) + [HBM],
        out_specs=ANY,
        scratch_shapes=stream_scratch(depth, strip)
        + [pltpu.VMEM((2, depth, XT, strip), BF16), pltpu.SemaphoreType.DMA((2,))],
        compiler_params=limit(12),
        cost_estimate=cost(2 * spread.shape[0] * size, 5 * size),
        name="gradient",
    )(place, beta, spread, mine, arrived, *chunks, regular)


def shards(volume, measured, ray_weight, view_owner, band_offset, band_width, beta):
    slabs = lax.axis_size("slab")
    tiles = lax.axis_size("tile")
    slab, tile = lax.axis_index("slab"), lax.axis_index("tile")
    depth = volume.shape[0]
    place = jnp.stack([slab, tile, jnp.int32(tiles), jnp.int32(slabs)])

    def along_z(block, by):
        return lax.ppermute(block, "tile", [(i, (i + 2 * by) % tiles) for i in range(tiles)])

    def along_y(block):
        return lax.ppermute(block, "tile", [(i, i ^ 1) for i in range(tiles)])

    packed = pack(view_owner[:, :, 0], band_offset, band_width, ray_weight, measured, slabs)
    packed, after = lax.optimization_barrier((packed, volume))
    got = lax.all_to_all(packed, "slab", split_axis=0, concat_axis=0, tiled=True)
    top, bottom = after[depth - 1 :], after[:1]
    below = lax.ppermute(top, "slab", [(i, i + 1) for i in range(slabs - 1)])
    above = lax.ppermute(bottom, "slab", [(i + 1, i) for i in range(slabs - 1)])
    flat = got.reshape(slabs * SLOTS, ROWS, BAND)
    volume = pltpu.with_memory_space_constraint(volume, pltpu.HBM)

    own, up2, down2, near_up, near_down, far_up, far_down = forward(
        place, flat, volume, tiles, top, bottom
    )
    near_up, near_down, far_up, far_down, below, above = lax.optimization_barrier(
        (near_up, near_down, far_up, far_down, below, above)
    )
    near = along_z(near_up, 1), along_z(near_down, -1)
    far = along_z(far_up, 2), along_z(far_down, -2)
    regular, token = regularizer(0, None, place, beta, volume, below, above, far_up)
    up, down = round_sums(up2, near[0], far[0], down2, near[1], far[1], token)
    two = along_z(up, 2), along_z(down, -2)
    regular, token = regularizer(1, regular, place, beta, volume, below, above, up)
    kept, strips, sent = last_sums(place, own, near_up, *near, *two, token)
    arrived = along_y(sent)
    images = residual_images(place, kept, strips, arrived, flat)

    partner = along_y(images)
    regular, token = regularizer(2, regular, place, beta, volume, below, above, images)
    pair = join(images, partner, token)
    up2, down2 = along_z(pair, 2), along_z(pair, -2)
    up1, down1 = along_z(pair, 1), along_z(pair, -1)
    spread = spread_rows(place, flat, tiles, pair)
    regular, token = regularizer(3, regular, place, beta, volume, below, above, pair, spread)
    up3, down3 = along_z(up2, 1), along_z(down2, -1)
    far_up, far_down = along_z(up2[:RUN], 2), along_z(down2[RUN:], -2)
    chunks = [pair, down1, up1, down2, up2, down3, up3, far_up, far_down]
    regular = pltpu.with_memory_space_constraint(regular, pltpu.HBM)
    return gradient(place, beta, spread, near_up, arrived, chunks, regular)


def solution(mesh):
    in_specs = (
        P("slab", None, "tile"),
        P(None, "slab", None, "tile"),
        P(None, "slab", "tile"),
        P(None, "slab", None),
        P(None, "slab"),
        P(None, "slab"),
        P(),
    )
    out_specs = P("slab", None, "tile")
    return jax.shard_map(shards, mesh=mesh, in_specs=in_specs, out_specs=out_specs, check_vma=False)
```

```python
import functools

import jax
import jax.numpy as jnp
from jax import lax
from jax.experimental import pallas as pl
from jax.experimental.pallas import tpu as pltpu
from jax.sharding import PartitionSpec as P

BAND = 128
BATCHES = 2
CAPP = 2
SLOTS = BATCHES * CAPP
ROWS = 16
RUN = SLOTS * 8
PAIR = 2 * RUN
LINES = 16
EDGE = 16
PIECES = 4


def limit(mib):
    return pltpu.CompilerParams(vmem_limit_bytes=mib << 20)

XT = 256
F32 = jnp.float32
BF16 = jnp.bfloat16
VMEM = pl.BlockSpec(memory_space=pltpu.VMEM)
SMEM = pl.BlockSpec(memory_space=pltpu.SMEM)
ANY = pl.BlockSpec(memory_space=pl.ANY)
HBM = pl.BlockSpec(memory_space=pltpu.HBM)


def cost(flops, moved):
    return pl.CostEstimate(flops=flops, bytes_accessed=moved, transcendentals=0)


def iota(shape, dim):
    return lax.broadcasted_iota(jnp.int32, shape, dim)


def pack_kernel(owner_ref, offset_ref, width_ref, weight_ref, measured_ref, out_ref, count_ref):
    out_ref[...] = jnp.zeros_like(out_ref)
    slabs = out_ref.shape[0]
    views = owner_ref.shape[1]
    row = iota((ROWS, BAND), 0)
    lane = iota((ROWS, BAND), 1)
    empty = jnp.zeros((8, BAND), F32)
    for batch in range(BATCHES):
        for slab in range(slabs):
            count_ref[slab] = 0
        for view in range(views):
            owner = owner_ref[batch, view]
            rank = count_ref[owner]
            count_ref[owner] = rank + 1
            rows = jnp.concatenate([measured_ref[batch, view].astype(F32), empty], axis=0)
            band = jnp.where(
                lane == 0,
                offset_ref[batch, view].astype(F32),
                jnp.where(lane == 1, width_ref[batch, view].astype(F32), 0.0),
            )
            rows = jnp.where(row == 8, weight_ref[view].astype(F32)[batch : batch + 1], jnp.where(row == 9, band, rows))
            out_ref[owner, batch * CAPP + rank] = rows.astype(BF16)


def pack(owner, offset, width, weight, measured, slabs):
    return pl.pallas_call(
        pack_kernel,
        out_shape=jax.ShapeDtypeStruct((slabs, SLOTS, ROWS, BAND), BF16),
        in_specs=[SMEM, SMEM, SMEM, VMEM, VMEM],
        out_specs=VMEM,
        scratch_shapes=[pltpu.SMEM((slabs,), jnp.int32)],
        name="pack_messages",
    )(owner, offset, width, jnp.transpose(weight, (1, 0, 2)), measured)


def joined(block):
    return jnp.concatenate([block[z] for z in range(block.shape[0])], axis=1)


def tile_copies(ref, buffer_ref, sem_ref, index, first=0, edge=0):
    slot = lax.rem(index, 2)
    extent = ref.shape[1]
    start = (first + index) * XT
    parts = [(start, edge, XT)]
    if edge:
        parts.append((jnp.maximum(start - edge, 0), 0, edge))
        parts.append((jnp.minimum(start + XT, extent - edge), edge + XT, edge))
    return [
        pltpu.make_async_copy(
            ref.at[:, pl.ds(pl.multiple_of(source, 16), size)],
            buffer_ref.at[slot, :, pl.ds(target, size)],
            sem_ref.at[slot, part],
        )
        for part, (source, target, size) in enumerate(parts)
    ]


def start(copies):
    for copy in copies:
        copy.start()


def streamed(ref, buffer_ref, sem_ref, step, steps, first=0, edge=0):
    @pl.when(step + 1 < steps)
    def _():
        start(tile_copies(ref, buffer_ref, sem_ref, step + 1, first, edge))

    for copy in tile_copies(ref, buffer_ref, sem_ref, step, first, edge):
        copy.wait()
    return buffer_ref.at[lax.rem(step, 2)]


def stream_scratch(depth, strip, edge=0):
    return [
        pltpu.VMEM((2, depth, XT + 2 * edge, strip), BF16),
        pltpu.SemaphoreType.DMA((2, 3 if edge else 1)),
    ]


def spread_weights(tiles, out_ref, first, depth):
    rows = tiles.shape[0] * depth
    weights = jnp.broadcast_to(
        tiles.astype(F32)[:, 8:9, :], (tiles.shape[0], depth, BAND)
    ).reshape(rows, BAND)
    slice_of = lax.rem(iota((rows, BAND), 0), depth)
    for z in range(depth):
        out_ref[first : first + rows, z * BAND : (z + 1) * BAND] = jnp.where(
            slice_of == z, weights, 0.0
        ).astype(BF16)


def hops(tiles):
    half = tiles // 4
    return [0] + [sign * hop for hop in range(1, half) for sign in (1, -1)] + [half]


def fill_spread(tiles, me, got_ref, spread_ref):
    row = 0
    for hop in hops(tiles):
        tile = lax.rem(me + 2 * hop + tiles, tiles)
        for source in (tile, tile ^ 1):
            spread_weights(got_ref[pl.ds(source * SLOTS, SLOTS)], spread_ref, row, 8)
            row += RUN
    shape = (LINES, spread_ref.shape[1])
    line = iota(shape, 0)
    target = jnp.where(line < 8, line * BAND, (line - 8) * BAND + BAND - 1)
    spread_ref[row:] = jnp.where(iota(shape, 1) == target, 1.0, 0.0).astype(BF16)


def spread_kernel(tiles, place_ref, got_ref, order_ref, out_ref):
    fill_spread(tiles, place_ref[1], got_ref, out_ref)


def spread_rows(place, got, tiles, order):
    shape = (got.shape[0] * 8 + LINES, 8 * BAND)
    return pl.pallas_call(
        functools.partial(spread_kernel, tiles),
        out_shape=jax.ShapeDtypeStruct(shape, BF16),
        in_specs=[SMEM, VMEM, ANY],
        out_specs=VMEM,
        compiler_params=limit(8),
        cost_estimate=cost(4 * shape[0] * shape[1], 4 * shape[0] * shape[1]),
        name="spread_rows",
    )(place, got, order)


def measured_rows(got_ref, source):
    rows = got_ref[pl.ds(source * SLOTS, SLOTS)].astype(F32)[:, :8]
    return rows.reshape(RUN, BAND).astype(BF16)


def forward_kernel(tiles, place_ref, got_ref, volume_ref, *refs):
    outs, (ends_ref, spread_ref, buffer_ref, sem_ref, last_ref, first_ref) = refs[:-6], refs[-6:]
    extent = volume_ref.shape[1]
    me = place_ref[1]
    start(tile_copies(volume_ref, buffer_ref, sem_ref, 0))
    fill_spread(tiles, me, got_ref, spread_ref)
    where = [(ref, row) for ref in outs for row in range(0, ref.shape[0], RUN)]
    beyond = pl.ds(extent, BAND)
    for index, hop in enumerate(hops(tiles)):
        tile = lax.rem(me + 2 * hop + tiles, tiles)
        for turn, source in enumerate((tile, tile ^ 1)):
            ref, row = where[2 * index + turn]
            ref[row : row + RUN, beyond] = measured_rows(got_ref, source)
    steps = extent // XT

    def body(step, carry):
        block_ref = streamed(volume_ref, buffer_ref, sem_ref, step, steps)
        out = lax.dot_general(
            spread_ref[...],
            joined(block_ref),
            (((1,), (1,)), ((), ())),
            preferred_element_type=F32,
        ).astype(BF16)
        here = pl.ds(pl.multiple_of(step * XT, XT), XT)
        for index, (ref, row) in enumerate(where):
            ref[row : row + RUN, here] = out[index * RUN : (index + 1) * RUN]
        ends_ref[:, here] = out[-LINES:]
        ends = out[-LINES:].astype(F32)
        there = pl.ds(pl.multiple_of(step * 8, 8), 8)
        first_ref[there] = ends[:8]
        last_ref[there] = ends[8:]
        return carry

    lax.fori_loop(0, steps, body, 0)
    outs[1][:, extent + BAND :] = last_ref[...].astype(BF16)
    outs[2][:, extent + BAND :] = first_ref[...].astype(BF16)


def forward(place, got, volume, tiles, *order):
    depth, extent, strip = volume.shape
    slots = got.shape[0]
    rows = [PAIR] * (tiles // 2 - 1) + [RUN] * 2
    lanes = [extent + BAND + (XT if index in (1, 2) else 0) for index in range(len(rows))]

    def kernel(place_ref, got_ref, volume_ref, *refs):
        forward_kernel(tiles, place_ref, got_ref, volume_ref, *refs[len(order) :])

    return pl.pallas_call(
        kernel,
        out_shape=[jax.ShapeDtypeStruct(shape, BF16) for shape in zip(rows, lanes)]
        + [jax.ShapeDtypeStruct((LINES, extent), BF16)],
        in_specs=[SMEM, VMEM, HBM] + [ANY] * len(order),
        out_specs=[VMEM] * (len(rows) + 1),
        scratch_shapes=[pltpu.VMEM((slots * depth + LINES, depth * strip), BF16)]
        + stream_scratch(depth, strip)
        + [pltpu.VMEM((extent // XT * 8, XT), F32)] * 2,
        compiler_params=limit(10),
        cost_estimate=cost(2 * slots * depth * volume.size, 3 * volume.size),
        name="forward",
    )(place, got, volume, *order)


def sums_kernel(extent, from_below_ref, up_ref, from_above_ref, down_ref, *refs):
    for came_ref, own_ref, low, out_ref in (
        (from_below_ref, up_ref, 0, refs[-2]),
        (from_above_ref, down_ref, RUN, refs[-1]),
    ):
        came_lanes = came_ref.shape[1] - extent
        past = extent + BAND
        for row in (0, RUN):
            rows = slice(row, row + RUN)
            total = own_ref[rows, :extent].astype(F32)
            strips = jnp.zeros((RUN, came_lanes), BF16)
            if came_ref.shape[0] > RUN or row == low:
                came = rows if came_ref.shape[0] > RUN else slice(0, RUN)
                total = total + came_ref[came, :extent].astype(F32)
                strips = came_ref[came, extent:]
            out_ref[rows, :extent] = total.astype(BF16)
            out_ref[rows, extent:past] = own_ref[rows, extent:past]
            out_ref[rows, past : past + came_lanes] = strips
        if own_ref.shape[1] > past:
            out_ref[:, past + came_lanes :] = own_ref[:, past:]


def ring_sums(from_below, up, from_above, down, extent, *order):
    out = jax.ShapeDtypeStruct((PAIR, up.shape[1] + from_below.shape[1] - extent), BF16)
    return pl.pallas_call(
        functools.partial(sums_kernel, extent),
        out_shape=(out, out),
        in_specs=[VMEM] * 4 + [ANY] * len(order),
        out_specs=(VMEM, VMEM),
        compiler_params=limit(8),
        cost_estimate=cost(6 * out.size, 12 * out.size),
        name="ring_sums",
    )(from_below, up, from_above, down, *order)


STRIPS = (0, -1, 1, -2, 2, -3, 3, 4)


def last_sums_kernel(place_ref, own_ref, ends_ref, below_ref, above_ref, *refs):
    kept_ref, strips_ref, sent_ref = refs[-3:]
    extent = ends_ref.shape[1]
    blocks = [slice(extent + n * BAND, extent + (n + 1) * BAND) for n in range(4)]
    for row in (0, RUN):
        rows = slice(row, row + RUN)
        total = (
            own_ref[rows, :extent].astype(F32)
            + below_ref[rows, :extent].astype(F32)
            + above_ref[rows, :extent].astype(F32)
        )
        strips = [own_ref[rows, blocks[0]]]
        for n in range(3):
            strips += [below_ref[rows, blocks[n]], above_ref[rows, blocks[n]]]
        strips.append((below_ref if row == 0 else above_ref)[rows, blocks[3]])
        if row == 0:
            kept_ref[...] = total
            for index, strip in enumerate(strips):
                strips_ref[:, index * BAND : (index + 1) * BAND] = strip
        else:
            sent_ref[:RUN] = total.astype(BF16)
            halves = [strip[low : low + 16] for strip in strips for low in (0, 16)]
            sent_ref[RUN + LINES :] = jnp.concatenate(halves, axis=1)

    def column(ref):
        tiled = ref[:, blocks[3].stop :].astype(F32)
        return jnp.concatenate([tiled[n * 8 : (n + 1) * 8] for n in range(extent // XT)], axis=1)

    mine = ends_ref[...].astype(F32)
    even = place_ref[1] % 2 == 0
    left = jnp.where(even, mine[8:], column(below_ref))
    right = jnp.where(even, column(above_ref), mine[:8])
    sent_ref[RUN : RUN + LINES] = jnp.concatenate([left, right], axis=0).astype(BF16)


def last_sums(place, own, ends, below, above, *order):
    extent = ends.shape[1]
    return pl.pallas_call(
        last_sums_kernel,
        out_shape=(
            jax.ShapeDtypeStruct((RUN, extent), F32),
            jax.ShapeDtypeStruct((RUN, len(STRIPS) * BAND), BF16),
            jax.ShapeDtypeStruct((RUN + LINES + 16, extent), BF16),
        ),
        in_specs=[SMEM] + [VMEM] * 4 + [ANY] * len(order),
        out_specs=(VMEM,) * 3,
        compiler_params=limit(8),
        cost_estimate=cost(5 * own.size, 14 * own.size),
        name="last_sums",
    )(place, own, ends, below, above, *order)


def residual_kernel(place_ref, kept_ref, strips_ref, arrived_ref, got_ref, *refs):
    out_ref, measured_ref = refs[-2:]
    extent = kept_ref.shape[1]
    blocks = extent // BAND
    me = place_ref[1]
    for index, hop in enumerate(STRIPS):
        tile = lax.rem(me + 2 * hop + blocks, blocks)
        measured_ref[tile] = strips_ref[:, index * BAND : (index + 1) * BAND].astype(F32)
        for half in (0, 1):
            lanes = slice((2 * index + half) * BAND, (2 * index + half + 1) * BAND)
            measured_ref[tile ^ 1, half * 16 : (half + 1) * 16] = arrived_ref[
                RUN + LINES :, lanes
            ].astype(F32)
    empty = jnp.zeros((8, BAND), F32)
    arrived = arrived_ref[:RUN].astype(F32)
    for slot in range(SLOTS):
        low = slot * 8
        total = kept_ref[low : low + 8] + arrived[low : low + 8]
        band = got_ref[me * SLOTS + slot].astype(F32)
        offset = band[9:10, 0:1].astype(jnp.int32)
        width = jnp.maximum(band[9:10, 1:2], 1.0)
        recip = 1.0 / width
        width = width.astype(jnp.int32)

        def inside(delta):
            delta = delta - offset
            return jnp.where((delta >= 0) & (delta < width), recip, 0.0).astype(BF16)

        shape = (2 * BAND, BAND)
        onward = inside(iota(shape, 1) + BAND - iota(shape, 0))
        back = inside(iota(shape, 0) - iota(shape, 1))
        parts = [total[:, n * BAND : (n + 1) * BAND] for n in range(blocks)]
        here = jnp.concatenate(parts, axis=0)
        before = jnp.concatenate([empty] + parts[:-1], axis=0)
        paired = jnp.concatenate([before, here], axis=1)
        high = paired.astype(BF16)
        rest = (paired - high.astype(F32)).astype(BF16)
        sums = jnp.dot(high, onward, preferred_element_type=F32) + jnp.dot(
            rest, onward, preferred_element_type=F32
        )
        rows = measured_ref[:, low : low + 8].reshape(blocks * 8, BAND)
        residual = (sums - rows).astype(BF16).astype(F32)
        later = jnp.concatenate([residual[8:], empty], axis=0)
        both = jnp.concatenate([residual, later], axis=1).astype(BF16)
        image = jnp.dot(both, back, preferred_element_type=F32)
        image = jnp.concatenate([image[n * 8 : (n + 1) * 8] for n in range(blocks)], axis=1)
        if slot % 2 == 0:
            even = image
        else:
            out_ref[low - 8 : low + 8] = jnp.concatenate([even, image], axis=0).astype(BF16)


def residual_images(place, kept, strips, arrived, got, *order):
    return pl.pallas_call(
        residual_kernel,
        out_shape=jax.ShapeDtypeStruct(kept.shape, BF16),
        in_specs=[SMEM] + [VMEM] * 4 + [ANY] * len(order),
        out_specs=VMEM,
        scratch_shapes=[pltpu.VMEM((kept.shape[1] // BAND, RUN, BAND), F32)],
        compiler_params=limit(8),
        cost_estimate=cost(4 * 8 * 16 * 256 * 128 * 6, 12 * kept.size),
        name="residual_images",
    )(place, kept, strips, arrived, got, *order)


def penalty(diff):
    return diff * lax.rsqrt(1.0 + diff * diff)


def regularizer_kernel(
    first_tile,
    count,
    place_ref,
    beta_ref,
    volume_ref,
    below_ref,
    above_ref,
    *refs,
):
    out_ref, token_ref, under_ref, buffer_ref, sem_ref = refs[-5:]
    step, steps = pl.program_id(0), pl.num_programs(0)

    @pl.when(step == 0)
    def _():
        start(tile_copies(volume_ref, buffer_ref, sem_ref, 0, first_tile, EDGE))

    block_ref = streamed(volume_ref, buffer_ref, sem_ref, step, steps, first_tile, EDGE)
    depth, strip, tile = block_ref.shape[0], block_ref.shape[2], XT
    at = pl.program_id(0) + first_tile
    beta = beta_ref[0]
    has_below = (place_ref[0] > 0).astype(F32)
    has_above = (place_ref[0] < place_ref[3] - 1).astype(F32)
    has_before = (at > 0).astype(F32)
    has_after = (at < count - 1).astype(F32)
    here = pl.ds(EDGE, tile)
    under_ref[...] = (
        penalty(block_ref[0, here].astype(F32) - below_ref[0].astype(F32)) * has_below
    )
    row = iota((tile, strip), 0)
    lane = iota((tile, strip), 1)

    def body(z, carry):
        center = block_ref[z, here].astype(F32)
        top = z == depth - 1
        upper = jnp.where(top, above_ref[0], block_ref[jnp.minimum(z + 1, depth - 1), here])
        over = penalty(upper.astype(F32) - center) * jnp.where(top, has_above, 1.0)
        total = under_ref[...] - over
        under_ref[...] = over
        ahead = block_ref[z, pl.ds(EDGE + tile, EDGE)].astype(F32)[0:1]
        behind = block_ref[z, pl.ds(0, EDGE)].astype(F32)[EDGE - 1 :]
        behind = penalty(center[0:1] - behind) * has_before
        along = penalty(jnp.where(row == tile - 1, ahead, pltpu.roll(center, tile - 1, 0)) - center)
        along = jnp.where(row == tile - 1, along * has_after, along)
        total = total + jnp.where(row == 0, behind, pltpu.roll(along, 1, 0)) - along
        across = penalty(pltpu.roll(center, strip - 1, 1) - center)
        across = jnp.where(lane == strip - 1, 0.0, across)
        total = total + pltpu.roll(across, 1, 1) - across
        out_ref[z] = (total * beta).astype(BF16)
        return carry

    lax.fori_loop(0, depth, body, 0, unroll=2)
    token_ref[...] = under_ref[:8]


def regularizer(index, done, place, beta, volume, below, above, *order):
    depth, extent, strip = volume.shape
    count = extent // XT
    length = count // PIECES
    origin = index * length
    plane = pl.BlockSpec((1, XT, strip), lambda i: (0, origin + i, 0))
    block = pl.BlockSpec((depth, XT, strip), lambda i: (0, origin + i, 0))
    specs = [SMEM, SMEM, HBM]
    specs += [plane] * 2 + [ANY] * len(order)
    before = [] if done is None else [done]
    return pl.pallas_call(
        functools.partial(regularizer_kernel, origin, count),
        grid=(length,),
        out_shape=(pltpu.HBM(volume.shape, BF16), jax.ShapeDtypeStruct((8, strip), F32)),
        in_specs=specs + [HBM] * len(before),
        out_specs=(block, pl.BlockSpec((8, strip), lambda i: (0, 0))),
        scratch_shapes=[pltpu.VMEM((XT, strip), F32)] + stream_scratch(depth, strip, EDGE),
        compiler_params=limit(8),
        input_output_aliases={len(specs): 0} if before else {},
        cost_estimate=cost(30 * volume.size // PIECES, 8 * volume.size // PIECES),
        name="regularizer",
    )(place, beta, volume, below, above, *order, *before)


def gradient_kernel(place_ref, beta_ref, spread_ref, mine_ref, beside_ref, *refs):
    chunk_refs = refs[:-6]
    whole_ref, out_ref, buffer_ref, sem_ref, result_ref, result_sem_ref = refs[-6:]
    depth, extent, strip = whole_ref.shape
    steps = extent // XT
    beta = beta_ref[0]
    has_left = (place_ref[1] > 0).astype(F32)
    has_right = (place_ref[1] < place_ref[2] - 1).astype(F32)
    start(tile_copies(whole_ref, buffer_ref, sem_ref, 0))

    def result(step):
        slot = lax.rem(step, 2)
        here = pl.ds(pl.multiple_of(step * XT, XT), XT)
        return pltpu.make_async_copy(
            result_ref.at[slot], out_ref.at[:, here], result_sem_ref.at[slot]
        )

    def body(step, carry):
        here = pl.ds(pl.multiple_of(step * XT, XT), XT)
        mine = mine_ref[:, here].astype(F32)
        beside = beside_ref[RUN : RUN + LINES, here].astype(F32)
        on_left = penalty(mine[:8] - beside[:8]) * (has_left * beta)
        on_right = penalty(mine[8:] - beside[8:]) * (has_right * beta)
        ends = jnp.concatenate([on_left, on_right], axis=0).astype(BF16)
        rows = jnp.concatenate([ref[:, here] for ref in chunk_refs] + [ends], axis=0)
        out = lax.dot_general(
            rows, spread_ref[...], (((0,), (0,)), ((), ())), preferred_element_type=F32
        )
        regular_ref = streamed(whole_ref, buffer_ref, sem_ref, step, steps)

        @pl.when(step >= 2)
        def _():
            result(step - 2).wait()

        slot = lax.rem(step, 2)
        for z in range(depth):
            regular = regular_ref[z].astype(F32)
            result_ref[slot, z] = (out[:, z * strip : (z + 1) * strip] + regular).astype(BF16)
        result(step).start()
        return carry

    lax.fori_loop(0, steps, body, 0)
    result(jnp.int32(steps - 2)).wait()
    result(jnp.int32(steps - 1)).wait()


def gradient(place, beta, spread, mine, arrived, chunks, regular):
    depth, extent, strip = regular.shape
    size = depth * extent * strip
    return pl.pallas_call(
        gradient_kernel,
        out_shape=jax.ShapeDtypeStruct(regular.shape, BF16),
        in_specs=[SMEM, SMEM] + [VMEM] * (3 + len(chunks)) + [HBM],
        out_specs=ANY,
        scratch_shapes=stream_scratch(depth, strip)
        + [pltpu.VMEM((2, depth, XT, strip), BF16), pltpu.SemaphoreType.DMA((2,))],
        compiler_params=limit(12),
        cost_estimate=cost(2 * spread.shape[0] * size, 5 * size),
        name="gradient",
    )(place, beta, spread, mine, arrived, *chunks, regular)


def shards(volume, measured, ray_weight, view_owner, band_offset, band_width, beta):
    slabs = lax.axis_size("slab")
    tiles = lax.axis_size("tile")
    slab, tile = lax.axis_index("slab"), lax.axis_index("tile")
    depth = volume.shape[0]
    place = jnp.stack([slab, tile, jnp.int32(tiles), jnp.int32(slabs)])

    def along_z(block, by):
        return lax.ppermute(block, "tile", [(i, (i + 2 * by) % tiles) for i in range(tiles)])

    def along_y(block):
        return lax.ppermute(block, "tile", [(i, i ^ 1) for i in range(tiles)])

    packed = pack(view_owner[:, :, 0], band_offset, band_width, ray_weight, measured, slabs)
    packed, after = lax.optimization_barrier((packed, volume))
    got = lax.all_to_all(packed, "slab", split_axis=0, concat_axis=0, tiled=True)
    top, bottom = after[depth - 1 :], after[:1]
    below = lax.ppermute(top, "slab", [(i, i + 1) for i in range(slabs - 1)])
    above = lax.ppermute(bottom, "slab", [(i + 1, i) for i in range(slabs - 1)])
    flat = got.reshape(slabs * SLOTS, ROWS, BAND)
    volume = pltpu.with_memory_space_constraint(volume, pltpu.HBM)

    own, up1, down1, up2, down2, up3, down3, up, down, ends = forward(
        place, flat, volume, tiles, top, bottom
    )
    extent = ends.shape[1]
    spread = spread_rows(place, flat, tiles, ends)
    order, regular = [spread], None
    for index, (own_up, own_down) in enumerate([(up3, down3), (up2, down2), (up1, down1)]):
        came = along_z(up, 1), along_z(down, -1)
        up, down = ring_sums(came[0], own_up, came[1], own_down, extent, *order)
        regular, token = regularizer(index, regular, place, beta, volume, below, above, up)
        order = [token]
    came = along_z(up, 1), along_z(down, -1)
    kept, strips, sent = last_sums(place, own, ends, *came, *order)
    arrived = along_y(sent)
    regular, token = regularizer(3, regular, place, beta, volume, below, above, sent)
    images = residual_images(place, kept, strips, arrived, flat, token)

    partner = along_y(images)
    rings = []
    for first, past in ((images, 1), (partner, -1)):
        up, down = first, first
        ring = {0: first}
        for hop in range(1, tiles // 4):
            up, down = along_z(up, 1), along_z(down, -1)
            ring[-hop], ring[hop] = up, down
        ring[tiles // 4] = along_z(up, 1) if past == 1 else along_z(down, -1)
        rings.append(ring)
    chunks = [ring[hop] for hop in hops(tiles) for ring in rings]
    regular = pltpu.with_memory_space_constraint(regular, pltpu.HBM)
    return gradient(place, beta, spread, ends, arrived, chunks, regular)


def solution(mesh):
    in_specs = (
        P("slab", None, "tile"),
        P(None, "slab", None, "tile"),
        P(None, "slab", "tile"),
        P(None, "slab", None),
        P(None, "slab"),
        P(None, "slab"),
        P(),
    )
    out_specs = P("slab", None, "tile")
    return jax.shard_map(shards, mesh=mesh, in_specs=in_specs, out_specs=out_specs, check_vma=False)
```

```python
import functools

import jax
import jax.numpy as jnp
from jax import lax
from jax.experimental import pallas as pl
from jax.experimental.pallas import tpu as pltpu
from jax.sharding import PartitionSpec as P

BAND = 128
BATCHES = 2
CAPP = 2
SLOTS = BATCHES * CAPP
ROWS = 16
RUN = SLOTS * 8
PAIR = 2 * RUN
LINES = 16
EDGE = 16
PIECES = 4


def limit(mib):
    return pltpu.CompilerParams(vmem_limit_bytes=mib << 20)

XT = 256
WIDE = 512
F32 = jnp.float32
BF16 = jnp.bfloat16
VMEM = pl.BlockSpec(memory_space=pltpu.VMEM)
SMEM = pl.BlockSpec(memory_space=pltpu.SMEM)
ANY = pl.BlockSpec(memory_space=pl.ANY)
HBM = pl.BlockSpec(memory_space=pltpu.HBM)


def cost(flops, moved):
    return pl.CostEstimate(flops=flops, bytes_accessed=moved, transcendentals=0)


def iota(shape, dim):
    return lax.broadcasted_iota(jnp.int32, shape, dim)


def pack_kernel(owner_ref, offset_ref, width_ref, weight_ref, measured_ref, out_ref, count_ref):
    out_ref[...] = jnp.zeros_like(out_ref)
    slabs = out_ref.shape[0]
    views = owner_ref.shape[1]
    row = iota((ROWS, BAND), 0)
    lane = iota((ROWS, BAND), 1)
    empty = jnp.zeros((8, BAND), F32)
    for batch in range(BATCHES):
        for slab in range(slabs):
            count_ref[slab] = 0
        for view in range(views):
            owner = owner_ref[batch, view]
            rank = count_ref[owner]
            count_ref[owner] = rank + 1
            rows = jnp.concatenate([measured_ref[batch, view].astype(F32), empty], axis=0)
            band = jnp.where(
                lane == 0,
                offset_ref[batch, view].astype(F32),
                jnp.where(lane == 1, width_ref[batch, view].astype(F32), 0.0),
            )
            rows = jnp.where(row == 8, weight_ref[view].astype(F32)[batch : batch + 1], jnp.where(row == 9, band, rows))
            out_ref[owner, batch * CAPP + rank] = rows.astype(BF16)


def pack(owner, offset, width, weight, measured, slabs):
    return pl.pallas_call(
        pack_kernel,
        out_shape=jax.ShapeDtypeStruct((slabs, SLOTS, ROWS, BAND), BF16),
        in_specs=[SMEM, SMEM, SMEM, VMEM, VMEM],
        out_specs=VMEM,
        scratch_shapes=[pltpu.SMEM((slabs,), jnp.int32)],
        name="pack_messages",
    )(owner, offset, width, jnp.transpose(weight, (1, 0, 2)), measured)


def joined(block):
    return jnp.concatenate([block[z] for z in range(block.shape[0])], axis=1)


def tile_copies(ref, buffer_ref, sem_ref, index, first=0, edge=0, tile=XT):
    slot = lax.rem(index, 2)
    extent = ref.shape[1]
    start = (first + index) * tile
    parts = [(start, edge, tile)]
    if edge:
        parts.append((jnp.maximum(start - edge, 0), 0, edge))
        parts.append((jnp.minimum(start + tile, extent - edge), edge + tile, edge))
    return [
        pltpu.make_async_copy(
            ref.at[:, pl.ds(pl.multiple_of(source, 16), size)],
            buffer_ref.at[slot, :, pl.ds(target, size)],
            sem_ref.at[slot, part],
        )
        for part, (source, target, size) in enumerate(parts)
    ]


def start(copies):
    for copy in copies:
        copy.start()


def streamed(ref, buffer_ref, sem_ref, step, steps, first=0, edge=0, tile=XT):
    @pl.when(step + 1 < steps)
    def _():
        start(tile_copies(ref, buffer_ref, sem_ref, step + 1, first, edge, tile))

    for copy in tile_copies(ref, buffer_ref, sem_ref, step, first, edge, tile):
        copy.wait()
    return buffer_ref.at[lax.rem(step, 2)]


def stream_scratch(depth, strip, edge=0, tile=XT):
    return [
        pltpu.VMEM((2, depth, tile + 2 * edge, strip), BF16),
        pltpu.SemaphoreType.DMA((2, 3 if edge else 1)),
    ]


def spread_weights(tiles, out_ref, first, depth):
    rows = tiles.shape[0] * depth
    weights = jnp.broadcast_to(
        tiles.astype(F32)[:, 8:9, :], (tiles.shape[0], depth, BAND)
    ).reshape(rows, BAND)
    slice_of = lax.rem(iota((rows, BAND), 0), depth)
    for z in range(depth):
        out_ref[first : first + rows, z * BAND : (z + 1) * BAND] = jnp.where(
            slice_of == z, weights, 0.0
        ).astype(BF16)


def hops(tiles):
    half = tiles // 4
    return [0] + [sign * hop for hop in range(1, half) for sign in (1, -1)] + [half]


def fill_spread(tiles, me, got_ref, spread_ref):
    row = 0
    for hop in hops(tiles):
        tile = lax.rem(me + 2 * hop + tiles, tiles)
        for source in (tile, tile ^ 1):
            spread_weights(got_ref[pl.ds(source * SLOTS, SLOTS)], spread_ref, row, 8)
            row += RUN
    shape = (LINES, spread_ref.shape[1])
    line = iota(shape, 0)
    target = jnp.where(line < 8, line * BAND, (line - 8) * BAND + BAND - 1)
    spread_ref[row:] = jnp.where(iota(shape, 1) == target, 1.0, 0.0).astype(BF16)


def spread_kernel(tiles, place_ref, got_ref, order_ref, out_ref):
    fill_spread(tiles, place_ref[1], got_ref, out_ref)


def spread_rows(place, got, tiles, order):
    shape = (got.shape[0] * 8 + LINES, 8 * BAND)
    return pl.pallas_call(
        functools.partial(spread_kernel, tiles),
        out_shape=jax.ShapeDtypeStruct(shape, BF16),
        in_specs=[SMEM, VMEM, ANY],
        out_specs=VMEM,
        compiler_params=limit(8),
        cost_estimate=cost(4 * shape[0] * shape[1], 4 * shape[0] * shape[1]),
        name="spread_rows",
    )(place, got, order)


def measured_rows(got_ref, source):
    rows = got_ref[pl.ds(source * SLOTS, SLOTS)].astype(F32)[:, :8]
    return rows.reshape(RUN, BAND).astype(BF16)


def forward_kernel(tiles, place_ref, got_ref, volume_ref, *refs):
    outs, (ends_ref, spread_ref, buffer_ref, sem_ref, last_ref, first_ref) = refs[:-6], refs[-6:]
    extent = volume_ref.shape[1]
    me = place_ref[1]
    start(tile_copies(volume_ref, buffer_ref, sem_ref, 0))
    fill_spread(tiles, me, got_ref, spread_ref)
    where = [(ref, row) for ref in outs for row in range(0, ref.shape[0], RUN)]
    beyond = pl.ds(extent, BAND)
    for index, hop in enumerate(hops(tiles)):
        tile = lax.rem(me + 2 * hop + tiles, tiles)
        for turn, source in enumerate((tile, tile ^ 1)):
            ref, row = where[2 * index + turn]
            ref[row : row + RUN, beyond] = measured_rows(got_ref, source)
    steps = extent // XT

    def body(step, carry):
        block_ref = streamed(volume_ref, buffer_ref, sem_ref, step, steps)
        out = lax.dot_general(
            spread_ref[...],
            joined(block_ref),
            (((1,), (1,)), ((), ())),
            preferred_element_type=F32,
        ).astype(BF16)
        here = pl.ds(pl.multiple_of(step * XT, XT), XT)
        for index, (ref, row) in enumerate(where):
            ref[row : row + RUN, here] = out[index * RUN : (index + 1) * RUN]
        ends_ref[:, here] = out[-LINES:]
        ends = out[-LINES:].astype(F32)
        there = pl.ds(pl.multiple_of(step * 8, 8), 8)
        first_ref[there] = ends[:8]
        last_ref[there] = ends[8:]
        return carry

    lax.fori_loop(0, steps, body, 0)
    outs[1][:, extent + BAND :] = last_ref[...].astype(BF16)
    outs[2][:, extent + BAND :] = first_ref[...].astype(BF16)


def forward(place, got, volume, tiles, *order):
    depth, extent, strip = volume.shape
    slots = got.shape[0]
    rows = [PAIR] * (tiles // 2 - 1) + [RUN] * 2
    lanes = [extent + BAND + (XT if index in (1, 2) else 0) for index in range(len(rows))]

    def kernel(place_ref, got_ref, volume_ref, *refs):
        forward_kernel(tiles, place_ref, got_ref, volume_ref, *refs[len(order) :])

    return pl.pallas_call(
        kernel,
        out_shape=[jax.ShapeDtypeStruct(shape, BF16) for shape in zip(rows, lanes)]
        + [jax.ShapeDtypeStruct((LINES, extent), BF16)],
        in_specs=[SMEM, VMEM, HBM] + [ANY] * len(order),
        out_specs=[VMEM] * (len(rows) + 1),
        scratch_shapes=[pltpu.VMEM((slots * depth + LINES, depth * strip), BF16)]
        + stream_scratch(depth, strip)
        + [pltpu.VMEM((extent // XT * 8, XT), F32)] * 2,
        compiler_params=limit(10),
        cost_estimate=cost(2 * slots * depth * volume.size, 3 * volume.size),
        name="forward",
    )(place, got, volume, *order)


def sums_kernel(extent, from_below_ref, up_ref, from_above_ref, down_ref, *refs):
    for came_ref, own_ref, low, out_ref in (
        (from_below_ref, up_ref, 0, refs[-2]),
        (from_above_ref, down_ref, RUN, refs[-1]),
    ):
        came_lanes = came_ref.shape[1] - extent
        past = extent + BAND
        for row in (0, RUN):
            rows = slice(row, row + RUN)
            total = own_ref[rows, :extent].astype(F32)
            strips = jnp.zeros((RUN, came_lanes), BF16)
            if came_ref.shape[0] > RUN or row == low:
                came = rows if came_ref.shape[0] > RUN else slice(0, RUN)
                total = total + came_ref[came, :extent].astype(F32)
                strips = came_ref[came, extent:]
            out_ref[rows, :extent] = total.astype(BF16)
            out_ref[rows, extent:past] = own_ref[rows, extent:past]
            out_ref[rows, past : past + came_lanes] = strips
        if own_ref.shape[1] > past:
            out_ref[:, past + came_lanes :] = own_ref[:, past:]


def ring_sums(from_below, up, from_above, down, extent, *order):
    out = jax.ShapeDtypeStruct((PAIR, up.shape[1] + from_below.shape[1] - extent), BF16)
    return pl.pallas_call(
        functools.partial(sums_kernel, extent),
        out_shape=(out, out),
        in_specs=[VMEM] * 4 + [ANY] * len(order),
        out_specs=(VMEM, VMEM),
        compiler_params=limit(8),
        cost_estimate=cost(6 * out.size, 12 * out.size),
        name="ring_sums",
    )(from_below, up, from_above, down, *order)


STRIPS = (0, -1, 1, -2, 2, -3, 3, 4)


def last_sums_kernel(place_ref, own_ref, ends_ref, below_ref, above_ref, *refs):
    kept_ref, strips_ref, sent_ref = refs[-3:]
    extent = ends_ref.shape[1]
    blocks = [slice(extent + n * BAND, extent + (n + 1) * BAND) for n in range(4)]
    for row in (0, RUN):
        rows = slice(row, row + RUN)
        total = (
            own_ref[rows, :extent].astype(F32)
            + below_ref[rows, :extent].astype(F32)
            + above_ref[rows, :extent].astype(F32)
        )
        strips = [own_ref[rows, blocks[0]]]
        for n in range(3):
            strips += [below_ref[rows, blocks[n]], above_ref[rows, blocks[n]]]
        strips.append((below_ref if row == 0 else above_ref)[rows, blocks[3]])
        if row == 0:
            kept_ref[...] = total
            for index, strip in enumerate(strips):
                strips_ref[:, index * BAND : (index + 1) * BAND] = strip
        else:
            sent_ref[:RUN] = total.astype(BF16)
            halves = [strip[low : low + 16] for strip in strips for low in (0, 16)]
            sent_ref[RUN + LINES :] = jnp.concatenate(halves, axis=1)

    def column(ref):
        tiled = ref[:, blocks[3].stop :].astype(F32)
        return jnp.concatenate([tiled[n * 8 : (n + 1) * 8] for n in range(extent // XT)], axis=1)

    mine = ends_ref[...].astype(F32)
    even = place_ref[1] % 2 == 0
    left = jnp.where(even, mine[8:], column(below_ref))
    right = jnp.where(even, column(above_ref), mine[:8])
    sent_ref[RUN : RUN + LINES] = jnp.concatenate([left, right], axis=0).astype(BF16)


def last_sums(place, own, ends, below, above, *order):
    extent = ends.shape[1]
    return pl.pallas_call(
        last_sums_kernel,
        out_shape=(
            jax.ShapeDtypeStruct((RUN, extent), F32),
            jax.ShapeDtypeStruct((RUN, len(STRIPS) * BAND), BF16),
            jax.ShapeDtypeStruct((RUN + LINES + 16, extent), BF16),
        ),
        in_specs=[SMEM] + [VMEM] * 4 + [ANY] * len(order),
        out_specs=(VMEM,) * 3,
        compiler_params=limit(8),
        cost_estimate=cost(5 * own.size, 14 * own.size),
        name="last_sums",
    )(place, own, ends, below, above, *order)


def residual_kernel(place_ref, kept_ref, strips_ref, arrived_ref, got_ref, *refs):
    out_ref, measured_ref = refs[-2:]
    extent = kept_ref.shape[1]
    blocks = extent // BAND
    me = place_ref[1]
    for index, hop in enumerate(STRIPS):
        tile = lax.rem(me + 2 * hop + blocks, blocks)
        measured_ref[tile] = strips_ref[:, index * BAND : (index + 1) * BAND].astype(F32)
        for half in (0, 1):
            lanes = slice((2 * index + half) * BAND, (2 * index + half + 1) * BAND)
            measured_ref[tile ^ 1, half * 16 : (half + 1) * 16] = arrived_ref[
                RUN + LINES :, lanes
            ].astype(F32)
    empty = jnp.zeros((8, BAND), F32)
    arrived = arrived_ref[:RUN].astype(F32)
    for slot in range(SLOTS):
        low = slot * 8
        total = kept_ref[low : low + 8] + arrived[low : low + 8]
        band = got_ref[me * SLOTS + slot].astype(F32)
        offset = band[9:10, 0:1].astype(jnp.int32)
        width = jnp.maximum(band[9:10, 1:2], 1.0)
        recip = 1.0 / width
        width = width.astype(jnp.int32)

        def inside(delta):
            delta = delta - offset
            return jnp.where((delta >= 0) & (delta < width), recip, 0.0).astype(BF16)

        shape = (2 * BAND, BAND)
        onward = inside(iota(shape, 1) + BAND - iota(shape, 0))
        back = inside(iota(shape, 0) - iota(shape, 1))
        parts = [total[:, n * BAND : (n + 1) * BAND] for n in range(blocks)]
        here = jnp.concatenate(parts, axis=0)
        before = jnp.concatenate([empty] + parts[:-1], axis=0)
        paired = jnp.concatenate([before, here], axis=1)
        high = paired.astype(BF16)
        rest = (paired - high.astype(F32)).astype(BF16)
        sums = jnp.dot(high, onward, preferred_element_type=F32) + jnp.dot(
            rest, onward, preferred_element_type=F32
        )
        rows = measured_ref[:, low : low + 8].reshape(blocks * 8, BAND)
        residual = (sums - rows).astype(BF16).astype(F32)
        later = jnp.concatenate([residual[8:], empty], axis=0)
        both = jnp.concatenate([residual, later], axis=1).astype(BF16)
        image = jnp.dot(both, back, preferred_element_type=F32)
        image = jnp.concatenate([image[n * 8 : (n + 1) * 8] for n in range(blocks)], axis=1)
        if slot % 2 == 0:
            even = image
        else:
            out_ref[low - 8 : low + 8] = jnp.concatenate([even, image], axis=0).astype(BF16)


def residual_images(place, kept, strips, arrived, got, *order):
    return pl.pallas_call(
        residual_kernel,
        out_shape=jax.ShapeDtypeStruct(kept.shape, BF16),
        in_specs=[SMEM] + [VMEM] * 4 + [ANY] * len(order),
        out_specs=VMEM,
        scratch_shapes=[pltpu.VMEM((kept.shape[1] // BAND, RUN, BAND), F32)],
        compiler_params=limit(8),
        cost_estimate=cost(4 * 8 * 16 * 256 * 128 * 6, 12 * kept.size),
        name="residual_images",
    )(place, kept, strips, arrived, got, *order)


def penalty(diff):
    return diff * lax.rsqrt(1.0 + diff * diff)


def regularizer_kernel(
    first_tile,
    count,
    place_ref,
    beta_ref,
    volume_ref,
    below_ref,
    above_ref,
    *refs,
):
    out_ref, token_ref, under_ref, buffer_ref, sem_ref = refs[-5:]
    step, steps = pl.program_id(0), pl.num_programs(0)

    @pl.when(step == 0)
    def _():
        start(tile_copies(volume_ref, buffer_ref, sem_ref, 0, first_tile, EDGE))

    block_ref = streamed(volume_ref, buffer_ref, sem_ref, step, steps, first_tile, EDGE)
    depth, strip, tile = block_ref.shape[0], block_ref.shape[2], XT
    at = pl.program_id(0) + first_tile
    beta = beta_ref[0]
    has_below = (place_ref[0] > 0).astype(F32)
    has_above = (place_ref[0] < place_ref[3] - 1).astype(F32)
    has_before = (at > 0).astype(F32)
    has_after = (at < count - 1).astype(F32)
    here = pl.ds(EDGE, tile)
    under_ref[...] = (
        penalty(block_ref[0, here].astype(F32) - below_ref[0].astype(F32)) * has_below
    )
    row = iota((tile, strip), 0)
    lane = iota((tile, strip), 1)

    def body(z, carry):
        center = block_ref[z, here].astype(F32)
        top = z == depth - 1
        upper = jnp.where(top, above_ref[0], block_ref[jnp.minimum(z + 1, depth - 1), here])
        over = penalty(upper.astype(F32) - center) * jnp.where(top, has_above, 1.0)
        total = under_ref[...] - over
        under_ref[...] = over
        ahead = block_ref[z, pl.ds(EDGE + tile, EDGE)].astype(F32)[0:1]
        behind = block_ref[z, pl.ds(0, EDGE)].astype(F32)[EDGE - 1 :]
        behind = penalty(center[0:1] - behind) * has_before
        along = penalty(jnp.where(row == tile - 1, ahead, pltpu.roll(center, tile - 1, 0)) - center)
        along = jnp.where(row == tile - 1, along * has_after, along)
        total = total + jnp.where(row == 0, behind, pltpu.roll(along, 1, 0)) - along
        across = penalty(pltpu.roll(center, strip - 1, 1) - center)
        across = jnp.where(lane == strip - 1, 0.0, across)
        total = total + pltpu.roll(across, 1, 1) - across
        out_ref[z] = (total * beta).astype(BF16)
        return carry

    lax.fori_loop(0, depth, body, 0, unroll=2)
    token_ref[...] = under_ref[:8]


def regularizer(index, done, place, beta, volume, below, above, *order):
    depth, extent, strip = volume.shape
    count = extent // XT
    length = count // PIECES
    origin = index * length
    plane = pl.BlockSpec((1, XT, strip), lambda i: (0, origin + i, 0))
    block = pl.BlockSpec((depth, XT, strip), lambda i: (0, origin + i, 0))
    specs = [SMEM, SMEM, HBM]
    specs += [plane] * 2 + [ANY] * len(order)
    before = [] if done is None else [done]
    return pl.pallas_call(
        functools.partial(regularizer_kernel, origin, count),
        grid=(length,),
        out_shape=(pltpu.HBM(volume.shape, BF16), jax.ShapeDtypeStruct((8, strip), F32)),
        in_specs=specs + [HBM] * len(before),
        out_specs=(block, pl.BlockSpec((8, strip), lambda i: (0, 0))),
        scratch_shapes=[pltpu.VMEM((XT, strip), F32)] + stream_scratch(depth, strip, EDGE),
        compiler_params=limit(8),
        input_output_aliases={len(specs): 0} if before else {},
        cost_estimate=cost(30 * volume.size // PIECES, 8 * volume.size // PIECES),
        name="regularizer",
    )(place, beta, volume, below, above, *order, *before)


def gradient_kernel(place_ref, beta_ref, spread_ref, mine_ref, beside_ref, *refs):
    chunk_refs = refs[:-6]
    whole_ref, out_ref, buffer_ref, sem_ref, result_ref, result_sem_ref = refs[-6:]
    depth, extent, strip = whole_ref.shape
    steps = extent // WIDE
    beta = beta_ref[0]
    has_left = (place_ref[1] > 0).astype(F32)
    has_right = (place_ref[1] < place_ref[2] - 1).astype(F32)
    start(tile_copies(whole_ref, buffer_ref, sem_ref, 0, tile=WIDE))

    def result(step):
        slot = lax.rem(step, 2)
        here = pl.ds(pl.multiple_of(step * WIDE, WIDE), WIDE)
        return pltpu.make_async_copy(
            result_ref.at[slot], out_ref.at[:, here], result_sem_ref.at[slot]
        )

    def body(step, carry):
        here = pl.ds(pl.multiple_of(step * WIDE, WIDE), WIDE)
        mine = mine_ref[:, here].astype(F32)
        beside = beside_ref[RUN : RUN + LINES, here].astype(F32)
        on_left = penalty(mine[:8] - beside[:8]) * (has_left * beta)
        on_right = penalty(mine[8:] - beside[8:]) * (has_right * beta)
        ends = jnp.concatenate([on_left, on_right], axis=0).astype(BF16)
        rows = jnp.concatenate([ref[:, here] for ref in chunk_refs] + [ends], axis=0)
        out = lax.dot_general(
            rows, spread_ref[...], (((0,), (0,)), ((), ())), preferred_element_type=F32
        )
        regular_ref = streamed(whole_ref, buffer_ref, sem_ref, step, steps, tile=WIDE)

        @pl.when(step >= 2)
        def _():
            result(step - 2).wait()

        slot = lax.rem(step, 2)
        for z in range(depth):
            regular = regular_ref[z].astype(F32)
            result_ref[slot, z] = (out[:, z * strip : (z + 1) * strip] + regular).astype(BF16)
        result(step).start()
        return carry

    lax.fori_loop(0, steps, body, 0)
    result(jnp.int32(steps - 2)).wait()
    result(jnp.int32(steps - 1)).wait()


def gradient(place, beta, spread, mine, arrived, chunks, regular):
    depth, extent, strip = regular.shape
    size = depth * extent * strip
    return pl.pallas_call(
        gradient_kernel,
        out_shape=jax.ShapeDtypeStruct(regular.shape, BF16),
        in_specs=[SMEM, SMEM] + [VMEM] * (3 + len(chunks)) + [HBM],
        out_specs=ANY,
        scratch_shapes=stream_scratch(depth, strip, tile=WIDE)
        + [pltpu.VMEM((2, depth, WIDE, strip), BF16), pltpu.SemaphoreType.DMA((2,))],
        compiler_params=limit(16),
        cost_estimate=cost(2 * spread.shape[0] * size, 5 * size),
        name="gradient",
    )(place, beta, spread, mine, arrived, *chunks, regular)


def shards(volume, measured, ray_weight, view_owner, band_offset, band_width, beta):
    slabs = lax.axis_size("slab")
    tiles = lax.axis_size("tile")
    slab, tile = lax.axis_index("slab"), lax.axis_index("tile")
    depth = volume.shape[0]
    place = jnp.stack([slab, tile, jnp.int32(tiles), jnp.int32(slabs)])

    def along_z(block, by):
        return lax.ppermute(block, "tile", [(i, (i + 2 * by) % tiles) for i in range(tiles)])

    def along_y(block):
        return lax.ppermute(block, "tile", [(i, i ^ 1) for i in range(tiles)])

    packed = pack(view_owner[:, :, 0], band_offset, band_width, ray_weight, measured, slabs)
    packed, after = lax.optimization_barrier((packed, volume))
    got = lax.all_to_all(packed, "slab", split_axis=0, concat_axis=0, tiled=True)
    top, bottom = after[depth - 1 :], after[:1]
    below = lax.ppermute(top, "slab", [(i, i + 1) for i in range(slabs - 1)])
    above = lax.ppermute(bottom, "slab", [(i + 1, i) for i in range(slabs - 1)])
    flat = got.reshape(slabs * SLOTS, ROWS, BAND)
    volume = pltpu.with_memory_space_constraint(volume, pltpu.HBM)

    own, up1, down1, up2, down2, up3, down3, up, down, ends = forward(
        place, flat, volume, tiles, top, bottom
    )
    extent = ends.shape[1]
    spread = spread_rows(place, flat, tiles, ends)
    order, regular = [spread], None
    for index, (own_up, own_down) in enumerate([(up3, down3), (up2, down2), (up1, down1)]):
        came = along_z(up, 1), along_z(down, -1)
        up, down = ring_sums(came[0], own_up, came[1], own_down, extent, *order)
        regular, token = regularizer(index, regular, place, beta, volume, below, above, up)
        order = [token]
    came = along_z(up, 1), along_z(down, -1)
    kept, strips, sent = last_sums(place, own, ends, *came, *order)
    arrived = along_y(sent)
    regular, token = regularizer(3, regular, place, beta, volume, below, above, sent)
    images = residual_images(place, kept, strips, arrived, flat, token)

    partner = along_y(images)
    rings = []
    for first, past in ((images, 1), (partner, -1)):
        up, down = first, first
        ring = {0: first}
        for hop in range(1, tiles // 4):
            up, down = along_z(up, 1), along_z(down, -1)
            ring[-hop], ring[hop] = up, down
        ring[tiles // 4] = along_z(ring[-2 * past], 2 * past)
        rings.append(ring)
    chunks = [ring[hop] for hop in hops(tiles) for ring in rings]
    regular = pltpu.with_memory_space_constraint(regular, pltpu.HBM)
    return gradient(place, beta, spread, ends, arrived, chunks, regular)


def solution(mesh):
    in_specs = (
        P("slab", None, "tile"),
        P(None, "slab", None, "tile"),
        P(None, "slab", "tile"),
        P(None, "slab", None),
        P(None, "slab"),
        P(None, "slab"),
        P(),
    )
    out_specs = P("slab", None, "tile")
    return jax.shard_map(shards, mesh=mesh, in_specs=in_specs, out_specs=out_specs, check_vma=False)
```

```python
import functools

import jax
import jax.numpy as jnp
from jax import lax
from jax.experimental import pallas as pl
from jax.experimental.pallas import tpu as pltpu
from jax.sharding import PartitionSpec as P

BAND = 128
BATCHES = 2
CAPP = 2
SLOTS = BATCHES * CAPP
ROWS = 16
RUN = SLOTS * 8
PAIR = 2 * RUN
LINES = 16
EDGE = 16
PIECES = 4


def limit(mib):
    return pltpu.CompilerParams(vmem_limit_bytes=mib << 20)

XT = 256
WIDE = 512
F32 = jnp.float32
BF16 = jnp.bfloat16
VMEM = pl.BlockSpec(memory_space=pltpu.VMEM)
SMEM = pl.BlockSpec(memory_space=pltpu.SMEM)
ANY = pl.BlockSpec(memory_space=pl.ANY)
HBM = pl.BlockSpec(memory_space=pltpu.HBM)


def cost(flops, moved):
    return pl.CostEstimate(flops=flops, bytes_accessed=moved, transcendentals=0)


def iota(shape, dim):
    return lax.broadcasted_iota(jnp.int32, shape, dim)


def pack_kernel(
    owner_ref,
    offset_ref,
    width_ref,
    weight_ref,
    measured_ref,
    volume_ref,
    out_ref,
    top_ref,
    bottom_ref,
    count_ref,
    sem_ref,
):
    depth = volume_ref.shape[0]
    slices = [
        pltpu.make_async_copy(volume_ref.at[pl.ds(z, 1)], ref, sem_ref.at[index])
        for index, (z, ref) in enumerate(((depth - 1, top_ref), (0, bottom_ref)))
    ]
    for copy in slices:
        copy.start()
    out_ref[...] = jnp.zeros_like(out_ref)
    slabs = out_ref.shape[0]
    views = owner_ref.shape[1]
    row = iota((ROWS, BAND), 0)
    lane = iota((ROWS, BAND), 1)
    empty = jnp.zeros((8, BAND), F32)
    for batch in range(BATCHES):
        for slab in range(slabs):
            count_ref[slab] = 0
        for view in range(views):
            owner = owner_ref[batch, view]
            rank = count_ref[owner]
            count_ref[owner] = rank + 1
            rows = jnp.concatenate([measured_ref[batch, view].astype(F32), empty], axis=0)
            band = jnp.where(
                lane == 0,
                offset_ref[batch, view].astype(F32),
                jnp.where(lane == 1, width_ref[batch, view].astype(F32), 0.0),
            )
            rows = jnp.where(row == 8, weight_ref[view].astype(F32)[batch : batch + 1], jnp.where(row == 9, band, rows))
            out_ref[owner, batch * CAPP + rank] = rows.astype(BF16)
    for copy in slices:
        copy.wait()


def pack(owner, offset, width, weight, measured, volume, slabs):
    plane = jax.ShapeDtypeStruct((1,) + volume.shape[1:], BF16)
    return pl.pallas_call(
        pack_kernel,
        out_shape=(
            jax.ShapeDtypeStruct((slabs, SLOTS, ROWS, BAND), BF16),
            plane,
            plane,
        ),
        in_specs=[SMEM, SMEM, SMEM, VMEM, VMEM, HBM],
        out_specs=(VMEM, ANY, ANY),
        scratch_shapes=[pltpu.SMEM((slabs,), jnp.int32), pltpu.SemaphoreType.DMA((2,))],
        name="pack_messages",
    )(owner, offset, width, jnp.transpose(weight, (1, 0, 2)), measured, volume)


def joined(block):
    return jnp.concatenate([block[z] for z in range(block.shape[0])], axis=1)


def tile_copies(ref, buffer_ref, sem_ref, index, first=0, edge=0, tile=XT):
    slot = lax.rem(index, 2)
    extent = ref.shape[1]
    start = (first + index) * tile
    parts = [(start, edge, tile)]
    if edge:
        parts.append((jnp.maximum(start - edge, 0), 0, edge))
        parts.append((jnp.minimum(start + tile, extent - edge), edge + tile, edge))
    return [
        pltpu.make_async_copy(
            ref.at[:, pl.ds(pl.multiple_of(source, 16), size)],
            buffer_ref.at[slot, pl.ds(0, ref.shape[0]), pl.ds(target, size)],
            sem_ref.at[slot, part],
        )
        for part, (source, target, size) in enumerate(parts)
    ]


def start(copies):
    for copy in copies:
        copy.start()


def streamed(ref, buffer_ref, sem_ref, step, steps, first=0, edge=0, tile=XT):
    @pl.when(step + 1 < steps)
    def _():
        start(tile_copies(ref, buffer_ref, sem_ref, step + 1, first, edge, tile))

    for copy in tile_copies(ref, buffer_ref, sem_ref, step, first, edge, tile):
        copy.wait()
    return buffer_ref.at[lax.rem(step, 2)]


def stream_scratch(depth, strip, edge=0, tile=XT):
    return [
        pltpu.VMEM((2, depth + (1 if edge else 0), tile + 2 * edge, strip), BF16),
        pltpu.SemaphoreType.DMA((2, 3 if edge else 1)),
    ]


def spread_weights(tiles, out_ref, first, depth):
    rows = tiles.shape[0] * depth
    weights = jnp.broadcast_to(
        tiles.astype(F32)[:, 8:9, :], (tiles.shape[0], depth, BAND)
    ).reshape(rows, BAND)
    slice_of = lax.rem(iota((rows, BAND), 0), depth)
    for z in range(depth):
        out_ref[first : first + rows, z * BAND : (z + 1) * BAND] = jnp.where(
            slice_of == z, weights, 0.0
        ).astype(BF16)


def hops(tiles):
    half = tiles // 4
    return [0] + [sign * hop for hop in range(1, half) for sign in (1, -1)] + [half]


def fill_spread(tiles, me, got_ref, spread_ref):
    row = 0
    for hop in hops(tiles):
        tile = lax.rem(me + 2 * hop + tiles, tiles)
        for source in (tile, tile ^ 1):
            spread_weights(got_ref[pl.ds(source * SLOTS, SLOTS)], spread_ref, row, 8)
            row += RUN
    shape = (LINES, spread_ref.shape[1])
    line = iota(shape, 0)
    target = jnp.where(line < 8, line * BAND, (line - 8) * BAND + BAND - 1)
    spread_ref[row:] = jnp.where(iota(shape, 1) == target, 1.0, 0.0).astype(BF16)


def spread_kernel(tiles, place_ref, got_ref, order_ref, out_ref):
    fill_spread(tiles, place_ref[1], got_ref, out_ref)


def spread_rows(place, got, tiles, order):
    shape = (got.shape[0] * 8 + LINES, 8 * BAND)
    return pl.pallas_call(
        functools.partial(spread_kernel, tiles),
        out_shape=jax.ShapeDtypeStruct(shape, BF16),
        in_specs=[SMEM, VMEM, ANY],
        out_specs=VMEM,
        compiler_params=limit(8),
        cost_estimate=cost(4 * shape[0] * shape[1], 4 * shape[0] * shape[1]),
        name="spread_rows",
    )(place, got, order)


def measured_rows(got_ref, source):
    rows = got_ref[pl.ds(source * SLOTS, SLOTS)].astype(F32)[:, :8]
    return rows.reshape(RUN, BAND).astype(BF16)


def forward_kernel(tiles, place_ref, got_ref, volume_ref, *refs):
    outs, (ends_ref, spread_ref, buffer_ref, sem_ref, last_ref, first_ref) = refs[:-6], refs[-6:]
    extent = volume_ref.shape[1]
    me = place_ref[1]
    start(tile_copies(volume_ref, buffer_ref, sem_ref, 0, tile=WIDE))
    fill_spread(tiles, me, got_ref, spread_ref)
    where = [(ref, row) for ref in outs for row in range(0, ref.shape[0], RUN)]
    beyond = pl.ds(extent, BAND)
    for index, hop in enumerate(hops(tiles)):
        tile = lax.rem(me + 2 * hop + tiles, tiles)
        for turn, source in enumerate((tile, tile ^ 1)):
            ref, row = where[2 * index + turn]
            ref[row : row + RUN, beyond] = measured_rows(got_ref, source)
    steps = extent // WIDE

    def body(step, carry):
        block_ref = streamed(volume_ref, buffer_ref, sem_ref, step, steps, tile=WIDE)
        out = lax.dot_general(
            spread_ref[...],
            joined(block_ref),
            (((1,), (1,)), ((), ())),
            preferred_element_type=F32,
        ).astype(BF16)
        here = pl.ds(pl.multiple_of(step * WIDE, WIDE), WIDE)
        for index, (ref, row) in enumerate(where):
            ref[row : row + RUN, here] = out[index * RUN : (index + 1) * RUN]
        ends_ref[:, here] = out[-LINES:]
        ends = out[-LINES:].astype(F32)
        count = WIDE // XT
        for part in range(count):
            there = pl.ds(pl.multiple_of((step * count + part) * 8, 8), 8)
            first_ref[there] = ends[:8, part * XT : (part + 1) * XT]
            last_ref[there] = ends[8:, part * XT : (part + 1) * XT]
        return carry

    lax.fori_loop(0, steps, body, 0)
    outs[1][:, extent + BAND :] = last_ref[...].astype(BF16)
    outs[2][:, extent + BAND :] = first_ref[...].astype(BF16)


def forward(place, got, volume, tiles, *order):
    depth, extent, strip = volume.shape
    slots = got.shape[0]
    rows = [PAIR] * (tiles // 2 - 1) + [RUN] * 2
    lanes = [extent + BAND + (XT if index in (1, 2) else 0) for index in range(len(rows))]

    def kernel(place_ref, got_ref, volume_ref, *refs):
        forward_kernel(tiles, place_ref, got_ref, volume_ref, *refs[len(order) :])

    return pl.pallas_call(
        kernel,
        out_shape=[jax.ShapeDtypeStruct(shape, BF16) for shape in zip(rows, lanes)]
        + [jax.ShapeDtypeStruct((LINES, extent), BF16)],
        in_specs=[SMEM, VMEM, HBM] + [ANY] * len(order),
        out_specs=[VMEM] * (len(rows) + 1),
        scratch_shapes=[pltpu.VMEM((slots * depth + LINES, depth * strip), BF16)]
        + stream_scratch(depth, strip, tile=WIDE)
        + [pltpu.VMEM((extent // XT * 8, XT), F32)] * 2,
        compiler_params=limit(12),
        cost_estimate=cost(2 * slots * depth * volume.size, 3 * volume.size),
        name="forward",
    )(place, got, volume, *order)


def sums_kernel(extent, from_below_ref, up_ref, from_above_ref, down_ref, *refs):
    for came_ref, own_ref, low, out_ref in (
        (from_below_ref, up_ref, 0, refs[-2]),
        (from_above_ref, down_ref, RUN, refs[-1]),
    ):
        came_lanes = came_ref.shape[1] - extent
        past = extent + BAND
        for row in (0, RUN):
            rows = slice(row, row + RUN)
            total = own_ref[rows, :extent].astype(F32)
            strips = jnp.zeros((RUN, came_lanes), BF16)
            if came_ref.shape[0] > RUN or row == low:
                came = rows if came_ref.shape[0] > RUN else slice(0, RUN)
                total = total + came_ref[came, :extent].astype(F32)
                strips = came_ref[came, extent:]
            out_ref[rows, :extent] = total.astype(BF16)
            out_ref[rows, extent:past] = own_ref[rows, extent:past]
            out_ref[rows, past : past + came_lanes] = strips
        if own_ref.shape[1] > past:
            out_ref[:, past + came_lanes :] = own_ref[:, past:]


def ring_sums(from_below, up, from_above, down, extent, *order):
    out = jax.ShapeDtypeStruct((PAIR, up.shape[1] + from_below.shape[1] - extent), BF16)
    return pl.pallas_call(
        functools.partial(sums_kernel, extent),
        out_shape=(out, out),
        in_specs=[VMEM] * 4 + [ANY] * len(order),
        out_specs=(VMEM, VMEM),
        compiler_params=limit(8),
        cost_estimate=cost(6 * out.size, 12 * out.size),
        name="ring_sums",
    )(from_below, up, from_above, down, *order)


STRIPS = (0, -1, 1, -2, 2, -3, 3, 4)


def last_sums_kernel(place_ref, own_ref, ends_ref, below_ref, above_ref, *refs):
    kept_ref, strips_ref, sent_ref = refs[-3:]
    extent = ends_ref.shape[1]
    blocks = [slice(extent + n * BAND, extent + (n + 1) * BAND) for n in range(4)]
    for row in (0, RUN):
        rows = slice(row, row + RUN)
        total = (
            own_ref[rows, :extent].astype(F32)
            + below_ref[rows, :extent].astype(F32)
            + above_ref[rows, :extent].astype(F32)
        )
        strips = [own_ref[rows, blocks[0]]]
        for n in range(3):
            strips += [below_ref[rows, blocks[n]], above_ref[rows, blocks[n]]]
        strips.append((below_ref if row == 0 else above_ref)[rows, blocks[3]])
        if row == 0:
            kept_ref[...] = total
            for index, strip in enumerate(strips):
                strips_ref[:, index * BAND : (index + 1) * BAND] = strip
        else:
            sent_ref[:RUN] = total.astype(BF16)
            halves = [strip[low : low + 16] for strip in strips for low in (0, 16)]
            sent_ref[RUN + LINES :] = jnp.concatenate(halves, axis=1)

    def column(ref):
        tiled = ref[:, blocks[3].stop :].astype(F32)
        return jnp.concatenate([tiled[n * 8 : (n + 1) * 8] for n in range(extent // XT)], axis=1)

    mine = ends_ref[...].astype(F32)
    even = place_ref[1] % 2 == 0
    left = jnp.where(even, mine[8:], column(below_ref))
    right = jnp.where(even, column(above_ref), mine[:8])
    sent_ref[RUN : RUN + LINES] = jnp.concatenate([left, right], axis=0).astype(BF16)


def last_sums(place, own, ends, below, above, *order):
    extent = ends.shape[1]
    return pl.pallas_call(
        last_sums_kernel,
        out_shape=(
            jax.ShapeDtypeStruct((RUN, extent), F32),
            jax.ShapeDtypeStruct((RUN, len(STRIPS) * BAND), BF16),
            jax.ShapeDtypeStruct((RUN + LINES + 16, extent), BF16),
        ),
        in_specs=[SMEM] + [VMEM] * 4 + [ANY] * len(order),
        out_specs=(VMEM,) * 3,
        compiler_params=limit(8),
        cost_estimate=cost(5 * own.size, 14 * own.size),
        name="last_sums",
    )(place, own, ends, below, above, *order)


def residual_kernel(place_ref, kept_ref, strips_ref, arrived_ref, got_ref, *refs):
    out_ref, measured_ref = refs[-2:]
    extent = kept_ref.shape[1]
    blocks = extent // BAND
    me = place_ref[1]
    for index, hop in enumerate(STRIPS):
        tile = lax.rem(me + 2 * hop + blocks, blocks)
        measured_ref[tile] = strips_ref[:, index * BAND : (index + 1) * BAND].astype(F32)
        for half in (0, 1):
            lanes = slice((2 * index + half) * BAND, (2 * index + half + 1) * BAND)
            measured_ref[tile ^ 1, half * 16 : (half + 1) * 16] = arrived_ref[
                RUN + LINES :, lanes
            ].astype(F32)
    empty = jnp.zeros((8, BAND), F32)
    arrived = arrived_ref[:RUN].astype(F32)
    for slot in range(SLOTS):
        low = slot * 8
        total = kept_ref[low : low + 8] + arrived[low : low + 8]
        band = got_ref[me * SLOTS + slot].astype(F32)
        offset = band[9:10, 0:1].astype(jnp.int32)
        width = jnp.maximum(band[9:10, 1:2], 1.0)
        recip = 1.0 / width
        width = width.astype(jnp.int32)

        def inside(delta):
            delta = delta - offset
            return jnp.where((delta >= 0) & (delta < width), recip, 0.0).astype(BF16)

        shape = (2 * BAND, BAND)
        onward = inside(iota(shape, 1) + BAND - iota(shape, 0))
        back = inside(iota(shape, 0) - iota(shape, 1))
        parts = [total[:, n * BAND : (n + 1) * BAND] for n in range(blocks)]
        here = jnp.concatenate(parts, axis=0)
        before = jnp.concatenate([empty] + parts[:-1], axis=0)
        paired = jnp.concatenate([before, here], axis=1)
        high = paired.astype(BF16)
        rest = (paired - high.astype(F32)).astype(BF16)
        sums = jnp.dot(high, onward, preferred_element_type=F32) + jnp.dot(
            rest, onward, preferred_element_type=F32
        )
        rows = measured_ref[:, low : low + 8].reshape(blocks * 8, BAND)
        residual = (sums - rows).astype(BF16).astype(F32)
        later = jnp.concatenate([residual[8:], empty], axis=0)
        both = jnp.concatenate([residual, later], axis=1).astype(BF16)
        image = jnp.dot(both, back, preferred_element_type=F32)
        image = jnp.concatenate([image[n * 8 : (n + 1) * 8] for n in range(blocks)], axis=1)
        if slot % 2 == 0:
            even = image
        else:
            out_ref[low - 8 : low + 8] = jnp.concatenate([even, image], axis=0).astype(BF16)


def residual_images(place, kept, strips, arrived, got, *order):
    return pl.pallas_call(
        residual_kernel,
        out_shape=jax.ShapeDtypeStruct(kept.shape, BF16),
        in_specs=[SMEM] + [VMEM] * 4 + [ANY] * len(order),
        out_specs=VMEM,
        scratch_shapes=[pltpu.VMEM((kept.shape[1] // BAND, RUN, BAND), F32)],
        compiler_params=limit(8),
        cost_estimate=cost(4 * 8 * 16 * 256 * 128 * 6, 12 * kept.size),
        name="residual_images",
    )(place, kept, strips, arrived, got, *order)


def penalty(diff):
    return diff * lax.rsqrt(1.0 + diff * diff)


def regularizer_kernel(
    first_tile,
    count,
    place_ref,
    beta_ref,
    volume_ref,
    below_ref,
    above_ref,
    *refs,
):
    out_ref, token_ref, under_ref, buffer_ref, sem_ref = refs[-5:]
    step, steps = pl.program_id(0), pl.num_programs(0)

    @pl.when(step == 0)
    def _():
        start(tile_copies(volume_ref, buffer_ref, sem_ref, 0, first_tile, EDGE))

    block_ref = streamed(volume_ref, buffer_ref, sem_ref, step, steps, first_tile, EDGE)
    depth, strip, tile = volume_ref.shape[0], volume_ref.shape[2], XT
    at = pl.program_id(0) + first_tile
    beta = beta_ref[0]
    has_below, has_above = place_ref[0] > 0, place_ref[0] < place_ref[3] - 1
    here = pl.ds(EDGE, tile)
    bottom, top = block_ref[0, here], block_ref[depth - 1, here]
    below = jnp.where(has_below, below_ref[0], bottom).astype(F32)
    block_ref[depth, here] = jnp.where(has_above, above_ref[0], top)
    under_ref[...] = penalty(bottom.astype(F32) - below)
    row = iota((tile, strip), 0)
    lane = iota((tile, strip), 1)

    def body(z, carry):
        center = block_ref[z, here].astype(F32)
        over = penalty(block_ref[z + 1, here].astype(F32) - center)
        total = under_ref[...] - over
        under_ref[...] = over
        behind = block_ref[z, pl.ds(0, EDGE)].astype(F32)
        behind = jnp.where(at > 0, behind[EDGE - 1 :], behind[:1])
        ahead = block_ref[z, pl.ds(EDGE + tile, EDGE)].astype(F32)
        ahead = jnp.where(at < count - 1, ahead[:1], ahead[EDGE - 1 :])
        along = penalty(jnp.where(row == tile - 1, ahead, pltpu.roll(center, tile - 1, 0)) - center)
        behind = penalty(center[:1] - behind)
        total = total + jnp.where(row == 0, behind, pltpu.roll(along, 1, 0)) - along
        across = penalty(pltpu.roll(center, strip - 1, 1) - center)
        across = jnp.where(lane == strip - 1, 0.0, across)
        total = total + pltpu.roll(across, 1, 1) - across
        out_ref[z] = (total * beta).astype(BF16)
        return carry

    lax.fori_loop(0, depth, body, 0, unroll=2)
    token_ref[...] = under_ref[:8]


def regularizer(index, done, place, beta, volume, below, above, *order):
    depth, extent, strip = volume.shape
    count = extent // XT
    length = count // PIECES
    origin = index * length
    plane = pl.BlockSpec((1, XT, strip), lambda i: (0, origin + i, 0))
    block = pl.BlockSpec((depth, XT, strip), lambda i: (0, origin + i, 0))
    specs = [SMEM, SMEM, HBM]
    specs += [plane] * 2 + [ANY] * len(order)
    before = [] if done is None else [done]
    return pl.pallas_call(
        functools.partial(regularizer_kernel, origin, count),
        grid=(length,),
        out_shape=(pltpu.HBM(volume.shape, BF16), jax.ShapeDtypeStruct((8, strip), F32)),
        in_specs=specs + [HBM] * len(before),
        out_specs=(block, pl.BlockSpec((8, strip), lambda i: (0, 0))),
        scratch_shapes=[pltpu.VMEM((XT, strip), F32)] + stream_scratch(depth, strip, EDGE),
        compiler_params=limit(8),
        input_output_aliases={len(specs): 0} if before else {},
        cost_estimate=cost(30 * volume.size // PIECES, 8 * volume.size // PIECES),
        name="regularizer",
    )(place, beta, volume, below, above, *order, *before)


def gradient_kernel(place_ref, beta_ref, spread_ref, mine_ref, beside_ref, *refs):
    chunk_refs = refs[:-6]
    whole_ref, out_ref, buffer_ref, sem_ref, result_ref, result_sem_ref = refs[-6:]
    depth, extent, strip = whole_ref.shape
    steps = extent // WIDE
    beta = beta_ref[0]
    has_left = (place_ref[1] > 0).astype(F32)
    has_right = (place_ref[1] < place_ref[2] - 1).astype(F32)
    start(tile_copies(whole_ref, buffer_ref, sem_ref, 0, tile=WIDE))

    def result(step):
        slot = lax.rem(step, 2)
        here = pl.ds(pl.multiple_of(step * WIDE, WIDE), WIDE)
        return pltpu.make_async_copy(
            result_ref.at[slot], out_ref.at[:, here], result_sem_ref.at[slot]
        )

    def body(step, carry):
        here = pl.ds(pl.multiple_of(step * WIDE, WIDE), WIDE)
        mine = mine_ref[:, here].astype(F32)
        beside = beside_ref[RUN : RUN + LINES, here].astype(F32)
        on_left = penalty(mine[:8] - beside[:8]) * (has_left * beta)
        on_right = penalty(mine[8:] - beside[8:]) * (has_right * beta)
        ends = jnp.concatenate([on_left, on_right], axis=0).astype(BF16)
        rows = jnp.concatenate([ref[:, here] for ref in chunk_refs] + [ends], axis=0)
        out = lax.dot_general(
            rows, spread_ref[...], (((0,), (0,)), ((), ())), preferred_element_type=F32
        )
        regular_ref = streamed(whole_ref, buffer_ref, sem_ref, step, steps, tile=WIDE)

        @pl.when(step >= 2)
        def _():
            result(step - 2).wait()

        slot = lax.rem(step, 2)
        for z in range(depth):
            regular = regular_ref[z].astype(F32)
            result_ref[slot, z] = (out[:, z * strip : (z + 1) * strip] + regular).astype(BF16)
        result(step).start()
        return carry

    lax.fori_loop(0, steps, body, 0)
    result(jnp.int32(steps - 2)).wait()
    result(jnp.int32(steps - 1)).wait()


def gradient(place, beta, spread, mine, arrived, chunks, regular):
    depth, extent, strip = regular.shape
    size = depth * extent * strip
    return pl.pallas_call(
        gradient_kernel,
        out_shape=jax.ShapeDtypeStruct(regular.shape, BF16),
        in_specs=[SMEM, SMEM] + [VMEM] * (3 + len(chunks)) + [HBM],
        out_specs=ANY,
        scratch_shapes=stream_scratch(depth, strip, tile=WIDE)
        + [pltpu.VMEM((2, depth, WIDE, strip), BF16), pltpu.SemaphoreType.DMA((2,))],
        compiler_params=limit(16),
        cost_estimate=cost(2 * spread.shape[0] * size, 5 * size),
        name="gradient",
    )(place, beta, spread, mine, arrived, *chunks, regular)


def shards(volume, measured, ray_weight, view_owner, band_offset, band_width, beta):
    slabs = lax.axis_size("slab")
    tiles = lax.axis_size("tile")
    slab, tile = lax.axis_index("slab"), lax.axis_index("tile")
    place = jnp.stack([slab, tile, jnp.int32(tiles), jnp.int32(slabs)])

    def along_z(block, by):
        return lax.ppermute(block, "tile", [(i, (i + 2 * by) % tiles) for i in range(tiles)])

    def along_y(block):
        return lax.ppermute(block, "tile", [(i, i ^ 1) for i in range(tiles)])

    volume = pltpu.with_memory_space_constraint(volume, pltpu.HBM)
    packed, top, bottom = pack(
        view_owner[:, :, 0], band_offset, band_width, ray_weight, measured, volume, slabs
    )
    got = lax.all_to_all(packed, "slab", split_axis=0, concat_axis=0, tiled=True)
    below = lax.ppermute(top, "slab", [(i, i + 1) for i in range(slabs - 1)])
    above = lax.ppermute(bottom, "slab", [(i + 1, i) for i in range(slabs - 1)])
    flat = got.reshape(slabs * SLOTS, ROWS, BAND)

    own, up1, down1, up2, down2, up3, down3, up, down, ends = forward(place, flat, volume, tiles)
    extent = ends.shape[1]
    spread = spread_rows(place, flat, tiles, ends)
    order, regular = [spread], None
    for index, (own_up, own_down) in enumerate([(up3, down3), (up2, down2), (up1, down1)]):
        came = along_z(up, 1), along_z(down, -1)
        up, down = ring_sums(came[0], own_up, came[1], own_down, extent, *order)
        regular, token = regularizer(index, regular, place, beta, volume, below, above, up)
        order = [token]
    came = along_z(up, 1), along_z(down, -1)
    kept, strips, sent = last_sums(place, own, ends, *came, *order)
    arrived = along_y(sent)
    regular, token = regularizer(3, regular, place, beta, volume, below, above, sent)
    images = residual_images(place, kept, strips, arrived, flat, token)

    partner = along_y(images)
    rings = []
    for first, past in ((images, 1), (partner, -1)):
        up, down = first, first
        ring = {0: first}
        for hop in range(1, tiles // 4):
            up, down = along_z(up, 1), along_z(down, -1)
            ring[-hop], ring[hop] = up, down
        ring[tiles // 4] = along_z(ring[-2 * past], 2 * past)
        rings.append(ring)
    chunks = [ring[hop] for hop in hops(tiles) for ring in rings]
    regular = pltpu.with_memory_space_constraint(regular, pltpu.HBM)
    return gradient(place, beta, spread, ends, arrived, chunks, regular)


def solution(mesh):
    in_specs = (
        P("slab", None, "tile"),
        P(None, "slab", None, "tile"),
        P(None, "slab", "tile"),
        P(None, "slab", None),
        P(None, "slab"),
        P(None, "slab"),
        P(),
    )
    out_specs = P("slab", None, "tile")
    return jax.shard_map(shards, mesh=mesh, in_specs=in_specs, out_specs=out_specs, check_vma=False)
```

```python
import functools

import jax
import jax.numpy as jnp
from jax import lax
from jax.experimental import pallas as pl
from jax.experimental.pallas import tpu as pltpu
from jax.sharding import PartitionSpec as P

BAND = 128
BATCHES = 2
CAPP = 2
SLOTS = BATCHES * CAPP
ROWS = 16
RUN = SLOTS * 8
PAIR = 2 * RUN
LINES = 16
EDGE = 16
PIECES = 4


def limit(mib):
    return pltpu.CompilerParams(vmem_limit_bytes=mib << 20)

XT = 256
WIDE = 512
TALL = 1024
F32 = jnp.float32
BF16 = jnp.bfloat16
VMEM = pl.BlockSpec(memory_space=pltpu.VMEM)
SMEM = pl.BlockSpec(memory_space=pltpu.SMEM)
ANY = pl.BlockSpec(memory_space=pl.ANY)
HBM = pl.BlockSpec(memory_space=pltpu.HBM)


def cost(flops, moved):
    return pl.CostEstimate(flops=flops, bytes_accessed=moved, transcendentals=0)


def iota(shape, dim):
    return lax.broadcasted_iota(jnp.int32, shape, dim)


def pack_kernel(owner_ref, offset_ref, width_ref, weight_ref, measured_ref, out_ref, count_ref):
    out_ref[...] = jnp.zeros_like(out_ref)
    slabs = out_ref.shape[0]
    views = owner_ref.shape[1]
    row = iota((ROWS, BAND), 0)
    lane = iota((ROWS, BAND), 1)
    empty = jnp.zeros((8, BAND), F32)
    for batch in range(BATCHES):
        for slab in range(slabs):
            count_ref[slab] = 0
        for view in range(views):
            owner = owner_ref[batch, view]
            rank = count_ref[owner]
            count_ref[owner] = rank + 1
            rows = jnp.concatenate([measured_ref[batch, view].astype(F32), empty], axis=0)
            band = jnp.where(
                lane == 0,
                offset_ref[batch, view].astype(F32),
                jnp.where(lane == 1, width_ref[batch, view].astype(F32), 0.0),
            )
            rows = jnp.where(row == 8, weight_ref[view].astype(F32)[batch : batch + 1], jnp.where(row == 9, band, rows))
            out_ref[owner, batch * CAPP + rank] = rows.astype(BF16)


def pack(owner, offset, width, weight, measured, slabs):
    return pl.pallas_call(
        pack_kernel,
        out_shape=jax.ShapeDtypeStruct((slabs, SLOTS, ROWS, BAND), BF16),
        in_specs=[SMEM, SMEM, SMEM, VMEM, VMEM],
        out_specs=VMEM,
        scratch_shapes=[pltpu.SMEM((slabs,), jnp.int32)],
        name="pack_messages",
    )(owner, offset, width, jnp.transpose(weight, (1, 0, 2)), measured)


def joined(block):
    return jnp.concatenate([block[z] for z in range(block.shape[0])], axis=1)


def tile_copies(ref, buffer_ref, sem_ref, index, first=0, edge=0, tile=XT):
    slot = lax.rem(index, 2)
    extent = ref.shape[1]
    start = (first + index) * tile
    parts = [(start, edge, tile)]
    if edge:
        parts.append((jnp.maximum(start - edge, 0), 0, edge))
        parts.append((jnp.minimum(start + tile, extent - edge), edge + tile, edge))
    return [
        pltpu.make_async_copy(
            ref.at[:, pl.ds(pl.multiple_of(source, 16), size)],
            buffer_ref.at[slot, pl.ds(0, ref.shape[0]), pl.ds(target, size)],
            sem_ref.at[slot, part],
        )
        for part, (source, target, size) in enumerate(parts)
    ]


def start(copies):
    for copy in copies:
        copy.start()


def streamed(ref, buffer_ref, sem_ref, step, steps, first=0, edge=0, tile=XT):
    @pl.when(step + 1 < steps)
    def _():
        start(tile_copies(ref, buffer_ref, sem_ref, step + 1, first, edge, tile))

    for copy in tile_copies(ref, buffer_ref, sem_ref, step, first, edge, tile):
        copy.wait()
    return buffer_ref.at[lax.rem(step, 2)]


def stream_scratch(depth, strip, edge=0, tile=XT):
    return [
        pltpu.VMEM((2, depth + (1 if edge else 0), tile + 2 * edge, strip), BF16),
        pltpu.SemaphoreType.DMA((2, 3 if edge else 1)),
    ]


def spread_weights(tiles, out_ref, first, depth):
    rows = tiles.shape[0] * depth
    weights = jnp.broadcast_to(
        tiles.astype(F32)[:, 8:9, :], (tiles.shape[0], depth, BAND)
    ).reshape(rows, BAND)
    slice_of = lax.rem(iota((rows, BAND), 0), depth)
    for z in range(depth):
        out_ref[first : first + rows, z * BAND : (z + 1) * BAND] = jnp.where(
            slice_of == z, weights, 0.0
        ).astype(BF16)


def hops(tiles):
    half = tiles // 4
    return [0] + [sign * hop for hop in range(1, half) for sign in (1, -1)] + [half]


def fill_spread(tiles, me, got_ref, spread_ref):
    row = 0
    for hop in hops(tiles):
        tile = lax.rem(me + 2 * hop + tiles, tiles)
        for source in (tile, tile ^ 1):
            spread_weights(got_ref[pl.ds(source * SLOTS, SLOTS)], spread_ref, row, 8)
            row += RUN
    shape = (LINES, spread_ref.shape[1])
    line = iota(shape, 0)
    target = jnp.where(line < 8, line * BAND, (line - 8) * BAND + BAND - 1)
    spread_ref[row:] = jnp.where(iota(shape, 1) == target, 1.0, 0.0).astype(BF16)


def spread_kernel(tiles, place_ref, got_ref, order_ref, out_ref):
    fill_spread(tiles, place_ref[1], got_ref, out_ref)


def spread_rows(place, got, tiles, order):
    shape = (got.shape[0] * 8 + LINES, 8 * BAND)
    return pl.pallas_call(
        functools.partial(spread_kernel, tiles),
        out_shape=jax.ShapeDtypeStruct(shape, BF16),
        in_specs=[SMEM, VMEM, ANY],
        out_specs=VMEM,
        compiler_params=limit(8),
        cost_estimate=cost(4 * shape[0] * shape[1], 4 * shape[0] * shape[1]),
        name="spread_rows",
    )(place, got, order)


def measured_rows(got_ref, source):
    rows = got_ref[pl.ds(source * SLOTS, SLOTS)].astype(F32)[:, :8]
    return rows.reshape(RUN, BAND).astype(BF16)


def forward_kernel(tiles, place_ref, got_ref, volume_ref, *refs):
    outs, (ends_ref, spread_ref, buffer_ref, sem_ref, last_ref, first_ref) = refs[:-6], refs[-6:]
    extent = volume_ref.shape[1]
    me = place_ref[1]
    start(tile_copies(volume_ref, buffer_ref, sem_ref, 0, tile=TALL))
    fill_spread(tiles, me, got_ref, spread_ref)
    where = [(ref, row) for ref in outs for row in range(0, ref.shape[0], RUN)]
    beyond = pl.ds(extent, BAND)
    for index, hop in enumerate(hops(tiles)):
        tile = lax.rem(me + 2 * hop + tiles, tiles)
        for turn, source in enumerate((tile, tile ^ 1)):
            ref, row = where[2 * index + turn]
            ref[row : row + RUN, beyond] = measured_rows(got_ref, source)
    steps = extent // TALL

    def body(step, carry):
        block_ref = streamed(volume_ref, buffer_ref, sem_ref, step, steps, tile=TALL)
        out = lax.dot_general(
            spread_ref[...],
            joined(block_ref),
            (((1,), (1,)), ((), ())),
            preferred_element_type=F32,
        ).astype(BF16)
        here = pl.ds(pl.multiple_of(step * TALL, TALL), TALL)
        for index, (ref, row) in enumerate(where):
            ref[row : row + RUN, here] = out[index * RUN : (index + 1) * RUN]
        ends_ref[:, here] = out[-LINES:]
        ends = out[-LINES:].astype(F32)
        count = TALL // XT
        for part in range(count):
            there = pl.ds(pl.multiple_of((step * count + part) * 8, 8), 8)
            first_ref[there] = ends[:8, part * XT : (part + 1) * XT]
            last_ref[there] = ends[8:, part * XT : (part + 1) * XT]
        return carry

    lax.fori_loop(0, steps, body, 0)
    outs[1][:, extent + BAND :] = last_ref[...].astype(BF16)
    outs[2][:, extent + BAND :] = first_ref[...].astype(BF16)


def forward(place, got, volume, tiles, *order):
    depth, extent, strip = volume.shape
    slots = got.shape[0]
    rows = [PAIR] * (tiles // 2 - 1) + [RUN] * 2
    lanes = [extent + BAND + (XT if index in (1, 2) else 0) for index in range(len(rows))]

    def kernel(place_ref, got_ref, volume_ref, *refs):
        forward_kernel(tiles, place_ref, got_ref, volume_ref, *refs[len(order) :])

    return pl.pallas_call(
        kernel,
        out_shape=[jax.ShapeDtypeStruct(shape, BF16) for shape in zip(rows, lanes)]
        + [jax.ShapeDtypeStruct((LINES, extent), BF16)],
        in_specs=[SMEM, VMEM, HBM] + [ANY] * len(order),
        out_specs=[VMEM] * (len(rows) + 1),
        scratch_shapes=[pltpu.VMEM((slots * depth + LINES, depth * strip), BF16)]
        + stream_scratch(depth, strip, tile=TALL)
        + [pltpu.VMEM((extent // XT * 8, XT), F32)] * 2,
        compiler_params=limit(16),
        cost_estimate=cost(2 * slots * depth * volume.size, 3 * volume.size),
        name="forward",
    )(place, got, volume, *order)


def sums_kernel(extent, from_below_ref, up_ref, from_above_ref, down_ref, *refs):
    for came_ref, own_ref, low, out_ref in (
        (from_below_ref, up_ref, 0, refs[-2]),
        (from_above_ref, down_ref, RUN, refs[-1]),
    ):
        came_lanes = came_ref.shape[1] - extent
        past = extent + BAND
        for row in (0, RUN):
            rows = slice(row, row + RUN)
            total = own_ref[rows, :extent].astype(F32)
            strips = jnp.zeros((RUN, came_lanes), BF16)
            if came_ref.shape[0] > RUN or row == low:
                came = rows if came_ref.shape[0] > RUN else slice(0, RUN)
                total = total + came_ref[came, :extent].astype(F32)
                strips = came_ref[came, extent:]
            out_ref[rows, :extent] = total.astype(BF16)
            out_ref[rows, extent:past] = own_ref[rows, extent:past]
            out_ref[rows, past : past + came_lanes] = strips
        if own_ref.shape[1] > past:
            out_ref[:, past + came_lanes :] = own_ref[:, past:]


def ring_sums(from_below, up, from_above, down, extent, *order):
    out = jax.ShapeDtypeStruct((PAIR, up.shape[1] + from_below.shape[1] - extent), BF16)
    return pl.pallas_call(
        functools.partial(sums_kernel, extent),
        out_shape=(out, out),
        in_specs=[VMEM] * 4 + [ANY] * len(order),
        out_specs=(VMEM, VMEM),
        compiler_params=limit(8),
        cost_estimate=cost(6 * out.size, 12 * out.size),
        name="ring_sums",
    )(from_below, up, from_above, down, *order)


STRIPS = (0, -1, 1, -2, 2, -3, 3, 4)


def last_sums_kernel(place_ref, own_ref, ends_ref, below_ref, above_ref, *refs):
    kept_ref, strips_ref, sent_ref = refs[-3:]
    extent = ends_ref.shape[1]
    blocks = [slice(extent + n * BAND, extent + (n + 1) * BAND) for n in range(4)]
    for row in (0, RUN):
        rows = slice(row, row + RUN)
        total = (
            own_ref[rows, :extent].astype(F32)
            + below_ref[rows, :extent].astype(F32)
            + above_ref[rows, :extent].astype(F32)
        )
        strips = [own_ref[rows, blocks[0]]]
        for n in range(3):
            strips += [below_ref[rows, blocks[n]], above_ref[rows, blocks[n]]]
        strips.append((below_ref if row == 0 else above_ref)[rows, blocks[3]])
        if row == 0:
            kept_ref[...] = total
            for index, strip in enumerate(strips):
                strips_ref[:, index * BAND : (index + 1) * BAND] = strip
        else:
            sent_ref[:RUN] = total.astype(BF16)
            halves = [strip[low : low + 16] for strip in strips for low in (0, 16)]
            sent_ref[RUN + LINES :] = jnp.concatenate(halves, axis=1)

    def column(ref):
        tiled = ref[:, blocks[3].stop :].astype(F32)
        return jnp.concatenate([tiled[n * 8 : (n + 1) * 8] for n in range(extent // XT)], axis=1)

    mine = ends_ref[...].astype(F32)
    even = place_ref[1] % 2 == 0
    left = jnp.where(even, mine[8:], column(below_ref))
    right = jnp.where(even, column(above_ref), mine[:8])
    sent_ref[RUN : RUN + LINES] = jnp.concatenate([left, right], axis=0).astype(BF16)


def last_sums(place, own, ends, below, above, *order):
    extent = ends.shape[1]
    return pl.pallas_call(
        last_sums_kernel,
        out_shape=(
            jax.ShapeDtypeStruct((RUN, extent), F32),
            jax.ShapeDtypeStruct((RUN, len(STRIPS) * BAND), BF16),
            jax.ShapeDtypeStruct((RUN + LINES + 16, extent), BF16),
        ),
        in_specs=[SMEM] + [VMEM] * 4 + [ANY] * len(order),
        out_specs=(VMEM,) * 3,
        compiler_params=limit(8),
        cost_estimate=cost(5 * own.size, 14 * own.size),
        name="last_sums",
    )(place, own, ends, below, above, *order)


def residual_kernel(place_ref, kept_ref, strips_ref, arrived_ref, got_ref, *refs):
    out_ref, measured_ref = refs[-2:]
    extent = kept_ref.shape[1]
    blocks = extent // BAND
    me = place_ref[1]
    for index, hop in enumerate(STRIPS):
        tile = lax.rem(me + 2 * hop + blocks, blocks)
        measured_ref[tile] = strips_ref[:, index * BAND : (index + 1) * BAND].astype(F32)
        for half in (0, 1):
            lanes = slice((2 * index + half) * BAND, (2 * index + half + 1) * BAND)
            measured_ref[tile ^ 1, half * 16 : (half + 1) * 16] = arrived_ref[
                RUN + LINES :, lanes
            ].astype(F32)
    empty = jnp.zeros((8, BAND), F32)
    arrived = arrived_ref[:RUN].astype(F32)
    for slot in range(SLOTS):
        low = slot * 8
        total = kept_ref[low : low + 8] + arrived[low : low + 8]
        band = got_ref[me * SLOTS + slot].astype(F32)
        offset = band[9:10, 0:1].astype(jnp.int32)
        width = jnp.maximum(band[9:10, 1:2], 1.0)
        recip = 1.0 / width
        width = width.astype(jnp.int32)

        def inside(delta):
            delta = delta - offset
            return jnp.where((delta >= 0) & (delta < width), recip, 0.0).astype(BF16)

        shape = (2 * BAND, BAND)
        onward = inside(iota(shape, 1) + BAND - iota(shape, 0))
        back = inside(iota(shape, 0) - iota(shape, 1))
        parts = [total[:, n * BAND : (n + 1) * BAND] for n in range(blocks)]
        here = jnp.concatenate(parts, axis=0)
        before = jnp.concatenate([empty] + parts[:-1], axis=0)
        paired = jnp.concatenate([before, here], axis=1)
        high = paired.astype(BF16)
        rest = (paired - high.astype(F32)).astype(BF16)
        sums = jnp.dot(high, onward, preferred_element_type=F32) + jnp.dot(
            rest, onward, preferred_element_type=F32
        )
        rows = measured_ref[:, low : low + 8].reshape(blocks * 8, BAND)
        residual = (sums - rows).astype(BF16).astype(F32)
        later = jnp.concatenate([residual[8:], empty], axis=0)
        both = jnp.concatenate([residual, later], axis=1).astype(BF16)
        image = jnp.dot(both, back, preferred_element_type=F32)
        image = jnp.concatenate([image[n * 8 : (n + 1) * 8] for n in range(blocks)], axis=1)
        if slot % 2 == 0:
            even = image
        else:
            out_ref[low - 8 : low + 8] = jnp.concatenate([even, image], axis=0).astype(BF16)


def residual_images(place, kept, strips, arrived, got, *order):
    return pl.pallas_call(
        residual_kernel,
        out_shape=jax.ShapeDtypeStruct(kept.shape, BF16),
        in_specs=[SMEM] + [VMEM] * 4 + [ANY] * len(order),
        out_specs=VMEM,
        scratch_shapes=[pltpu.VMEM((kept.shape[1] // BAND, RUN, BAND), F32)],
        compiler_params=limit(8),
        cost_estimate=cost(4 * 8 * 16 * 256 * 128 * 6, 12 * kept.size),
        name="residual_images",
    )(place, kept, strips, arrived, got, *order)


def penalty(diff):
    return diff * lax.rsqrt(1.0 + diff * diff)


def regularizer_kernel(
    first_tile,
    count,
    place_ref,
    beta_ref,
    volume_ref,
    below_ref,
    above_ref,
    *refs,
):
    out_ref, token_ref, under_ref, buffer_ref, sem_ref = refs[-5:]
    step, steps = pl.program_id(0), pl.num_programs(0)

    @pl.when(step == 0)
    def _():
        start(tile_copies(volume_ref, buffer_ref, sem_ref, 0, first_tile, EDGE))

    block_ref = streamed(volume_ref, buffer_ref, sem_ref, step, steps, first_tile, EDGE)
    depth, strip, tile = volume_ref.shape[0], volume_ref.shape[2], XT
    at = pl.program_id(0) + first_tile
    beta = beta_ref[0]
    has_below, has_above = place_ref[0] > 0, place_ref[0] < place_ref[3] - 1
    here = pl.ds(EDGE, tile)
    bottom, top = block_ref[0, here], block_ref[depth - 1, here]
    below = jnp.where(has_below, below_ref[0], bottom).astype(F32)
    block_ref[depth, here] = jnp.where(has_above, above_ref[0], top)
    under_ref[...] = penalty(bottom.astype(F32) - below)
    row = iota((tile, strip), 0)
    lane = iota((tile, strip), 1)

    def body(z, carry):
        center = block_ref[z, here].astype(F32)
        over = penalty(block_ref[z + 1, here].astype(F32) - center)
        total = under_ref[...] - over
        under_ref[...] = over
        behind = block_ref[z, pl.ds(0, EDGE)].astype(F32)
        behind = jnp.where(at > 0, behind[EDGE - 1 :], behind[:1])
        ahead = block_ref[z, pl.ds(EDGE + tile, EDGE)].astype(F32)
        ahead = jnp.where(at < count - 1, ahead[:1], ahead[EDGE - 1 :])
        along = penalty(jnp.where(row == tile - 1, ahead, pltpu.roll(center, tile - 1, 0)) - center)
        behind = penalty(center[:1] - behind)
        total = total + jnp.where(row == 0, behind, pltpu.roll(along, 1, 0)) - along
        across = penalty(pltpu.roll(center, strip - 1, 1) - center)
        across = jnp.where(lane == strip - 1, 0.0, across)
        total = total + pltpu.roll(across, 1, 1) - across
        out_ref[z] = (total * beta).astype(BF16)
        return carry

    lax.fori_loop(0, depth, body, 0, unroll=2)
    token_ref[...] = under_ref[:8]


def regularizer(index, done, place, beta, volume, below, above, *order):
    depth, extent, strip = volume.shape
    count = extent // XT
    length = count // PIECES
    origin = index * length
    plane = pl.BlockSpec((1, XT, strip), lambda i: (0, origin + i, 0))
    block = pl.BlockSpec((depth, XT, strip), lambda i: (0, origin + i, 0))
    specs = [SMEM, SMEM, HBM]
    specs += [plane] * 2 + [ANY] * len(order)
    before = [] if done is None else [done]
    return pl.pallas_call(
        functools.partial(regularizer_kernel, origin, count),
        grid=(length,),
        out_shape=(pltpu.HBM(volume.shape, BF16), jax.ShapeDtypeStruct((8, strip), F32)),
        in_specs=specs + [HBM] * len(before),
        out_specs=(block, pl.BlockSpec((8, strip), lambda i: (0, 0))),
        scratch_shapes=[pltpu.VMEM((XT, strip), F32)] + stream_scratch(depth, strip, EDGE),
        compiler_params=limit(8),
        input_output_aliases={len(specs): 0} if before else {},
        cost_estimate=cost(30 * volume.size // PIECES, 8 * volume.size // PIECES),
        name="regularizer",
    )(place, beta, volume, below, above, *order, *before)


def gradient_kernel(place_ref, beta_ref, spread_ref, mine_ref, beside_ref, *refs):
    chunk_refs = refs[:-6]
    whole_ref, out_ref, buffer_ref, sem_ref, result_ref, result_sem_ref = refs[-6:]
    depth, extent, strip = whole_ref.shape
    steps = extent // WIDE
    beta = beta_ref[0]
    has_left = (place_ref[1] > 0).astype(F32)
    has_right = (place_ref[1] < place_ref[2] - 1).astype(F32)
    start(tile_copies(whole_ref, buffer_ref, sem_ref, 0, tile=WIDE))

    def result(step):
        slot = lax.rem(step, 2)
        here = pl.ds(pl.multiple_of(step * WIDE, WIDE), WIDE)
        return pltpu.make_async_copy(
            result_ref.at[slot], out_ref.at[:, here], result_sem_ref.at[slot]
        )

    def body(step, carry):
        here = pl.ds(pl.multiple_of(step * WIDE, WIDE), WIDE)
        mine = mine_ref[:, here].astype(F32)
        beside = beside_ref[RUN : RUN + LINES, here].astype(F32)
        on_left = penalty(mine[:8] - beside[:8]) * (has_left * beta)
        on_right = penalty(mine[8:] - beside[8:]) * (has_right * beta)
        ends = jnp.concatenate([on_left, on_right], axis=0).astype(BF16)
        rows = jnp.concatenate([ref[:, here] for ref in chunk_refs] + [ends], axis=0)
        out = lax.dot_general(
            rows, spread_ref[...], (((0,), (0,)), ((), ())), preferred_element_type=F32
        )
        regular_ref = streamed(whole_ref, buffer_ref, sem_ref, step, steps, tile=WIDE)

        @pl.when(step >= 2)
        def _():
            result(step - 2).wait()

        slot = lax.rem(step, 2)
        for z in range(depth):
            regular = regular_ref[z].astype(F32)
            result_ref[slot, z] = (out[:, z * strip : (z + 1) * strip] + regular).astype(BF16)
        result(step).start()
        return carry

    lax.fori_loop(0, steps, body, 0)
    result(jnp.int32(steps - 2)).wait()
    result(jnp.int32(steps - 1)).wait()


def gradient(place, beta, spread, mine, arrived, chunks, regular):
    depth, extent, strip = regular.shape
    size = depth * extent * strip
    return pl.pallas_call(
        gradient_kernel,
        out_shape=jax.ShapeDtypeStruct(regular.shape, BF16),
        in_specs=[SMEM, SMEM] + [VMEM] * (3 + len(chunks)) + [HBM],
        out_specs=ANY,
        scratch_shapes=stream_scratch(depth, strip, tile=WIDE)
        + [pltpu.VMEM((2, depth, WIDE, strip), BF16), pltpu.SemaphoreType.DMA((2,))],
        compiler_params=limit(16),
        cost_estimate=cost(2 * spread.shape[0] * size, 5 * size),
        name="gradient",
    )(place, beta, spread, mine, arrived, *chunks, regular)


def shards(volume, measured, ray_weight, view_owner, band_offset, band_width, beta):
    slabs = lax.axis_size("slab")
    tiles = lax.axis_size("tile")
    slab, tile = lax.axis_index("slab"), lax.axis_index("tile")
    depth = volume.shape[0]
    place = jnp.stack([slab, tile, jnp.int32(tiles), jnp.int32(slabs)])

    def along_z(block, by):
        return lax.ppermute(block, "tile", [(i, (i + 2 * by) % tiles) for i in range(tiles)])

    def along_y(block):
        return lax.ppermute(block, "tile", [(i, i ^ 1) for i in range(tiles)])

    packed = pack(view_owner[:, :, 0], band_offset, band_width, ray_weight, measured, slabs)
    packed, after = lax.optimization_barrier((packed, volume))
    got = lax.all_to_all(packed, "slab", split_axis=0, concat_axis=0, tiled=True)
    top, bottom = after[depth - 1 :], after[:1]
    below = lax.ppermute(top, "slab", [(i, i + 1) for i in range(slabs - 1)])
    above = lax.ppermute(bottom, "slab", [(i + 1, i) for i in range(slabs - 1)])
    flat = got.reshape(slabs * SLOTS, ROWS, BAND)
    volume = pltpu.with_memory_space_constraint(volume, pltpu.HBM)

    own, up1, down1, up2, down2, up3, down3, up, down, ends = forward(
        place, flat, volume, tiles, top, bottom
    )
    extent = ends.shape[1]
    spread = spread_rows(place, flat, tiles, ends)
    order, regular = [spread], None
    for index, (own_up, own_down) in enumerate([(up3, down3), (up2, down2), (up1, down1)]):
        came = along_z(up, 1), along_z(down, -1)
        up, down = ring_sums(came[0], own_up, came[1], own_down, extent, *order)
        regular, token = regularizer(index, regular, place, beta, volume, below, above, up)
        order = [token]
    came = along_z(up, 1), along_z(down, -1)
    kept, strips, sent = last_sums(place, own, ends, *came, *order)
    arrived = along_y(sent)
    regular, token = regularizer(3, regular, place, beta, volume, below, above, sent)
    images = residual_images(place, kept, strips, arrived, flat, token)

    partner = along_y(images)
    rings = []
    for first, past in ((images, 1), (partner, -1)):
        up, down = first, first
        ring = {0: first}
        for hop in range(1, tiles // 4):
            up, down = along_z(up, 1), along_z(down, -1)
            ring[-hop], ring[hop] = up, down
        ring[tiles // 4] = along_z(ring[-2 * past], 2 * past)
        rings.append(ring)
    chunks = [ring[hop] for hop in hops(tiles) for ring in rings]
    regular = pltpu.with_memory_space_constraint(regular, pltpu.HBM)
    return gradient(place, beta, spread, ends, arrived, chunks, regular)


def solution(mesh):
    in_specs = (
        P("slab", None, "tile"),
        P(None, "slab", None, "tile"),
        P(None, "slab", "tile"),
        P(None, "slab", None),
        P(None, "slab"),
        P(None, "slab"),
        P(),
    )
    out_specs = P("slab", None, "tile")
    return jax.shard_map(shards, mesh=mesh, in_specs=in_specs, out_specs=out_specs, check_vma=False)
```

```python
import functools

import jax
import jax.numpy as jnp
from jax import lax
from jax.experimental import pallas as pl
from jax.experimental.pallas import tpu as pltpu
from jax.sharding import PartitionSpec as P

BAND = 128
BATCHES = 2
CAPP = 2
SLOTS = BATCHES * CAPP
ROWS = 16
RUN = SLOTS * 8
PAIR = 2 * RUN
LINES = 16
EDGE = 16
PIECES = 4


def limit(mib):
    return pltpu.CompilerParams(vmem_limit_bytes=mib << 20)

XT = 256
WIDE = 512
TALL = 1024
F32 = jnp.float32
BF16 = jnp.bfloat16
VMEM = pl.BlockSpec(memory_space=pltpu.VMEM)
SMEM = pl.BlockSpec(memory_space=pltpu.SMEM)
ANY = pl.BlockSpec(memory_space=pl.ANY)
HBM = pl.BlockSpec(memory_space=pltpu.HBM)


def cost(flops, moved):
    return pl.CostEstimate(flops=flops, bytes_accessed=moved, transcendentals=0)


def iota(shape, dim):
    return lax.broadcasted_iota(jnp.int32, shape, dim)


def pack_kernel(owner_ref, offset_ref, width_ref, weight_ref, measured_ref, out_ref, count_ref):
    out_ref[...] = jnp.zeros_like(out_ref)
    slabs = out_ref.shape[0]
    views = owner_ref.shape[1]
    row = iota((ROWS, BAND), 0)
    lane = iota((ROWS, BAND), 1)
    empty = jnp.zeros((8, BAND), F32)
    for batch in range(BATCHES):
        for slab in range(slabs):
            count_ref[slab] = 0
        for view in range(views):
            owner = owner_ref[batch, view]
            rank = count_ref[owner]
            count_ref[owner] = rank + 1
            rows = jnp.concatenate([measured_ref[batch, view].astype(F32), empty], axis=0)
            band = jnp.where(
                lane == 0,
                offset_ref[batch, view].astype(F32),
                jnp.where(lane == 1, width_ref[batch, view].astype(F32), 0.0),
            )
            rows = jnp.where(row == 8, weight_ref[view].astype(F32)[batch : batch + 1], jnp.where(row == 9, band, rows))
            out_ref[owner, batch * CAPP + rank] = rows.astype(BF16)


def pack(owner, offset, width, weight, measured, slabs):
    return pl.pallas_call(
        pack_kernel,
        out_shape=jax.ShapeDtypeStruct((slabs, SLOTS, ROWS, BAND), BF16),
        in_specs=[SMEM, SMEM, SMEM, VMEM, VMEM],
        out_specs=VMEM,
        scratch_shapes=[pltpu.SMEM((slabs,), jnp.int32)],
        name="pack_messages",
    )(owner, offset, width, jnp.transpose(weight, (1, 0, 2)), measured)


def joined(block):
    return jnp.concatenate([block[z] for z in range(block.shape[0])], axis=1)


def tile_copies(ref, buffer_ref, sem_ref, index, first=0, edge=0, tile=XT):
    slot = lax.rem(index, 2)
    extent = ref.shape[1]
    start = (first + index) * tile
    parts = [(start, edge, tile)]
    if edge:
        parts.append((jnp.maximum(start - edge, 0), 0, edge))
        parts.append((jnp.minimum(start + tile, extent - edge), edge + tile, edge))
    return [
        pltpu.make_async_copy(
            ref.at[:, pl.ds(pl.multiple_of(source, 16), size)],
            buffer_ref.at[slot, pl.ds(0, ref.shape[0]), pl.ds(target, size)],
            sem_ref.at[slot, part],
        )
        for part, (source, target, size) in enumerate(parts)
    ]


def start(copies):
    for copy in copies:
        copy.start()


def streamed(ref, buffer_ref, sem_ref, step, steps, first=0, edge=0, tile=XT):
    @pl.when(step + 1 < steps)
    def _():
        start(tile_copies(ref, buffer_ref, sem_ref, step + 1, first, edge, tile))

    for copy in tile_copies(ref, buffer_ref, sem_ref, step, first, edge, tile):
        copy.wait()
    return buffer_ref.at[lax.rem(step, 2)]


def stream_scratch(depth, strip, edge=0, tile=XT):
    return [
        pltpu.VMEM((2, depth + (1 if edge else 0), tile + 2 * edge, strip), BF16),
        pltpu.SemaphoreType.DMA((2, 3 if edge else 1)),
    ]


def spread_weights(tiles, out_ref, first, depth):
    rows = tiles.shape[0] * depth
    weights = jnp.broadcast_to(
        tiles.astype(F32)[:, 8:9, :], (tiles.shape[0], depth, BAND)
    ).reshape(rows, BAND)
    slice_of = lax.rem(iota((rows, BAND), 0), depth)
    for z in range(depth):
        out_ref[first : first + rows, z * BAND : (z + 1) * BAND] = jnp.where(
            slice_of == z, weights, 0.0
        ).astype(BF16)


def hops(tiles):
    half = tiles // 4
    return [0] + [sign * hop for hop in range(1, half) for sign in (1, -1)] + [half]


def fill_spread(tiles, me, got_ref, spread_ref):
    row = 0
    for hop in hops(tiles):
        tile = lax.rem(me + 2 * hop + tiles, tiles)
        for source in (tile, tile ^ 1):
            spread_weights(got_ref[pl.ds(source * SLOTS, SLOTS)], spread_ref, row, 8)
            row += RUN
    shape = (LINES, spread_ref.shape[1])
    line = iota(shape, 0)
    target = jnp.where(line < 8, line * BAND, (line - 8) * BAND + BAND - 1)
    spread_ref[row:] = jnp.where(iota(shape, 1) == target, 1.0, 0.0).astype(BF16)


def spread_kernel(tiles, place_ref, got_ref, order_ref, out_ref):
    fill_spread(tiles, place_ref[1], got_ref, out_ref)


def spread_rows(place, got, tiles, order):
    shape = (got.shape[0] * 8 + LINES, 8 * BAND)
    return pl.pallas_call(
        functools.partial(spread_kernel, tiles),
        out_shape=jax.ShapeDtypeStruct(shape, BF16),
        in_specs=[SMEM, VMEM, ANY],
        out_specs=VMEM,
        compiler_params=limit(8),
        cost_estimate=cost(4 * shape[0] * shape[1], 4 * shape[0] * shape[1]),
        name="spread_rows",
    )(place, got, order)


def measured_rows(got_ref, source):
    rows = got_ref[pl.ds(source * SLOTS, SLOTS)].astype(F32)[:, :8]
    return rows.reshape(RUN, BAND).astype(BF16)


def forward_kernel(tiles, place_ref, got_ref, volume_ref, *refs):
    outs, (ends_ref, spread_ref, buffer_ref, sem_ref, last_ref, first_ref) = refs[:-6], refs[-6:]
    extent = volume_ref.shape[1]
    me = place_ref[1]
    start(tile_copies(volume_ref, buffer_ref, sem_ref, 0, tile=TALL))
    fill_spread(tiles, me, got_ref, spread_ref)
    where = [(ref, row) for ref in outs for row in range(0, ref.shape[0], RUN)]
    beyond = pl.ds(extent, BAND)
    for index, hop in enumerate(hops(tiles)):
        tile = lax.rem(me + 2 * hop + tiles, tiles)
        for turn, source in enumerate((tile, tile ^ 1)):
            ref, row = where[2 * index + turn]
            ref[row : row + RUN, beyond] = measured_rows(got_ref, source)
    steps = extent // TALL

    def body(step, carry):
        block_ref = streamed(volume_ref, buffer_ref, sem_ref, step, steps, tile=TALL)
        out = lax.dot_general(
            spread_ref[...],
            joined(block_ref),
            (((1,), (1,)), ((), ())),
            preferred_element_type=F32,
        ).astype(BF16)
        here = pl.ds(pl.multiple_of(step * TALL, TALL), TALL)
        for index, (ref, row) in enumerate(where):
            ref[row : row + RUN, here] = out[index * RUN : (index + 1) * RUN]
        ends_ref[:, here] = out[-LINES:]
        ends = out[-LINES:].astype(F32)
        count = TALL // XT
        for part in range(count):
            there = pl.ds(pl.multiple_of((step * count + part) * 8, 8), 8)
            first_ref[there] = ends[:8, part * XT : (part + 1) * XT]
            last_ref[there] = ends[8:, part * XT : (part + 1) * XT]
        return carry

    lax.fori_loop(0, steps, body, 0)
    outs[1][:, extent + BAND :] = last_ref[...].astype(BF16)
    outs[2][:, extent + BAND :] = first_ref[...].astype(BF16)


def forward(place, got, volume, tiles, *order):
    depth, extent, strip = volume.shape
    slots = got.shape[0]
    rows = [PAIR] * (tiles // 2 - 1) + [RUN] * 2
    lanes = [extent + BAND + (XT if index in (1, 2) else 0) for index in range(len(rows))]

    def kernel(place_ref, got_ref, volume_ref, *refs):
        forward_kernel(tiles, place_ref, got_ref, volume_ref, *refs[len(order) :])

    return pl.pallas_call(
        kernel,
        out_shape=[jax.ShapeDtypeStruct(shape, BF16) for shape in zip(rows, lanes)]
        + [jax.ShapeDtypeStruct((LINES, extent), BF16)],
        in_specs=[SMEM, VMEM, HBM] + [ANY] * len(order),
        out_specs=[VMEM] * (len(rows) + 1),
        scratch_shapes=[pltpu.VMEM((slots * depth + LINES, depth * strip), BF16)]
        + stream_scratch(depth, strip, tile=TALL)
        + [pltpu.VMEM((extent // XT * 8, XT), F32)] * 2,
        compiler_params=limit(16),
        cost_estimate=cost(2 * slots * depth * volume.size, 3 * volume.size),
        name="forward",
    )(place, got, volume, *order)


def sums_kernel(extent, from_below_ref, up_ref, from_above_ref, down_ref, *refs):
    for came_ref, own_ref, low, out_ref in (
        (from_below_ref, up_ref, 0, refs[-2]),
        (from_above_ref, down_ref, RUN, refs[-1]),
    ):
        came_lanes = came_ref.shape[1] - extent
        past = extent + BAND
        for row in (0, RUN):
            rows = slice(row, row + RUN)
            total = own_ref[rows, :extent].astype(F32)
            strips = jnp.zeros((RUN, came_lanes), BF16)
            if came_ref.shape[0] > RUN or row == low:
                came = rows if came_ref.shape[0] > RUN else slice(0, RUN)
                total = total + came_ref[came, :extent].astype(F32)
                strips = came_ref[came, extent:]
            out_ref[rows, :extent] = total.astype(BF16)
            out_ref[rows, extent:past] = own_ref[rows, extent:past]
            out_ref[rows, past : past + came_lanes] = strips
        if own_ref.shape[1] > past:
            out_ref[:, past + came_lanes :] = own_ref[:, past:]


def ring_sums(from_below, up, from_above, down, extent, *order):
    out = jax.ShapeDtypeStruct((PAIR, up.shape[1] + from_below.shape[1] - extent), BF16)
    return pl.pallas_call(
        functools.partial(sums_kernel, extent),
        out_shape=(out, out),
        in_specs=[VMEM] * 4 + [ANY] * len(order),
        out_specs=(VMEM, VMEM),
        compiler_params=limit(8),
        cost_estimate=cost(6 * out.size, 12 * out.size),
        name="ring_sums",
    )(from_below, up, from_above, down, *order)


STRIPS = (0, -1, 1, -2, 2, -3, 3, 4)


def last_sums_kernel(place_ref, own_ref, ends_ref, below_ref, above_ref, *refs):
    kept_ref, strips_ref, sent_ref = refs[-3:]
    extent = ends_ref.shape[1]
    blocks = [slice(extent + n * BAND, extent + (n + 1) * BAND) for n in range(4)]
    for row in (0, RUN):
        rows = slice(row, row + RUN)
        total = (
            own_ref[rows, :extent].astype(F32)
            + below_ref[rows, :extent].astype(F32)
            + above_ref[rows, :extent].astype(F32)
        )
        strips = [own_ref[rows, blocks[0]]]
        for n in range(3):
            strips += [below_ref[rows, blocks[n]], above_ref[rows, blocks[n]]]
        strips.append((below_ref if row == 0 else above_ref)[rows, blocks[3]])
        if row == 0:
            kept_ref[...] = total
            for index, strip in enumerate(strips):
                strips_ref[:, index * BAND : (index + 1) * BAND] = strip
        else:
            sent_ref[:RUN] = total.astype(BF16)
            halves = [strip[low : low + 16] for strip in strips for low in (0, 16)]
            sent_ref[RUN + LINES :] = jnp.concatenate(halves, axis=1)

    def column(ref):
        tiled = ref[:, blocks[3].stop :].astype(F32)
        return jnp.concatenate([tiled[n * 8 : (n + 1) * 8] for n in range(extent // XT)], axis=1)

    mine = ends_ref[...].astype(F32)
    even = place_ref[1] % 2 == 0
    left = jnp.where(even, mine[8:], column(below_ref))
    right = jnp.where(even, column(above_ref), mine[:8])
    sent_ref[RUN : RUN + LINES] = jnp.concatenate([left, right], axis=0).astype(BF16)


def last_sums(place, own, ends, below, above, *order):
    extent = ends.shape[1]
    return pl.pallas_call(
        last_sums_kernel,
        out_shape=(
            jax.ShapeDtypeStruct((RUN, extent), F32),
            jax.ShapeDtypeStruct((RUN, len(STRIPS) * BAND), BF16),
            jax.ShapeDtypeStruct((RUN + LINES + 16, extent), BF16),
        ),
        in_specs=[SMEM] + [VMEM] * 4 + [ANY] * len(order),
        out_specs=(VMEM,) * 3,
        compiler_params=limit(8),
        cost_estimate=cost(5 * own.size, 14 * own.size),
        name="last_sums",
    )(place, own, ends, below, above, *order)


def residual_kernel(place_ref, kept_ref, strips_ref, arrived_ref, got_ref, *refs):
    out_ref, measured_ref = refs[-2:]
    extent = kept_ref.shape[1]
    blocks = extent // BAND
    me = place_ref[1]
    for index, hop in enumerate(STRIPS):
        tile = lax.rem(me + 2 * hop + blocks, blocks)
        measured_ref[tile] = strips_ref[:, index * BAND : (index + 1) * BAND].astype(F32)
        for half in (0, 1):
            lanes = slice((2 * index + half) * BAND, (2 * index + half + 1) * BAND)
            measured_ref[tile ^ 1, half * 16 : (half + 1) * 16] = arrived_ref[
                RUN + LINES :, lanes
            ].astype(F32)
    empty = jnp.zeros((8, BAND), F32)
    arrived = arrived_ref[:RUN].astype(F32)
    for slot in range(SLOTS):
        low = slot * 8
        total = kept_ref[low : low + 8] + arrived[low : low + 8]
        band = got_ref[me * SLOTS + slot].astype(F32)
        offset = band[9:10, 0:1].astype(jnp.int32)
        width = jnp.maximum(band[9:10, 1:2], 1.0)
        recip = 1.0 / width
        width = width.astype(jnp.int32)

        def inside(delta):
            delta = delta - offset
            return jnp.where((delta >= 0) & (delta < width), recip, 0.0).astype(BF16)

        shape = (2 * BAND, BAND)
        onward = inside(iota(shape, 1) + BAND - iota(shape, 0))
        back = inside(iota(shape, 0) - iota(shape, 1))
        parts = [total[:, n * BAND : (n + 1) * BAND] for n in range(blocks)]
        here = jnp.concatenate(parts, axis=0)
        before = jnp.concatenate([empty] + parts[:-1], axis=0)
        paired = jnp.concatenate([before, here], axis=1)
        high = paired.astype(BF16)
        rest = (paired - high.astype(F32)).astype(BF16)
        sums = jnp.dot(high, onward, preferred_element_type=F32) + jnp.dot(
            rest, onward, preferred_element_type=F32
        )
        rows = measured_ref[:, low : low + 8].reshape(blocks * 8, BAND)
        residual = (sums - rows).astype(BF16).astype(F32)
        later = jnp.concatenate([residual[8:], empty], axis=0)
        both = jnp.concatenate([residual, later], axis=1).astype(BF16)
        image = jnp.dot(both, back, preferred_element_type=F32)
        image = jnp.concatenate([image[n * 8 : (n + 1) * 8] for n in range(blocks)], axis=1)
        if slot % 2 == 0:
            even = image
        else:
            out_ref[low - 8 : low + 8] = jnp.concatenate([even, image], axis=0).astype(BF16)


def residual_images(place, kept, strips, arrived, got, *order):
    return pl.pallas_call(
        residual_kernel,
        out_shape=jax.ShapeDtypeStruct(kept.shape, BF16),
        in_specs=[SMEM] + [VMEM] * 4 + [ANY] * len(order),
        out_specs=VMEM,
        scratch_shapes=[pltpu.VMEM((kept.shape[1] // BAND, RUN, BAND), F32)],
        compiler_params=limit(8),
        cost_estimate=cost(4 * 8 * 16 * 256 * 128 * 6, 12 * kept.size),
        name="residual_images",
    )(place, kept, strips, arrived, got, *order)


def penalty(diff):
    return diff * lax.rsqrt(1.0 + diff * diff)


def regularizer_kernel(
    first_tile,
    count,
    place_ref,
    beta_ref,
    volume_ref,
    below_ref,
    above_ref,
    *refs,
):
    out_ref, token_ref, under_ref, buffer_ref, sem_ref = refs[-5:]
    step, steps = pl.program_id(0), pl.num_programs(0)

    @pl.when(step == 0)
    def _():
        start(tile_copies(volume_ref, buffer_ref, sem_ref, 0, first_tile, EDGE))

    block_ref = streamed(volume_ref, buffer_ref, sem_ref, step, steps, first_tile, EDGE)
    depth, strip, tile = volume_ref.shape[0], volume_ref.shape[2], XT
    at = pl.program_id(0) + first_tile
    beta = beta_ref[0]
    has_below, has_above = place_ref[0] > 0, place_ref[0] < place_ref[3] - 1
    here = pl.ds(EDGE, tile)
    bottom, top = block_ref[0, here], block_ref[depth - 1, here]
    below = jnp.where(has_below, below_ref[0], bottom).astype(F32)
    block_ref[depth, here] = jnp.where(has_above, above_ref[0], top)
    under_ref[...] = penalty(bottom.astype(F32) - below)
    row = iota((tile, strip), 0)
    lane = iota((tile, strip), 1)

    def body(z, carry):
        center = block_ref[z, here].astype(F32)
        over = penalty(block_ref[z + 1, here].astype(F32) - center)
        total = under_ref[...] - over
        under_ref[...] = over
        behind = block_ref[z, pl.ds(0, EDGE)].astype(F32)
        behind = jnp.where(at > 0, behind[EDGE - 1 :], behind[:1])
        ahead = block_ref[z, pl.ds(EDGE + tile, EDGE)].astype(F32)
        ahead = jnp.where(at < count - 1, ahead[:1], ahead[EDGE - 1 :])
        along = penalty(jnp.where(row == tile - 1, ahead, pltpu.roll(center, tile - 1, 0)) - center)
        behind = penalty(center[:1] - behind)
        total = total + jnp.where(row == 0, behind, pltpu.roll(along, 1, 0)) - along
        across = penalty(pltpu.roll(center, strip - 1, 1) - center)
        across = jnp.where(lane == strip - 1, 0.0, across)
        total = total + pltpu.roll(across, 1, 1) - across
        out_ref[z] = (total * beta).astype(BF16)
        return carry

    lax.fori_loop(0, depth, body, 0, unroll=4)
    token_ref[...] = under_ref[:8]


def regularizer(index, done, place, beta, volume, below, above, *order):
    depth, extent, strip = volume.shape
    count = extent // XT
    length = count // PIECES
    origin = index * length
    plane = pl.BlockSpec((1, XT, strip), lambda i: (0, origin + i, 0))
    block = pl.BlockSpec((depth, XT, strip), lambda i: (0, origin + i, 0))
    specs = [SMEM, SMEM, HBM]
    specs += [plane] * 2 + [ANY] * len(order)
    before = [] if done is None else [done]
    return pl.pallas_call(
        functools.partial(regularizer_kernel, origin, count),
        grid=(length,),
        out_shape=(pltpu.HBM(volume.shape, BF16), jax.ShapeDtypeStruct((8, strip), F32)),
        in_specs=specs + [HBM] * len(before),
        out_specs=(block, pl.BlockSpec((8, strip), lambda i: (0, 0))),
        scratch_shapes=[pltpu.VMEM((XT, strip), F32)] + stream_scratch(depth, strip, EDGE),
        compiler_params=limit(8),
        input_output_aliases={len(specs): 0} if before else {},
        cost_estimate=cost(30 * volume.size // PIECES, 8 * volume.size // PIECES),
        name="regularizer",
    )(place, beta, volume, below, above, *order, *before)


def gradient_kernel(place_ref, beta_ref, spread_ref, mine_ref, beside_ref, *refs):
    chunk_refs = refs[:-6]
    whole_ref, out_ref, buffer_ref, sem_ref, result_ref, result_sem_ref = refs[-6:]
    depth, extent, strip = whole_ref.shape
    steps = extent // WIDE
    beta = beta_ref[0]
    has_left = (place_ref[1] > 0).astype(F32)
    has_right = (place_ref[1] < place_ref[2] - 1).astype(F32)
    start(tile_copies(whole_ref, buffer_ref, sem_ref, 0, tile=WIDE))

    def result(step):
        slot = lax.rem(step, 2)
        here = pl.ds(pl.multiple_of(step * WIDE, WIDE), WIDE)
        return pltpu.make_async_copy(
            result_ref.at[slot], out_ref.at[:, here], result_sem_ref.at[slot]
        )

    def body(step, carry):
        here = pl.ds(pl.multiple_of(step * WIDE, WIDE), WIDE)
        mine = mine_ref[:, here].astype(F32)
        beside = beside_ref[RUN : RUN + LINES, here].astype(F32)
        on_left = penalty(mine[:8] - beside[:8]) * (has_left * beta)
        on_right = penalty(mine[8:] - beside[8:]) * (has_right * beta)
        ends = jnp.concatenate([on_left, on_right], axis=0).astype(BF16)
        rows = jnp.concatenate([ref[:, here] for ref in chunk_refs] + [ends], axis=0)
        out = lax.dot_general(
            rows, spread_ref[...], (((0,), (0,)), ((), ())), preferred_element_type=F32
        )
        regular_ref = streamed(whole_ref, buffer_ref, sem_ref, step, steps, tile=WIDE)

        @pl.when(step >= 2)
        def _():
            result(step - 2).wait()

        slot = lax.rem(step, 2)
        for z in range(depth):
            regular = regular_ref[z].astype(F32)
            result_ref[slot, z] = (out[:, z * strip : (z + 1) * strip] + regular).astype(BF16)
        result(step).start()
        return carry

    lax.fori_loop(0, steps, body, 0)
    result(jnp.int32(steps - 2)).wait()
    result(jnp.int32(steps - 1)).wait()


def gradient(place, beta, spread, mine, arrived, chunks, regular):
    depth, extent, strip = regular.shape
    size = depth * extent * strip
    return pl.pallas_call(
        gradient_kernel,
        out_shape=jax.ShapeDtypeStruct(regular.shape, BF16),
        in_specs=[SMEM, SMEM] + [VMEM] * (3 + len(chunks)) + [HBM],
        out_specs=ANY,
        scratch_shapes=stream_scratch(depth, strip, tile=WIDE)
        + [pltpu.VMEM((2, depth, WIDE, strip), BF16), pltpu.SemaphoreType.DMA((2,))],
        compiler_params=limit(16),
        cost_estimate=cost(2 * spread.shape[0] * size, 5 * size),
        name="gradient",
    )(place, beta, spread, mine, arrived, *chunks, regular)


def shards(volume, measured, ray_weight, view_owner, band_offset, band_width, beta):
    slabs = lax.axis_size("slab")
    tiles = lax.axis_size("tile")
    slab, tile = lax.axis_index("slab"), lax.axis_index("tile")
    depth = volume.shape[0]
    place = jnp.stack([slab, tile, jnp.int32(tiles), jnp.int32(slabs)])

    def along_z(block, by):
        return lax.ppermute(block, "tile", [(i, (i + 2 * by) % tiles) for i in range(tiles)])

    def along_y(block):
        return lax.ppermute(block, "tile", [(i, i ^ 1) for i in range(tiles)])

    packed = pack(view_owner[:, :, 0], band_offset, band_width, ray_weight, measured, slabs)
    packed, after = lax.optimization_barrier((packed, volume))
    got = lax.all_to_all(packed, "slab", split_axis=0, concat_axis=0, tiled=True)
    top, bottom = after[depth - 1 :], after[:1]
    below = lax.ppermute(top, "slab", [(i, i + 1) for i in range(slabs - 1)])
    above = lax.ppermute(bottom, "slab", [(i + 1, i) for i in range(slabs - 1)])
    flat = got.reshape(slabs * SLOTS, ROWS, BAND)
    volume = pltpu.with_memory_space_constraint(volume, pltpu.HBM)

    own, up1, down1, up2, down2, up3, down3, up, down, ends = forward(
        place, flat, volume, tiles, top, bottom
    )
    extent = ends.shape[1]
    spread = spread_rows(place, flat, tiles, ends)
    order, regular = [spread], None
    for index, (own_up, own_down) in enumerate([(up3, down3), (up2, down2), (up1, down1)]):
        came = along_z(up, 1), along_z(down, -1)
        up, down = ring_sums(came[0], own_up, came[1], own_down, extent, *order)
        regular, token = regularizer(index, regular, place, beta, volume, below, above, up)
        order = [token]
    came = along_z(up, 1), along_z(down, -1)
    kept, strips, sent = last_sums(place, own, ends, *came, *order)
    arrived = along_y(sent)
    regular, token = regularizer(3, regular, place, beta, volume, below, above, sent)
    images = residual_images(place, kept, strips, arrived, flat, token)

    partner = along_y(images)
    rings = []
    for first, past in ((images, 1), (partner, -1)):
        up, down = first, first
        ring = {0: first}
        for hop in range(1, tiles // 4):
            up, down = along_z(up, 1), along_z(down, -1)
            ring[-hop], ring[hop] = up, down
        ring[tiles // 4] = along_z(ring[-2 * past], 2 * past)
        rings.append(ring)
    chunks = [ring[hop] for hop in hops(tiles) for ring in rings]
    regular = pltpu.with_memory_space_constraint(regular, pltpu.HBM)
    return gradient(place, beta, spread, ends, arrived, chunks, regular)


def solution(mesh):
    in_specs = (
        P("slab", None, "tile"),
        P(None, "slab", None, "tile"),
        P(None, "slab", "tile"),
        P(None, "slab", None),
        P(None, "slab"),
        P(None, "slab"),
        P(),
    )
    out_specs = P("slab", None, "tile")
    return jax.shard_map(shards, mesh=mesh, in_specs=in_specs, out_specs=out_specs, check_vma=False)
```
